32 devices in a mesh: wide: 8 (over z, y), tensor: 4 (over x, core).
Axes of the slice: x: 2, y: 2, z: 4, core: 2. Of those that a mesh axis runs over, the one named last changes fastest.
Arguments:
- tokens: bfloat16 [8192, 768], P(('wide', 'tensor')), may hold values from -6 to 6
- cotangent: bfloat16 [8192, 768], P(('wide', 'tensor')), may hold values from -6 to 6
- gate_logits: float32 [8192, 2], P('wide'), may hold values from -4 to 4
- routes: int32 [8192, 2], P('wide'), may hold values from 0 to 7, all different within a row; in each aligned block of 256 rows (0 to 255, 256 to 511, ...) at most 128 rows name the same one
- parents: int32 [8, 13], P('wide'), may hold values from 0 to 12, as said below
- mixing_in: float32 [768, 2304], P(('wide', 'tensor')), may hold values from -0.21875 to 0.21875
- mixing_in_mean: float32 [768, 2304], P(('wide', 'tensor')), may hold values from -512 to 512
- mixing_in_square: float32 [768, 2304], P(('wide', 'tensor')), may hold values from 8192 to 32768
- mixing_out: float32 [768, 768], P(('wide', 'tensor')), may hold values from -1.75 to 1.75
- mixing_out_mean: float32 [768, 768], P(('wide', 'tensor')), may hold values from -80 to 80
- mixing_out_square: float32 [768, 768], P(('wide', 'tensor')), may hold values from 184.32 to 737.28
- norm_gains: float32 [2, 768], P(None, ('wide', 'tensor')), may hold values from 0.5 to 1.5
- norm_gains_mean: float32 [2, 768], P(None, ('wide', 'tensor')), may hold values from -1024 to 1024
- norm_gains_square: float32 [2, 768], P(None, ('wide', 'tensor')), may hold values from 32768 to 131072
- shared_in: float32 [768, 2, 2048], P('wide', None, 'tensor'), may hold values from -0.21875 to 0.21875
- shared_in_mean: float32 [768, 2, 2048], P('wide', None, 'tensor'), may hold values from -192 to 192
- shared_in_square: float32 [768, 2, 2048], P('wide', None, 'tensor'), may hold values from 1003.52 to 4014.08
- shared_out: float32 [2048, 768], P('tensor', 'wide'), may hold values from -0.125 to 0.125
- shared_out_mean: float32 [2048, 768], P('tensor', 'wide'), may hold values from -320 to 320
- shared_out_square: float32 [2048, 768], P('tensor', 'wide'), may hold values from 2949.12 to 11796.48
- expert_in: float32 [8, 768, 2, 2048], P('wide', None, None, 'tensor'), may hold values from -0.21875 to 0.21875
- expert_in_mean: float32 [8, 768, 2, 2048], P('wide', None, None, 'tensor'), may hold values from -48 to 48
- expert_in_square: float32 [8, 768, 2, 2048], P('wide', None, None, 'tensor'), may hold values from 59.1872 to 236.7488
- expert_out: float32 [8, 2048, 768], P('wide', 'tensor'), may hold values from -0.125 to 0.125
- expert_out_mean: float32 [8, 2048, 768], P('wide', 'tensor'), may hold values from -80 to 80
- expert_out_square: float32 [8, 2048, 768], P('wide', 'tensor'), may hold values from 184.32 to 737.28
Outputs:
- mixed: bfloat16 [8192, 768], P(('wide', 'tensor'))
- input_grad: float32 [8192, 768], P(('wide', 'tensor'))
- logit_grad: float32 [8192, 2], P(('wide', 'tensor'))
- mixing_in_mean_new: float32 [768, 2304], P(('wide', 'tensor'))
- mixing_in_square_new: float32 [768, 2304], P(('wide', 'tensor'))
- mixing_in_updated: float32 [768, 2304], P(('wide', 'tensor'))
- mixing_out_mean_new: float32 [768, 768], P(('wide', 'tensor'))
- mixing_out_square_new: float32 [768, 768], P(('wide', 'tensor'))
- mixing_out_updated: float32 [768, 768], P(('wide', 'tensor'))
- norm_gains_mean_new: float32 [2, 768], P(None, ('wide', 'tensor'))
- norm_gains_square_new: float32 [2, 768], P(None, ('wide', 'tensor'))
- norm_gains_updated: float32 [2, 768], P(None, ('wide', 'tensor'))
- shared_in_mean_new: float32 [768, 2, 2048], P('wide', None, 'tensor')
- shared_in_square_new: float32 [768, 2, 2048], P('wide', None, 'tensor')
- shared_in_updated: float32 [768, 2, 2048], P('wide', None, 'tensor')
- shared_out_mean_new: float32 [2048, 768], P('tensor', 'wide')
- shared_out_square_new: float32 [2048, 768], P('tensor', 'wide')
- shared_out_updated: float32 [2048, 768], P('tensor', 'wide')
- expert_in_mean_new: float32 [8, 768, 2, 2048], P('wide', None, None, 'tensor')
- expert_in_square_new: float32 [8, 768, 2, 2048], P('wide', None, None, 'tensor')
- expert_in_updated: float32 [8, 768, 2, 2048], P('wide', None, None, 'tensor')
- expert_out_mean_new: float32 [8, 2048, 768], P('wide', 'tensor')
- expert_out_square_new: float32 [8, 2048, 768], P('wide', 'tensor')
- expert_out_updated: float32 [8, 2048, 768], P('wide', 'tensor')
The draws below stay inside these ranges and needn't reach their ends.
Inputs may be any that keep to these rules, and one draw needn't show every extreme that they name: `routes`: A token's 2 experts differ; in the rows of one device (aligned blocks of 256 tokens) no expert is named more than 128 times. `parents`: in each tree, entry 0 is 0; 4 of the other segments have parent 0 and each of them is the parent of exactly 2 segments.
All inputs are finite; a program needn't handle non-finite values.
Results may differ from the reference program's by a relative error of at most 0.019.
Values may be sent and summed in bfloat16 or wider, within the bound.
No kernel may reach another device: no remote copies, remote signals or barrier semaphores. Data moves between devices by JAX's collectives and lax.ppermute only.
A program may use at most 256 MiB of HBM per device.

```python
import math
import jax
import jax.numpy as jnp
import numpy as np
from jax import lax

D = 768
HEADS = 12
HEAD = 64
FF = 2048
TOP = 2
TRUNK = 256
SEG = 64
BRANCHES = 4
LEAVES = 2
STEP = 5
SEGS = 13
W_TOK = 1024
TREES = 8
TOKENS = 8192
TOK_DEV = 256
EXPERTS = 8
CAP_DEV = 128
N_WIDE = 8
N_TENSOR = 4


def draw_parents(key, part):
    key = jax.random.fold_in(key, 7)
    tree_keys = jax.random.split(key, TREES)

    def one_tree(tree_key):
        shuffled = (jax.random.permutation(tree_key, SEGS - 1) + 1).astype(jnp.int32)
        branches = shuffled[:BRANCHES]
        leaves = shuffled[BRANCHES:]
        owners = branches[jnp.arange(BRANCHES * LEAVES, dtype=jnp.int32) // LEAVES]
        parent_row = jnp.zeros((SEGS,), jnp.int32)
        return parent_row.at[leaves].set(owners)
    return jax.vmap(one_tree)(tree_keys).astype(jnp.int32)


def levels(own_key, extent, shards, least, high):
    def one(axis_at, blocks):
        draws = jax.random.uniform(jax.random.fold_in(jax.random.fold_in(own_key, 6), axis_at), (blocks,), jnp.float32, least / len(shards), high / len(shards))
        return jnp.repeat(jnp.exp(draws), extent[axis_at] // blocks).reshape((-1,) + (1,) * (len(extent) - axis_at - 1))

    level = one(*shards[0])
    for cut in shards[1:]:
        level = level * one(*cut)
    return level


def assign_block(own_key, own, number, rows, count, top, limit, skew):
    order = jax.random.permutation(own_key, count)
    crowded, ordinary = load_shares(count, rows * top, limit, skew, True), load_shares(count, rows * top, limit, skew, False)
    places = jnp.arange(count)

    def named(sizes, rotation):
        used = int((sizes > 0).sum())
        fixed = max(1, used // 4)
        shifted = fixed + (places - fixed + rotation * (used - fixed)) % max(1, count - fixed)
        return jnp.zeros((count,), jnp.int32).at[order[jnp.where(places < fixed, places, shifted)]].set(jnp.asarray(sizes, jnp.int32))

    sizes = jnp.where(number % 4 == 0, named(crowded, number // 4), named(ordinary, number - number // 4 - 1))
    mixed = jax.random.permutation(jax.random.fold_in(own, 3), count)
    donor, sink = mixed[0:count // 2 * 2:2], mixed[1:count // 2 * 2:2]
    slack = jnp.minimum(sizes[donor] - 1, limit - sizes[sink]) // 2
    slack = jnp.where((donor == order[0]) | (sink == order[0]) | (sizes[sink] == 0), 0, jnp.maximum(slack, 0))
    shifted = jax.random.randint(jax.random.fold_in(own, 4), (count // 2,), 0, 1 << 20) % (slack + 1)
    sizes = sizes.at[donor].add(-shifted).at[sink].add(shifted)
    items = jnp.searchsorted(jnp.cumsum(sizes), jnp.arange(rows * top), side="right").astype(jnp.int32)
    grid = items.reshape(top, rows).T
    grid = grid[jax.random.permutation(jax.random.fold_in(own, 1), rows)]
    rotation = jax.random.randint(jax.random.fold_in(own, 2), (rows, 1), 0, top)
    return jnp.take_along_axis(grid, (jnp.arange(top)[None, :] + rotation) % top, axis=1)


def load_shares(amount, total, bound, skew, full):
    loads = [(1 << 20) // math.isqrt(grade ** skew) + 1 for grade in range(1, amount + 1)]
    largest = bound if full else min(bound, max(-(-total // amount), total * loads[0] // sum(loads)))
    least = 1 if total - largest >= amount - 1 else 0
    counts, rest = [largest] + [least] * (amount - 1), total - largest - least * (amount - 1)
    while rest > 0:
        candidates = [i for i in range(1, amount) if counts[i] < largest] or [i for i in range(1, amount) if counts[i] < bound]
        pool, budget = sum([loads[i] for i in candidates]), rest
        for i in candidates:
            extra = min(bound - counts[i], max(1, budget * loads[i] // pool), rest)
            counts[i] = counts[i] + extra
            rest = rest - extra
    return np.array(counts)


def scatter_about(stream_key, dims, scale, bound, cuts=(), kind=jnp.bfloat16):
    entries = scale * jax.random.normal(stream_key, dims, jnp.float32)
    if cuts:
        entries = entries * levels(stream_key, dims, cuts, -0.22, 0.18)
    return jnp.clip(entries, -bound, bound).astype(kind)


def setup_inputs(seed: int = 0) -> dict:
    seeds = jax.random.split(jax.random.key(seed), 27)
    tokens = scatter_about(seeds[0], (TOKENS, D), 1.0, 6.0, ((0, 32),))
    cotangent = scatter_about(seeds[1], (TOKENS, D), 1.0, 6.0, ((0, 32),))
    gate_logits = scatter_about(seeds[2], (TOKENS, TOP), 0.7, 4.0, ((0, 8),), jnp.float32)
    routes_keys = jax.random.split(jax.random.fold_in(seeds[3], 1), TOKENS // TOK_DEV)
    routes_turns = jax.random.permutation(jax.random.fold_in(seeds[3], 3), TOKENS // TOK_DEV)
    routes = jax.vmap(lambda own, number: assign_block(jax.random.fold_in(seeds[3], 2), own, number, TOK_DEV, EXPERTS, TOP, CAP_DEV, 2))(routes_keys, routes_turns).reshape((TOKENS, TOP))
    parents = draw_parents(jax.random.fold_in(seeds[26], 71), 0)
    mixing_in = scatter_about(seeds[5], (D, 3 * D), D ** -0.5, 0.21875, ((0, 32),), jnp.float32)
    mixing_in_mean = scatter_about(seeds[6], (D, 3 * D), (1.0 * TOKENS ** 0.5), 512.0, ((0, 32),), jnp.float32)
    mixing_in_square = jnp.clip(jnp.exp(math.log(32768.0) - 1.3862944 * jax.random.uniform(seeds[7], (D, 3 * D), jnp.float32) ** levels(seeds[7], (D, 3 * D), ((0, 32),), -0.2, 0.2)), 8192.0, 32768.0)
    mixing_out = scatter_about(seeds[8], (D, D), (D // 64) ** -0.5, 1.75, ((0, 32),), jnp.float32)
    mixing_out_mean = scatter_about(seeds[9], (D, D), (0.15 * TOKENS ** 0.5), 80.0, ((0, 32),), jnp.float32)
    mixing_out_square = jnp.clip(jnp.exp(math.log(737.28) - 1.3862944 * jax.random.uniform(seeds[10], (D, D), jnp.float32) ** levels(seeds[10], (D, D), ((0, 32),), -0.2, 0.2)), 184.32, 737.28)
    norm_gains = jnp.clip(1.0 + 0.1 * jax.random.normal(seeds[11], (2, D), jnp.float32), 0.5, 1.5)
    norm_gains_mean = scatter_about(seeds[12], (2, D), (2.0 * TOKENS ** 0.5), 1024.0, ((1, 32),), jnp.float32)
    norm_gains_square = jnp.clip(jnp.exp(math.log(131072.0) - 1.3862944 * jax.random.uniform(seeds[13], (2, D), jnp.float32) ** levels(seeds[13], (2, D), ((1, 32),), -0.2, 0.2)), 32768.0, 131072.0)
    shared_in = scatter_about(seeds[14], (D, 2, FF), D ** -0.5, 0.21875, ((0, 8), (2, 4)), jnp.float32)
    shared_in_mean = scatter_about(seeds[15], (D, 2, FF), (0.35 * TOKENS ** 0.5), 192.0, ((0, 8), (2, 4)), jnp.float32)
    shared_in_square = jnp.clip(jnp.exp(math.log(4014.08) - 1.3862944 * jax.random.uniform(seeds[16], (D, 2, FF), jnp.float32) ** levels(seeds[16], (D, 2, FF), ((0, 8), (2, 4)), -0.2, 0.2)), 1003.52, 4014.08)
    shared_out = scatter_about(seeds[17], (FF, D), FF ** -0.5, 0.125, ((0, 4), (1, 8)), jnp.float32)
    shared_out_mean = scatter_about(seeds[18], (FF, D), (0.6 * TOKENS ** 0.5), 320.0, ((0, 4), (1, 8)), jnp.float32)
    shared_out_square = jnp.clip(jnp.exp(math.log(11796.48) - 1.3862944 * jax.random.uniform(seeds[19], (FF, D), jnp.float32) ** levels(seeds[19], (FF, D), ((0, 4), (1, 8)), -0.2, 0.2)), 2949.12, 11796.48)
    expert_in = scatter_about(seeds[20], (EXPERTS, D, 2, FF), D ** -0.5, 0.21875, ((0, 8), (3, 4)), jnp.float32)
    expert_in_mean = scatter_about(seeds[21], (EXPERTS, D, 2, FF), (0.17 * (2 * W_TOK) ** 0.5), 48.0, ((0, 8), (3, 4)), jnp.float32)
    expert_in_square = jnp.clip(jnp.exp(math.log(236.7488) - 1.3862944 * jax.random.uniform(seeds[22], (EXPERTS, D, 2, FF), jnp.float32) ** levels(seeds[22], (EXPERTS, D, 2, FF), ((0, 8), (3, 4)), -0.2, 0.2)), 59.1872, 236.7488)
    expert_out = scatter_about(seeds[23], (EXPERTS, FF, D), FF ** -0.5, 0.125, ((0, 8), (1, 4)), jnp.float32)
    expert_out_mean = scatter_about(seeds[24], (EXPERTS, FF, D), (0.3 * (2 * W_TOK) ** 0.5), 80.0, ((0, 8), (1, 4)), jnp.float32)
    expert_out_square = jnp.clip(jnp.exp(math.log(737.28) - 1.3862944 * jax.random.uniform(seeds[25], (EXPERTS, FF, D), jnp.float32) ** levels(seeds[25], (EXPERTS, FF, D), ((0, 8), (1, 4)), -0.2, 0.2)), 184.32, 737.28)
    return dict(tokens=tokens, cotangent=cotangent, gate_logits=gate_logits, routes=routes, parents=parents, mixing_in=mixing_in, mixing_in_mean=mixing_in_mean, mixing_in_square=mixing_in_square, mixing_out=mixing_out, mixing_out_mean=mixing_out_mean, mixing_out_square=mixing_out_square, norm_gains=norm_gains, norm_gains_mean=norm_gains_mean, norm_gains_square=norm_gains_square, shared_in=shared_in, shared_in_mean=shared_in_mean, shared_in_square=shared_in_square, shared_out=shared_out, shared_out_mean=shared_out_mean, shared_out_square=shared_out_square, expert_in=expert_in, expert_in_mean=expert_in_mean, expert_in_square=expert_in_square, expert_out=expert_out, expert_out_mean=expert_out_mean, expert_out_square=expert_out_square)


@jax.custom_vjp
def low(v):
    return lax.optimization_barrier(v.astype(jnp.bfloat16)).astype(jnp.float32)

@jax.custom_vjp
def low_back(v):
    return v

def low_keep(v):
    return (low(v), None)

def low_pass(kept, grad):
    return (grad,)

def back_keep(v):
    return (v, None)

def back_low(kept, grad):
    return (low(grad),)
low.defvjp(low_keep, low_pass)
low_back.defvjp(back_keep, back_low)
HIGH = lax.Precision.HIGHEST
NORM_EPS = 1e-06
BETA_ONE = 0.5
BETA_TWO = 0.5
ADAM_EPS = 1e-08
DECAY = 0.01
RATES = (0.02, 0.15, 0.3, 0.02, 0.012, 0.02, 0.012)

def rms_norm(values, gain):
    factor = lax.rsqrt(lax.optimization_barrier(jnp.mean(values * values, axis=-1, keepdims=True)) + NORM_EPS)
    return values * factor * gain

def rotate(values, position):
    half = values.shape[-1] // 2
    frequency = 10000.0 ** (-jnp.arange(half, dtype=position.dtype) / half)
    angles = position[:, None] * frequency[None, :]
    cosine = jnp.cos(angles)[:, None, :]
    sine_part = jnp.sin(angles)[:, None, :]
    first_half = values[..., :half]
    second_half = values[..., half:]
    return jnp.concatenate([first_half * cosine - second_half * sine_part, second_half * cosine + first_half * sine_part], axis=-1)

def tree_layout(parent_row, places):
    segment = jnp.where(places < TRUNK, 0, 1 + (places - TRUNK) // SEG).astype(jnp.int32)
    seg_start = jnp.where(segment == 0, 0, TRUNK + (segment - 1) * SEG)
    matches = segment[:, None] == jnp.arange(SEGS, dtype=jnp.int32)[None, :]
    upward = lax.optimization_barrier(jnp.sum(jnp.where(matches, parent_row[None, :], 0), axis=1)).astype(jnp.int32)
    depth_base = jnp.where(upward == 0, TRUNK, TRUNK + SEG)
    position = jnp.where(segment == 0, places, depth_base + places - seg_start)
    return (segment, upward, position)

def allowed_mask(seg_query, up_query, place_query, seg_key, place_key):
    same_segment = (seg_key[None, :] == seg_query[:, None]) & (place_key[None, :] <= place_query[:, None])
    ancestor = (seg_query[:, None] != 0) & ((seg_key[None, :] == 0) | (seg_key[None, :] == up_query[:, None]))
    return same_segment | ancestor

def tree_attention(row_block, parent_row, w_in, w_out, gain):
    places = jnp.arange(W_TOK, dtype=jnp.int32)
    segment, upward, position = tree_layout(parent_row, places)
    position = position.astype(row_block.dtype)
    normed = low(rms_norm(row_block, gain))
    mixed_proj = low_back(jnp.dot(normed, w_in, precision=HIGH))
    queries = low(rotate(mixed_proj[:, :D].reshape(W_TOK, HEADS, HEAD), position))
    keys_all = low(rotate(mixed_proj[:, D:2 * D].reshape(W_TOK, HEADS, HEAD), position))
    values_all = low(mixed_proj[:, 2 * D:].reshape(W_TOK, HEADS, HEAD))
    query_block = min(512, W_TOK)

    def one_block(block_start):
        part_query = lax.dynamic_slice_in_dim(queries, block_start, query_block, 0)
        seg_query = lax.dynamic_slice_in_dim(segment, block_start, query_block, 0)
        up_query = lax.dynamic_slice_in_dim(upward, block_start, query_block, 0)
        place_query = lax.dynamic_slice_in_dim(places, block_start, query_block, 0)
        allowed = allowed_mask(seg_query, up_query, place_query, segment, places)
        scores = low_back(jnp.einsum('qhd,khd->hqk', part_query, keys_all, precision=HIGH) / math.sqrt(HEAD))
        scores = jnp.where(allowed[None], scores, -1e+30)
        weights = low(jax.nn.softmax(scores, axis=-1))
        return low_back(jnp.einsum('hqk,khd->qhd', weights, values_all, precision=HIGH))
    starts = jnp.arange(W_TOK // query_block, dtype=jnp.int32) * query_block
    attended = lax.map(jax.checkpoint(one_block), starts).reshape(W_TOK, D)
    return low_back(jnp.dot(low(attended), w_out, precision=HIGH))

def swiglu(row_block, w_in, w_out):
    gate_up = low_back(jnp.einsum('rd,dcf->rcf', row_block, w_in, precision=HIGH))
    hidden = low(jax.nn.silu(gate_up[:, 0]) * gate_up[:, 1])
    return low_back(jnp.dot(hidden, w_out, precision=HIGH))

def whole_layer(tokens, gate_logits, routes, parents, mixing_in, mixing_out, norm_gains, shared_in, shared_out, expert_in, expert_out):
    gain_pair = low(norm_gains)
    w_mix_in = low(mixing_in)
    w_mix_out = low(mixing_out)
    w_sh_in = low(shared_in)
    w_sh_out = low(shared_out)
    w_ex_in = low(expert_in)
    w_ex_out = low(expert_out)
    tree_rows = tokens.reshape(TREES, W_TOK, D)
    attended = lax.map(jax.checkpoint(lambda packed: tree_attention(packed[0], packed[1], w_mix_in, w_mix_out, gain_pair[0])), (tree_rows, parents))
    residual = tokens + attended.reshape(TOKENS, D)
    normed = low(rms_norm(residual, gain_pair[1]))
    shared_part = lax.map(jax.checkpoint(lambda row_block: swiglu(row_block, w_sh_in, w_sh_out)), normed.reshape(TREES, W_TOK, D)).reshape(TOKENS, D)
    flat_routes = routes.reshape(-1)
    most_rows = N_WIDE * N_TENSOR * CAP_DEV
    expert_hits = lax.map(lambda expert_id: jnp.nonzero(flat_routes == expert_id, size=most_rows, fill_value=TOKENS * TOP)[0].astype(jnp.int32), jnp.arange(EXPERTS, dtype=jnp.int32))
    padded = jnp.concatenate([normed, jnp.zeros((1, D), normed.dtype)], axis=0)
    gates = jax.nn.softmax(gate_logits, axis=-1).reshape(-1)
    gates = jnp.concatenate([gates, jnp.zeros((1,), gates.dtype)])

    def one_expert(packed):
        w_in, w_out, hit_ids = packed
        return swiglu(padded[hit_ids // TOP], w_in, w_out) * gates[hit_ids][:, None]
    outputs = lax.map(jax.checkpoint(one_expert), (w_ex_in, w_ex_out, expert_hits))
    routed = jnp.zeros((TOKENS + 1, D), tokens.dtype).at[(expert_hits // TOP).reshape(-1)].add(outputs.reshape(-1, D))
    return residual + routed[:TOKENS] + shared_part

def adam_step(weight, mean_old, square_old, gradient, rate):
    mean_new = BETA_ONE * mean_old + (1.0 - BETA_ONE) * gradient
    square_new = BETA_TWO * square_old + (1.0 - BETA_TWO) * gradient * gradient
    mean_hat = mean_new / (1.0 - BETA_ONE ** STEP)
    square_hat = square_new / (1.0 - BETA_TWO ** STEP)
    updated = weight - rate * (mean_hat / (jnp.sqrt(square_hat) + ADAM_EPS) + DECAY * weight)
    return (mean_new, square_new, updated)

def reference(tokens, cotangent, gate_logits, routes, parents, mixing_in, mixing_in_mean, mixing_in_square, mixing_out, mixing_out_mean, mixing_out_square, norm_gains, norm_gains_mean, norm_gains_square, shared_in, shared_in_mean, shared_in_square, shared_out, shared_out_mean, shared_out_square, expert_in, expert_in_mean, expert_in_square, expert_out, expert_out_mean, expert_out_square):

    def forward(inputs, logits, w_one, w_two, w_three, w_four, w_five, w_six, w_seven):
        return whole_layer(inputs, logits, routes, parents, w_one, w_two, w_three, w_four, w_five, w_six, w_seven)
    layer_out, pullback = jax.vjp(forward, tokens.astype(jnp.float32), gate_logits, mixing_in, mixing_out, norm_gains, shared_in, shared_out, expert_in, expert_out)
    gradients = pullback(cotangent.astype(jnp.float32))
    weights = (mixing_in, mixing_out, norm_gains, shared_in, shared_out, expert_in, expert_out)
    means = (mixing_in_mean, mixing_out_mean, norm_gains_mean, shared_in_mean, shared_out_mean, expert_in_mean, expert_out_mean)
    squares = (mixing_in_square, mixing_out_square, norm_gains_square, shared_in_square, shared_out_square, expert_in_square, expert_out_square)
    results = [layer_out.astype(jnp.bfloat16), gradients[0], gradients[1]]
    for number in range(7):
        results.extend(adam_step(weights[number], means[number], squares[number], gradients[number + 2], RATES[number]))
    return tuple(results)
```

```python
import math

import jax
import jax.numpy as jnp
from jax import lax
from jax.sharding import PartitionSpec as P

HEAD = 64
TOP = 2
TRUNK = 256
SEG = 64
STEP = 5
SEGS = 13


NORM_EPS = 1e-06
BETA_ONE = 0.5
BETA_TWO = 0.5
ADAM_EPS = 1e-08
DECAY = 0.01
RATES = (0.02, 0.15, 0.3, 0.02, 0.012, 0.02, 0.012)

LOW = jnp.bfloat16
FULL = jnp.float32


def dot(a, b):
    return jnp.dot(a, b, preferred_element_type=FULL)


def dot_nt(a, b):
    return lax.dot_general(a, b, (((1,), (1,)), ((), ())), preferred_element_type=FULL)


def dot_tn(a, b):
    return lax.dot_general(a, b, (((0,), (0,)), ((), ())), preferred_element_type=FULL)


def rms_factor(values):
    return lax.rsqrt(jnp.mean(values * values, axis=-1, keepdims=True) + NORM_EPS)


def rms_back(values, factor, gain, grad):
    hat = values * factor
    scaled = grad * gain
    return factor * (scaled - hat * jnp.mean(scaled * hat, axis=-1, keepdims=True)), hat


def rotary_tables(position):
    half = HEAD // 2
    frequency = 10000.0 ** (-jnp.arange(half, dtype=FULL) / half)
    angles = position[:, None] * frequency[None, :]
    return jnp.cos(angles)[:, None, :], jnp.sin(angles)[:, None, :]


def rotate(values, cosine, sine):
    half = values.shape[-1] // 2
    one, two = values[..., :half], values[..., half:]
    return jnp.concatenate([one * cosine - two * sine, two * cosine + one * sine], axis=-1)


def tree_layout(parent_row, places):
    segment = jnp.where(places < TRUNK, 0, 1 + (places - TRUNK) // SEG)
    seg_start = jnp.where(segment == 0, 0, TRUNK + (segment - 1) * SEG)
    matches = segment[:, None] == jnp.arange(SEGS, dtype=jnp.int32)[None, :]
    upward = jnp.sum(jnp.where(matches, parent_row[None, :], 0), axis=1)
    depth_base = jnp.where(upward == 0, TRUNK, TRUNK + SEG)
    position = jnp.where(segment == 0, places, depth_base + places - seg_start)
    return (segment, upward, position)


def allowed_mask(segment, upward, places):
    same_segment = (segment[None, :] == segment[:, None]) & (places[None, :] <= places[:, None])
    ancestor = (segment[:, None] != 0) & (
        (segment[None, :] == 0) | (segment[None, :] == upward[:, None])
    )
    return same_segment | ancestor


def attend_forward(queries, keys, values, allowed):
    scale = 1.0 / math.sqrt(HEAD)
    scores = jnp.einsum("qhd,khd->hqk", queries, keys, preferred_element_type=FULL) * scale
    scores = jnp.where(allowed[None], scores, -1e30)
    row_top = jnp.max(scores, axis=-1, keepdims=True)
    shifted = jnp.exp(scores - row_top)
    row_total = jnp.sum(shifted, axis=-1, keepdims=True)
    weights = (shifted / row_total).astype(LOW)
    attended = jnp.einsum("hqk,khd->qhd", weights, values, preferred_element_type=FULL)
    return attended, row_top + jnp.log(row_total)


def attend_backward(queries, keys, values, allowed, grad_attended, log_totals):
    scale = 1.0 / math.sqrt(HEAD)
    scores = jnp.einsum("qhd,khd->hqk", queries, keys, preferred_element_type=FULL) * scale
    scores = jnp.where(allowed[None], scores, -1e30)
    probs = jnp.exp(scores - log_totals)
    grad_probs = jnp.einsum("qhd,khd->hqk", grad_attended, values, preferred_element_type=FULL)
    inner = jnp.sum(probs * grad_probs, axis=-1, keepdims=True)
    grad_scores = (probs * (grad_probs - inner)).astype(LOW)
    grad_query = jnp.einsum("hqk,khd->qhd", grad_scores, keys, preferred_element_type=FULL) * scale
    grad_key = jnp.einsum("hqk,qhd->khd", grad_scores, queries, preferred_element_type=FULL) * scale
    grad_value = jnp.einsum(
        "hqk,qhd->khd", probs.astype(LOW), grad_attended, preferred_element_type=FULL
    )
    return grad_query, grad_key, grad_value


def branch_forward(rows, w_gate, w_up):
    gate, up = dot(rows, w_gate), dot(rows, w_up)
    return gate, up, (jax.nn.silu(gate) * up).astype(LOW)


def branch_activation_grads(gate, up, grad_hidden):
    sigmoid = jax.nn.sigmoid(gate)
    grad_gate = grad_hidden * up * sigmoid * (1.0 + gate * (1.0 - sigmoid))
    grad_up = grad_hidden * gate * sigmoid
    return grad_gate.astype(LOW), grad_up.astype(LOW)


def adam_step(weight, mean_old, square_old, gradient, rate):
    mean_new = BETA_ONE * mean_old + (1.0 - BETA_ONE) * gradient
    square_new = BETA_TWO * square_old + (1.0 - BETA_TWO) * gradient * gradient
    mean_hat = mean_new / (1.0 - BETA_ONE**STEP)
    square_hat = square_new / (1.0 - BETA_TWO**STEP)
    updated = weight - rate * (mean_hat / (jnp.sqrt(square_hat) + ADAM_EPS) + DECAY * weight)
    return (mean_new, square_new, updated)


def swap_with(value, mask, count):
    return lax.ppermute(value, "tensor", [(i, i ^ mask) for i in range(count)])


def gather_chunks(parts, count):
    if count != 4:
        whole = [lax.all_gather(p, "tensor", axis=0) for p in parts]
        return [[w[j] for w in whole] for j in range(count)]
    far = [swap_with(p, 2, count) for p in parts]
    near = [swap_with(p, 1, count) for p in parts]
    both = [swap_with(p, 1, count) for p in far]
    return [parts, near, far, both]


def scatter_chunks(chunks, count):
    parts = range(len(chunks[0]))
    if count != 4:
        sums = []
        for p in parts:
            stacked = jnp.stack([chunks[j][p].astype(LOW) for j in range(count)])
            got = lax.all_to_all(stacked, "tensor", split_axis=0, concat_axis=0, tiled=True)
            sums.append(jnp.sum(got.astype(FULL), axis=0))
        return sums
    far = [swap_with(chunks[3][p].astype(LOW), 1, count) for p in parts]
    near = [swap_with(chunks[1][p].astype(LOW), 1, count) for p in parts]
    across = [
        swap_with((chunks[2][p] + far[p].astype(FULL)).astype(LOW), 2, count) for p in parts
    ]
    return [chunks[0][p] + near[p].astype(FULL) + across[p].astype(FULL) for p in parts]


def sum_rows(terms):
    return lax.psum_scatter(
        terms.astype(LOW), "tensor", scatter_dimension=0, tiled=True
    ).astype(FULL)


def exchange(value):
    return lax.all_to_all(value, "wide", split_axis=0, concat_axis=0, tiled=True)


def body(
    tokens,
    cotangent,
    gate_logits,
    routes,
    parents,
    mixing_in,
    mixing_in_mean,
    mixing_in_square,
    mixing_out,
    mixing_out_mean,
    mixing_out_square,
    norm_gains,
    norm_gains_mean,
    norm_gains_square,
    shared_in,
    shared_in_mean,
    shared_in_square,
    shared_out,
    shared_out_mean,
    shared_out_square,
    expert_in,
    expert_in_mean,
    expert_in_square,
    expert_out,
    expert_out_mean,
    expert_out_square,
):
    rows_dev, width = tokens.shape
    wide = lax.axis_size("wide")
    count = lax.axis_size("tensor")
    rank = lax.axis_index("tensor")
    tree_length = rows_dev * count
    capacity = 2 * rows_dev * TOP // wide
    slots = wide * capacity
    heads = width // HEAD
    heads_dev = -(-heads // count)
    head_pad = heads_dev * count - heads
    head_width = heads_dev * HEAD
    rows_weight = mixing_in.shape[0]

    cut = mixing_in.astype(LOW).reshape(rows_weight, 3, heads, HEAD)
    cut = jnp.pad(cut, ((0, 0), (0, 0), (0, head_pad), (0, 0)))
    cut = cut.reshape(rows_weight, 3, count, head_width).transpose(2, 0, 1, 3)
    cut = cut.reshape(count, rows_weight, 3 * head_width)
    gain_columns = jnp.broadcast_to(norm_gains.astype(LOW).T[None], (count, rows_weight, 2))
    cut = jnp.concatenate([cut, gain_columns], axis=2)
    sent = jnp.broadcast_to(cut[None], (wide,) + cut.shape).reshape(
        wide * count, rows_weight, 3 * head_width + 2
    )
    got = lax.all_to_all(sent, ("wide", "tensor"), split_axis=0, concat_axis=0, tiled=True)
    got = got.reshape(width, 3 * head_width + 2)
    w_qkv = got[:, : 3 * head_width]
    gain_pair = got[:, 3 * head_width :].astype(FULL).T

    tokens_all = lax.all_gather(tokens, "tensor", axis=0, tiled=True)
    w_mix_out = lax.all_gather(
        mixing_out.astype(LOW), ("wide", "tensor"), axis=0, tiled=True
    )
    shared_low = jnp.concatenate(
        [shared_in.astype(LOW), shared_out.astype(LOW).T[:, None]], axis=1
    )
    w_shared = lax.all_gather(shared_low, "wide", axis=0, tiled=True)
    cotangent_all = lax.all_gather(cotangent, "tensor", axis=0, tiled=True)
    expert_chunks = gather_chunks(
        [
            expert_in[0, :, 0].astype(LOW),
            expert_in[0, :, 1].astype(LOW),
            expert_out[0].astype(LOW),
        ],
        count,
    )

    own_routes = lax.dynamic_slice_in_dim(routes, rank * rows_dev, rows_dev, 0)
    own_logits = lax.dynamic_slice_in_dim(gate_logits, rank * rows_dev, rows_dev, 0)
    gates = jax.nn.softmax(own_logits, axis=-1)
    flat = own_routes.reshape(-1)
    named = (flat[:, None] == jnp.arange(wide, dtype=jnp.int32)[None, :]).astype(LOW)
    order = jnp.arange(flat.shape[0], dtype=jnp.int32)
    earlier = (order[None, :] < order[:, None]).astype(LOW)
    before = jnp.sum(dot(earlier, named) * named.astype(FULL), axis=1).astype(jnp.int32)
    places = (flat * capacity + before).reshape(rows_dev, TOP)
    slot_ids = jnp.arange(slots, dtype=jnp.int32)
    picks = [(slot_ids[:, None] == places[:, k][None, :]).astype(LOW) for k in range(TOP)]
    pick_any = picks[0] + picks[1]
    grad_out = cotangent.astype(FULL)
    grad_routes = [(gates[:, k : k + 1] * grad_out).astype(LOW) for k in range(TOP)]
    grad_slots = (dot(picks[0], grad_routes[0]) + dot(picks[1], grad_routes[1])).astype(LOW)
    expert_grads = exchange(grad_slots.reshape(wide, capacity, width)).reshape(slots, width)

    tree_places = jnp.arange(tree_length, dtype=jnp.int32)
    segment, upward, position = tree_layout(parents[0], tree_places)
    allowed = allowed_mask(segment, upward, tree_places)
    cosine, sine = rotary_tables(position.astype(FULL))
    tree_rows = tokens_all.astype(FULL)
    normed_one = (tree_rows * rms_factor(tree_rows) * gain_pair[0]).astype(LOW)
    projected = dot(normed_one, w_qkv).reshape(tree_length, 3, heads_dev, HEAD)
    queries = rotate(projected[:, 0], cosine, sine).astype(LOW)
    keys = rotate(projected[:, 1], cosine, sine).astype(LOW)
    values = projected[:, 2].astype(LOW)
    attended, log_totals = attend_forward(queries, keys, values, allowed)
    attended_low = lax.all_to_all(
        attended.astype(LOW).reshape(tree_length, head_width),
        "tensor",
        split_axis=0,
        concat_axis=1,
        tiled=True,
    )[:, :width]
    input_rows = tokens.astype(FULL)
    residual = input_rows + dot(attended_low, w_mix_out)
    factor_two = rms_factor(residual)
    normed_two = (residual * factor_two * gain_pair[1]).astype(LOW)

    row_slots = dot(pick_any, normed_two).astype(LOW)
    expert_rows = exchange(row_slots.reshape(wide, capacity, width)).reshape(slots, width)
    shared_rows = lax.all_gather(normed_two, "tensor", axis=0, tiled=True)
    sh_gate_w, sh_up_w, sh_out_t = w_shared[:, 0], w_shared[:, 1], w_shared[:, 2]
    sh_gate, sh_up, sh_hidden = branch_forward(shared_rows, sh_gate_w, sh_up_w)
    sh_grad_hidden = dot(cotangent_all, sh_out_t)
    sh_ggate, sh_gup = branch_activation_grads(sh_gate, sh_up, sh_grad_hidden)
    sh_grad_rows = sum_rows(dot_nt(sh_ggate, sh_gate_w) + dot_nt(sh_gup, sh_up_w))
    sh_part = sum_rows(dot_nt(sh_hidden, sh_out_t))
    sh_grads = jnp.stack(
        [
            dot_tn(shared_rows, sh_ggate).astype(LOW),
            dot_tn(shared_rows, sh_gup).astype(LOW),
            dot_tn(cotangent_all, sh_hidden).astype(LOW),
        ],
        axis=1,
    )

    states = []
    grad_rows = 0.0
    for gate_w, up_w, out_w in expert_chunks:
        gate, up, hidden = branch_forward(expert_rows, gate_w, up_w)
        ggate, gup = branch_activation_grads(gate, up, dot_nt(expert_grads, out_w))
        grad_rows = grad_rows + dot_nt(ggate, gate_w) + dot_nt(gup, up_w)
        states.append((hidden, ggate, gup))
    back_rows = exchange(grad_rows.astype(LOW).reshape(wide, capacity, width))
    back_rows = back_rows.reshape(slots, width)
    out_rows = 0.0
    for (hidden, _, _), (_, _, out_w) in zip(states, expert_chunks):
        out_rows = out_rows + dot(hidden, out_w)
    returned = exchange(out_rows.astype(LOW).reshape(wide, capacity, width))
    returned = returned.reshape(slots, width)
    weight_grads = [
        [dot_tn(expert_rows, ggate), dot_tn(expert_rows, gup), dot_tn(hidden, expert_grads)]
        for hidden, ggate, gup in states
    ]
    grad_ex_gate, grad_ex_up, grad_ex_out = scatter_chunks(weight_grads, count)
    grad_ex_in = jnp.stack([grad_ex_gate, grad_ex_up], axis=1)

    grad_normed_two = dot_tn(pick_any, back_rows) + sh_grad_rows
    grad_part, hat_two = rms_back(residual, factor_two, gain_pair[1], grad_normed_two)
    gain_two_part = jnp.sum(grad_normed_two * hat_two, axis=0)
    grad_residual = grad_out + grad_part
    grad_res_low = grad_residual.astype(LOW)
    grad_attended = dot_nt(grad_res_low, w_mix_out).astype(LOW)
    grad_attended = jnp.pad(grad_attended, ((0, 0), (0, head_pad * HEAD)))
    grad_attended = lax.all_to_all(
        grad_attended, "tensor", split_axis=1, concat_axis=0, tiled=True
    ).reshape(tree_length, heads_dev, HEAD)
    grad_mix_out = dot_tn(attended_low, grad_res_low).astype(LOW)
    grad_mix_out = lax.all_to_all(
        grad_mix_out.reshape(wide * count, rows_weight, width),
        ("wide", "tensor"),
        split_axis=0,
        concat_axis=0,
        tiled=True,
    )
    grad_mix_out = jnp.sum(grad_mix_out.astype(FULL), axis=0)

    grad_query, grad_key, grad_value = attend_backward(
        queries, keys, values, allowed, grad_attended, log_totals
    )
    grad_projected = jnp.stack(
        [rotate(grad_query, cosine, -sine), rotate(grad_key, cosine, -sine), grad_value], axis=1
    )
    grad_projected = grad_projected.astype(LOW).reshape(tree_length, 3 * head_width)
    grad_normed_one = sum_rows(dot_nt(grad_projected, w_qkv))
    grad_mix_in = dot_tn(normed_one, grad_projected).astype(LOW)
    sent = jnp.concatenate([grad_mix_in, gain_two_part.astype(LOW)[:, None]], axis=1)
    got = lax.all_to_all(
        sent.reshape(wide * count, rows_weight, 3 * head_width + 1),
        ("wide", "tensor"),
        split_axis=0,
        concat_axis=0,
        tiled=True,
    )
    got = jnp.sum(got.astype(FULL).reshape(wide, count, rows_weight, -1), axis=0)
    grad_gain_two = jnp.sum(got[:, :, 3 * head_width], axis=0)
    grad_mix_in = got[:, :, : 3 * head_width].reshape(count, rows_weight, 3, head_width)
    grad_mix_in = grad_mix_in.transpose(1, 2, 0, 3).reshape(rows_weight, 3, count * head_width)
    grad_mix_in = grad_mix_in[:, :, :width].reshape(rows_weight, 3 * width)
    grad_gain_one = jnp.sum(mixing_in.astype(LOW).astype(FULL) * grad_mix_in, axis=1)
    grad_gain_one = grad_gain_one / norm_gains[0].astype(LOW).astype(FULL)

    grad_part, _ = rms_back(input_rows, rms_factor(input_rows), gain_pair[0], grad_normed_one)
    input_grad = grad_residual + grad_part

    per_route = [dot_tn(picks[k], returned) for k in range(TOP)]
    mixed = (
        residual + gates[:, :1] * per_route[0] + gates[:, 1:] * per_route[1] + sh_part
    )
    gate_grad = jnp.stack([jnp.sum(grad_out * rows, axis=-1) for rows in per_route], axis=1)
    logit_grad = gates * (gate_grad - jnp.sum(gates * gate_grad, axis=-1, keepdims=True))

    sh_grads = exchange(sh_grads.reshape(wide, width // wide, 3, -1))
    sh_grads = jnp.sum(sh_grads.astype(FULL), axis=0)

    weights = (mixing_in, mixing_out, norm_gains, shared_in, shared_out, expert_in, expert_out)
    means = (
        mixing_in_mean,
        mixing_out_mean,
        norm_gains_mean,
        shared_in_mean,
        shared_out_mean,
        expert_in_mean,
        expert_out_mean,
    )
    squares = (
        mixing_in_square,
        mixing_out_square,
        norm_gains_square,
        shared_in_square,
        shared_out_square,
        expert_in_square,
        expert_out_square,
    )
    gradients = (
        grad_mix_in,
        grad_mix_out,
        jnp.stack([grad_gain_one, grad_gain_two]),
        sh_grads[:, :2],
        sh_grads[:, 2].T,
        grad_ex_in[None],
        grad_ex_out[None],
    )
    results = [mixed.astype(LOW), input_grad, logit_grad]
    for number in range(7):
        results.extend(
            adam_step(
                weights[number], means[number], squares[number], gradients[number], RATES[number]
            )
        )
    return tuple(results)


def solution(mesh):
    placed = (
        P(("wide", "tensor"), None),
        P(("wide", "tensor"), None),
        P("wide", None),
        P("wide", None),
        P("wide", None),
        P(("wide", "tensor"), None),
        P(("wide", "tensor"), None),
        P(("wide", "tensor"), None),
        P(("wide", "tensor"), None),
        P(("wide", "tensor"), None),
        P(("wide", "tensor"), None),
        P(None, ("wide", "tensor")),
        P(None, ("wide", "tensor")),
        P(None, ("wide", "tensor")),
        P("wide", None, "tensor"),
        P("wide", None, "tensor"),
        P("wide", None, "tensor"),
        P("tensor", "wide"),
        P("tensor", "wide"),
        P("tensor", "wide"),
        P("wide", None, None, "tensor"),
        P("wide", None, None, "tensor"),
        P("wide", None, None, "tensor"),
        P("wide", "tensor", None),
        P("wide", "tensor", None),
        P("wide", "tensor", None),
    )
    return jax.shard_map(
        body,
        mesh=mesh,
        in_specs=placed,
        out_specs=(
            P(("wide", "tensor"), None),
            P(("wide", "tensor"), None),
            P(("wide", "tensor"), None),
            P(("wide", "tensor"), None),
            P(("wide", "tensor"), None),
            P(("wide", "tensor"), None),
            P(("wide", "tensor"), None),
            P(("wide", "tensor"), None),
            P(("wide", "tensor"), None),
            P(None, ("wide", "tensor")),
            P(None, ("wide", "tensor")),
            P(None, ("wide", "tensor")),
            P("wide", None, "tensor"),
            P("wide", None, "tensor"),
            P("wide", None, "tensor"),
            P("tensor", "wide"),
            P("tensor", "wide"),
            P("tensor", "wide"),
            P("wide", None, None, "tensor"),
            P("wide", None, None, "tensor"),
            P("wide", None, None, "tensor"),
            P("wide", "tensor", None),
            P("wide", "tensor", None),
            P("wide", "tensor", None),
        ),
        check_vma=False,
    )
```

```python
import functools
import math

import jax
import jax.numpy as jnp
from jax import lax
from jax.experimental import pallas as pl
from jax.experimental.pallas import tpu as pltpu
from jax.sharding import PartitionSpec as P

HEAD = 64
TOP = 2
TRUNK = 256
SEG = 64
STEP = 5
SEGS = 13


NORM_EPS = 1e-06
BETA_ONE = 0.5
BETA_TWO = 0.5
ADAM_EPS = 1e-08
DECAY = 0.01
RATES = (0.02, 0.15, 0.3, 0.02, 0.012, 0.02, 0.012)

LOW = jnp.bfloat16
FULL = jnp.float32


def dot(a, b):
    return jnp.dot(a, b, preferred_element_type=FULL)


def dot_nt(a, b):
    return lax.dot_general(a, b, (((1,), (1,)), ((), ())), preferred_element_type=FULL)


def dot_tn(a, b):
    return lax.dot_general(a, b, (((0,), (0,)), ((), ())), preferred_element_type=FULL)


def rms_factor(values):
    return lax.rsqrt(jnp.mean(values * values, axis=-1, keepdims=True) + NORM_EPS)


def rms_back(values, factor, gain, grad):
    hat = values * factor
    scaled = grad * gain
    return factor * (scaled - hat * jnp.mean(scaled * hat, axis=-1, keepdims=True)), hat


def rotary_tables(position):
    half = HEAD // 2
    frequency = 10000.0 ** (-jnp.arange(half, dtype=FULL) / half)
    angles = position[:, None] * frequency[None, :]
    return jnp.cos(angles)[:, None, :], jnp.sin(angles)[:, None, :]


def rotate(values, cosine, sine):
    half = values.shape[-1] // 2
    one, two = values[..., :half], values[..., half:]
    return jnp.concatenate([one * cosine - two * sine, two * cosine + one * sine], axis=-1)


def tree_layout(parent_row, places):
    segment = jnp.where(places < TRUNK, 0, 1 + (places - TRUNK) // SEG)
    seg_start = jnp.where(segment == 0, 0, TRUNK + (segment - 1) * SEG)
    matches = segment[:, None] == jnp.arange(SEGS, dtype=jnp.int32)[None, :]
    upward = jnp.sum(jnp.where(matches, parent_row[None, :], 0), axis=1)
    depth_base = jnp.where(upward == 0, TRUNK, TRUNK + SEG)
    position = jnp.where(segment == 0, places, depth_base + places - seg_start)
    return (segment, upward, position)


def allowed_mask(segment, upward, places):
    same_segment = (segment[None, :] == segment[:, None]) & (places[None, :] <= places[:, None])
    ancestor = (segment[:, None] != 0) & (
        (segment[None, :] == 0) | (segment[None, :] == upward[:, None])
    )
    return same_segment | ancestor


def attend_forward(queries, keys, values, allowed):
    scale = 1.0 / math.sqrt(HEAD)
    scores = jnp.einsum("qhd,khd->hqk", queries, keys, preferred_element_type=FULL) * scale
    scores = jnp.where(allowed[None], scores, -1e30)
    row_top = jnp.max(scores, axis=-1, keepdims=True)
    shifted = jnp.exp(scores - row_top)
    row_total = jnp.sum(shifted, axis=-1, keepdims=True)
    weights = (shifted / row_total).astype(LOW)
    attended = jnp.einsum("hqk,khd->qhd", weights, values, preferred_element_type=FULL)
    return attended, row_top + jnp.log(row_total)


def attend_backward(queries, keys, values, allowed, grad_attended, log_totals):
    scale = 1.0 / math.sqrt(HEAD)
    scores = jnp.einsum("qhd,khd->hqk", queries, keys, preferred_element_type=FULL) * scale
    scores = jnp.where(allowed[None], scores, -1e30)
    probs = jnp.exp(scores - log_totals)
    grad_probs = jnp.einsum("qhd,khd->hqk", grad_attended, values, preferred_element_type=FULL)
    inner = jnp.sum(probs * grad_probs, axis=-1, keepdims=True)
    grad_scores = (probs * (grad_probs - inner)).astype(LOW)
    grad_query = jnp.einsum("hqk,khd->qhd", grad_scores, keys, preferred_element_type=FULL) * scale
    grad_key = jnp.einsum("hqk,qhd->khd", grad_scores, queries, preferred_element_type=FULL) * scale
    grad_value = jnp.einsum(
        "hqk,qhd->khd", probs.astype(LOW), grad_attended, preferred_element_type=FULL
    )
    return grad_query, grad_key, grad_value


def branch_rows_kernel(chunks, flipped, x_ref, g_ref, *refs):
    weights, (hidden_ref, ggate_ref, gup_ref, grad_ref) = refs[: 2 * chunks], refs[2 * chunks :]
    x, g = x_ref[...], g_ref[...]
    out_dot = dot if flipped else dot_nt
    total = None
    for chunk in range(chunks):
        w_in, w_out = weights[2 * chunk], weights[2 * chunk + 1]
        size = w_in.shape[2]
        at = pl.ds(chunk * size, size)
        gate, up = dot(x, w_in[0]), dot(x, w_in[1])
        grad_hidden = out_dot(g, w_out[...])
        sigmoid = 1.0 / (1.0 + jnp.exp(-gate))
        active = gate * sigmoid
        hidden_ref[:, at] = (active * up).astype(LOW)
        ggate = (grad_hidden * up * sigmoid * (1.0 + gate * (1.0 - sigmoid))).astype(LOW)
        gup = (grad_hidden * active).astype(LOW)
        ggate_ref[:, at] = ggate
        gup_ref[:, at] = gup
        part = dot_nt(ggate, w_in[0]) + dot_nt(gup, w_in[1])
        total = part if total is None else total + part
    grad_ref[...] = total.astype(LOW)


def branch_rows(x, g, chunks, flipped):
    rows, width = x.shape
    size = chunks[0][0].shape[2]
    hidden = size * len(chunks)
    block = math.gcd(rows, 256)
    row_spec = pl.BlockSpec((block, width), lambda i: (i, 0))
    hidden_spec = pl.BlockSpec((block, hidden), lambda i: (i, 0))
    weights = [w for chunk in chunks for w in chunk]
    whole = [
        pl.BlockSpec(w.shape, functools.partial(lambda n, i: (0,) * n, w.ndim),
                     pipeline_mode=pl.Buffered(1))
        for w in weights
    ]
    hidden_type = jax.ShapeDtypeStruct((rows, hidden), LOW)
    return pl.pallas_call(
        functools.partial(branch_rows_kernel, len(chunks), flipped),
        grid=(rows // block,),
        in_specs=[row_spec, row_spec] + whole,
        out_specs=[hidden_spec] * 3 + [row_spec],
        out_shape=[hidden_type] * 3 + [jax.ShapeDtypeStruct((rows, width), LOW)],
        compiler_params=pltpu.CompilerParams(vmem_limit_bytes=48 * 1024 * 1024),
        cost_estimate=pl.CostEstimate(
            flops=10 * rows * width * hidden,
            bytes_accessed=6 * (width * hidden + rows * hidden + rows * width),
            transcendentals=rows * hidden,
        ),
        name="branch_rows",
    )(x, g, *weights)


def branch_out_kernel(chunks, flipped, hidden_ref, *refs):
    weights, out_ref = refs[:chunks], refs[chunks]
    total = None
    for chunk in range(chunks):
        w_out = weights[chunk][...]
        size = w_out.shape[1 if flipped else 0]
        part = hidden_ref[:, pl.ds(chunk * size, size)]
        part = dot_nt(part, w_out) if flipped else dot(part, w_out)
        total = part if total is None else total + part
    out_ref[...] = total.astype(LOW)


def branch_out(hidden, outs, flipped):
    rows, size = hidden.shape
    width = outs[0].shape[0 if flipped else 1]
    block = math.gcd(rows, 256)
    return pl.pallas_call(
        functools.partial(branch_out_kernel, len(outs), flipped),
        grid=(rows // block,),
        in_specs=[pl.BlockSpec((block, size), lambda i: (i, 0))]
        + [
            pl.BlockSpec(w.shape, lambda i: (0, 0), pipeline_mode=pl.Buffered(1)) for w in outs
        ],
        out_specs=pl.BlockSpec((block, width), lambda i: (i, 0)),
        out_shape=jax.ShapeDtypeStruct((rows, width), LOW),
        compiler_params=pltpu.CompilerParams(vmem_limit_bytes=48 * 1024 * 1024),
        cost_estimate=pl.CostEstimate(
            flops=2 * rows * width * size,
            bytes_accessed=2 * (width * size + rows * size + rows * width),
            transcendentals=0,
        ),
        name="branch_out",
    )(hidden, *outs)


def branch_grads_kernel(x_ref, g_ref, hidden_ref, ggate_ref, gup_ref, in_ref, out_ref):
    x, g = x_ref[...], g_ref[...]
    in_ref[0, 0] = dot_tn(x, ggate_ref[...]).astype(LOW)
    in_ref[0, 1] = dot_tn(x, gup_ref[...]).astype(LOW)
    out_ref[0] = dot_tn(g, hidden_ref[...]).astype(LOW)


def branch_grads(x, g, hidden, ggate, gup, first, chunks, size):
    rows, width = x.shape
    block = math.gcd(width, 256)
    row_spec = pl.BlockSpec((rows, block), lambda j, i: (0, i))
    hidden_spec = pl.BlockSpec((rows, size), lambda j, i: (0, first + j))
    return pl.pallas_call(
        branch_grads_kernel,
        grid=(chunks, width // block),
        in_specs=[row_spec, row_spec, hidden_spec, hidden_spec, hidden_spec],
        out_specs=[
            pl.BlockSpec((1, 2, block, size), lambda j, i: (j, 0, i, 0)),
            pl.BlockSpec((1, block, size), lambda j, i: (j, i, 0)),
        ],
        out_shape=[
            jax.ShapeDtypeStruct((chunks, 2, width, size), LOW),
            jax.ShapeDtypeStruct((chunks, width, size), LOW),
        ],
        compiler_params=pltpu.CompilerParams(vmem_limit_bytes=48 * 1024 * 1024),
        cost_estimate=pl.CostEstimate(
            flops=6 * rows * width * size * chunks,
            bytes_accessed=6 * chunks * (width * size + rows * size + rows * width),
            transcendentals=0,
        ),
        name="branch_grads",
    )(x, g, hidden, ggate, gup)


def adam_step(weight, mean_old, square_old, gradient, rate):
    mean_new = BETA_ONE * mean_old + (1.0 - BETA_ONE) * gradient
    square_new = BETA_TWO * square_old + (1.0 - BETA_TWO) * gradient * gradient
    mean_hat = mean_new / (1.0 - BETA_ONE**STEP)
    square_hat = square_new / (1.0 - BETA_TWO**STEP)
    updated = weight - rate * (mean_hat / (jnp.sqrt(square_hat) + ADAM_EPS) + DECAY * weight)
    return (mean_new, square_new, updated)


def swap(value, axis, mask, count):
    return lax.ppermute(value, axis, [(i, i ^ mask) for i in range(count)])


def after(value, *earlier):
    return lax.optimization_barrier((value,) + earlier)[0]


def by_rank(parts, rank):
    count = len(parts)
    ordered = []
    for place in range(count):
        chosen = parts[place]
        for other in range(1, count):
            chosen = jnp.where(rank == other, parts[place ^ other], chosen)
        ordered.append(chosen)
    return ordered


def gather_relative(value, count):
    if count != 4:
        rank = lax.axis_index("tensor")
        every = lax.all_gather(value, "tensor", axis=0)
        return [lax.dynamic_index_in_dim(every, rank ^ m, 0, False) for m in range(count)]
    far = swap(value, "tensor", 2, count)
    near = swap(value, "tensor", 1, count)
    return [value, near, far, swap(far, "tensor", 1, count)]


def send_relative(parts):
    count = len(parts)
    return [parts[0]] + [swap(parts[m], "tensor", m, count) for m in range(1, count)]


def sum_relative(parts):
    got = send_relative([p.astype(LOW) for p in parts])
    total = parts[0].astype(FULL)
    for part in got[1:]:
        total = total + part.astype(FULL)
    return total


def sum_halving(parts, axis, count):
    parts = dict(enumerate(parts))
    mask = 1
    while mask < count:
        leaving = [m for m in parts if m & mask]
        sent = jnp.stack([parts[m].astype(LOW) for m in leaving])
        got = swap(sent, axis, mask, count).astype(FULL)
        parts = {
            m ^ mask: parts[m ^ mask].astype(FULL) + got[at] for at, m in enumerate(leaving)
        }
        mask *= 2
    return parts[0].astype(FULL)


def block_of(value, place, size, dim=0):
    return lax.dynamic_slice_in_dim(value, place * size, size, dim)


def exchange(value):
    return lax.all_to_all(value, "wide", split_axis=0, concat_axis=0, tiled=True)


def body(
    tokens,
    cotangent,
    gate_logits,
    routes,
    parents,
    mixing_in,
    mixing_in_mean,
    mixing_in_square,
    mixing_out,
    mixing_out_mean,
    mixing_out_square,
    norm_gains,
    norm_gains_mean,
    norm_gains_square,
    shared_in,
    shared_in_mean,
    shared_in_square,
    shared_out,
    shared_out_mean,
    shared_out_square,
    expert_in,
    expert_in_mean,
    expert_in_square,
    expert_out,
    expert_out_mean,
    expert_out_square,
):
    rows_dev, width = tokens.shape
    wide = lax.axis_size("wide")
    count = lax.axis_size("tensor")
    rank = lax.axis_index("tensor")
    tree_length = rows_dev * count
    capacity = 2 * rows_dev * TOP // wide
    slots = wide * capacity
    heads = width // HEAD
    heads_dev = -(-heads // count)
    head_pad = heads_dev * count - heads
    head_width = heads_dev * HEAD
    rows_weight = mixing_in.shape[0]

    cut = mixing_in.astype(LOW).reshape(rows_weight, 3, heads, HEAD)
    cut = jnp.pad(cut, ((0, 0), (0, 0), (0, head_pad), (0, 0)))
    cut = cut.reshape(rows_weight, 3, count, head_width).transpose(2, 0, 1, 3)
    cut = cut.reshape(count, rows_weight, 3 * head_width)
    gain_columns = jnp.broadcast_to(norm_gains.astype(LOW).T[None], (count, rows_weight, 2))
    cut = jnp.concatenate([cut, gain_columns], axis=2)
    sent = jnp.broadcast_to(cut[None], (wide,) + cut.shape).reshape(
        wide * count, rows_weight, 3 * head_width + 2
    )
    got = lax.all_to_all(sent, ("wide", "tensor"), split_axis=0, concat_axis=0, tiled=True)
    got = got.reshape(width, 3 * head_width + 2)
    w_qkv = got[:, : 3 * head_width]
    gain_pair = got[:, 3 * head_width :].astype(FULL).T

    tokens_all = jnp.concatenate(by_rank(gather_relative(tokens, count), rank), axis=0)
    w_mix_out = lax.all_gather(
        mixing_out.astype(LOW), ("wide", "tensor"), axis=0, tiled=True
    )
    shared_low = jnp.concatenate(
        [shared_in.astype(LOW).transpose(1, 0, 2), shared_out.astype(LOW).T[None]], axis=0
    )
    w_shared = lax.all_gather(shared_low, "wide", axis=1, tiled=True)
    cotangent_rel = jnp.concatenate(gather_relative(cotangent, count), axis=0)
    expert_chunks = list(
        zip(
            gather_relative(expert_in[0].astype(LOW).transpose(1, 0, 2), count),
            gather_relative(expert_out[0].astype(LOW), count),
        )
    )
    if count == 4:
        expert_chunks = [expert_chunks[m] for m in (0, 2, 1, 3)]

    own_routes = lax.dynamic_slice_in_dim(routes, rank * rows_dev, rows_dev, 0)
    own_logits = lax.dynamic_slice_in_dim(gate_logits, rank * rows_dev, rows_dev, 0)
    gates = jax.nn.softmax(own_logits, axis=-1)
    flat = own_routes.reshape(-1)
    named = (flat[:, None] == jnp.arange(wide, dtype=jnp.int32)[None, :]).astype(LOW)
    order = jnp.arange(flat.shape[0], dtype=jnp.int32)
    earlier = (order[None, :] < order[:, None]).astype(LOW)
    before = jnp.sum(dot(earlier, named) * named.astype(FULL), axis=1).astype(jnp.int32)
    places = (flat * capacity + before).reshape(rows_dev, TOP)
    slot_ids = jnp.arange(slots, dtype=jnp.int32)
    picks = [(slot_ids[:, None] == places[:, k][None, :]).astype(LOW) for k in range(TOP)]
    pick_any = picks[0] + picks[1]
    grad_out = cotangent.astype(FULL)
    grad_routes = [(gates[:, k : k + 1] * grad_out).astype(LOW) for k in range(TOP)]
    grad_slots = (dot(picks[0], grad_routes[0]) + dot(picks[1], grad_routes[1])).astype(LOW)
    grad_slots = after(grad_slots, got)
    expert_grads = exchange(grad_slots.reshape(wide, capacity, width)).reshape(slots, width)

    tree_places = jnp.arange(tree_length, dtype=jnp.int32)
    segment, upward, position = tree_layout(parents[0], tree_places)
    allowed = allowed_mask(segment, upward, tree_places)
    cosine, sine = rotary_tables(position.astype(FULL))
    tree_rows = tokens_all.astype(FULL)
    normed_one = (tree_rows * rms_factor(tree_rows) * gain_pair[0]).astype(LOW)
    projected = dot(normed_one, w_qkv).reshape(tree_length, 3, heads_dev, HEAD)
    queries = rotate(projected[:, 0], cosine, sine).astype(LOW)
    keys = rotate(projected[:, 1], cosine, sine).astype(LOW)
    values = projected[:, 2].astype(LOW)
    attended, log_totals = attend_forward(queries, keys, values, allowed)
    attended = after(attended.astype(LOW).reshape(tree_length, head_width), *expert_chunks[1])
    attended = send_relative([block_of(attended, rank ^ m, rows_dev) for m in range(count)])
    attended_low = jnp.concatenate(by_rank(attended, rank), axis=1)[:, :width]
    input_rows = tokens.astype(FULL)
    residual = input_rows + dot(attended_low, w_mix_out)
    factor_two = rms_factor(residual)
    normed_two = (residual * factor_two * gain_pair[1]).astype(LOW)

    row_slots = dot(pick_any, normed_two).astype(LOW)
    row_slots = after(row_slots, expert_grads)
    expert_rows = exchange(row_slots.reshape(wide, capacity, width)).reshape(slots, width)
    shared_rows = jnp.concatenate(gather_relative(normed_two, count), axis=0)
    shared_chunk = (w_shared[:2], w_shared[2])
    sh_hidden, sh_ggate, sh_gup, sh_grad_rows = branch_rows(
        shared_rows, cotangent_rel, [shared_chunk], True
    )
    sh_grad_rows = sum_relative(jnp.split(sh_grad_rows, count))
    sh_part = branch_out(sh_hidden, [shared_chunk[1]], True)
    sh_size = sh_hidden.shape[1]
    sh_grad_in, sh_grad_out = branch_grads(
        shared_rows, cotangent_rel, sh_hidden, sh_ggate, sh_gup, 0, 1, sh_size
    )

    ex_hidden, ex_ggate, ex_gup, ex_grad_rows = branch_rows(
        expert_rows, expert_grads, expert_chunks, False
    )
    back_rows = exchange(ex_grad_rows.reshape(wide, capacity, width)).reshape(slots, width)
    out_rows = branch_out(ex_hidden, [chunk[1] for chunk in expert_chunks], False)
    out_rows = after(out_rows, back_rows)
    returned = exchange(out_rows.reshape(wide, capacity, width)).reshape(slots, width)
    ex_size = ex_hidden.shape[1] // count
    ex_grads = functools.partial(
        branch_grads, expert_rows, expert_grads, ex_hidden, ex_ggate, ex_gup
    )
    if count == 4:
        sent = [swap(part, "tensor", 1, count).astype(FULL) for part in ex_grads(2, 2, ex_size)]
        kept = ex_grads(0, 2, ex_size)
        across = [
            swap((part[1] + got[1]).astype(LOW), "tensor", 2, count)
            for part, got in zip(kept, sent)
        ]
        grad_ex_in, grad_ex_out = [
            part[0] + got[0] + far.astype(FULL) for part, got, far in zip(kept, sent, across)
        ]
    else:
        grad_ex_in, grad_ex_out = [sum_relative(list(part)) for part in ex_grads(0, count, ex_size)]
    grad_ex_in = grad_ex_in.transpose(1, 0, 2)
    grad_ex_out = grad_ex_out.T

    grad_normed_two = dot_tn(pick_any, back_rows) + sh_grad_rows
    grad_part, hat_two = rms_back(residual, factor_two, gain_pair[1], grad_normed_two)
    gain_two_part = jnp.sum(grad_normed_two * hat_two, axis=0)
    grad_residual = grad_out + grad_part
    grad_res_low = grad_residual.astype(LOW)
    w_mix_pad = jnp.pad(w_mix_out, ((0, head_pad * HEAD), (0, 0)))
    grad_attended = send_relative(
        [
            dot_nt(grad_res_low, block_of(w_mix_pad, rank ^ m, head_width)).astype(LOW)
            for m in range(count)
        ]
    )
    grad_attended = jnp.concatenate(by_rank(grad_attended, rank), axis=0)
    grad_attended = grad_attended.reshape(tree_length, heads_dev, HEAD)
    grad_mix_out = dot_tn(attended_low, grad_res_low).reshape(wide, count, rows_weight, width)
    grad_mix_out = sum_relative(
        [lax.dynamic_index_in_dim(grad_mix_out, rank ^ m, 1, False) for m in range(count)]
    )
    grad_mix_out = after(grad_mix_out.astype(LOW), returned)
    grad_mix_out = jnp.sum(exchange(grad_mix_out).astype(FULL), axis=0)

    grad_query, grad_key, grad_value = attend_backward(
        queries, keys, values, allowed, grad_attended, log_totals
    )
    grad_projected = jnp.stack(
        [rotate(grad_query, cosine, -sine), rotate(grad_key, cosine, -sine), grad_value], axis=1
    )
    grad_projected = grad_projected.astype(LOW).reshape(tree_length, 3 * head_width)
    grad_normed_one = dot_nt(grad_projected, w_qkv).astype(LOW)
    grad_normed_one = sum_relative(
        [block_of(grad_normed_one, rank ^ m, rows_dev) for m in range(count)]
    )
    grad_mix_in = dot_tn(normed_one, grad_projected).astype(LOW)
    sent = jnp.concatenate([grad_mix_in, gain_two_part.astype(LOW)[:, None]], axis=1)
    got = lax.all_to_all(
        sent.reshape(wide * count, rows_weight, 3 * head_width + 1),
        ("wide", "tensor"),
        split_axis=0,
        concat_axis=0,
        tiled=True,
    )
    got = jnp.sum(got.astype(FULL).reshape(wide, count, rows_weight, -1), axis=0)
    grad_gain_two = jnp.sum(got[:, :, 3 * head_width], axis=0)
    grad_mix_in = got[:, :, : 3 * head_width].reshape(count, rows_weight, 3, head_width)
    grad_mix_in = grad_mix_in.transpose(1, 2, 0, 3).reshape(rows_weight, 3, count * head_width)
    grad_mix_in = grad_mix_in[:, :, :width].reshape(rows_weight, 3 * width)
    grad_gain_one = jnp.sum(mixing_in.astype(LOW).astype(FULL) * grad_mix_in, axis=1)
    grad_gain_one = grad_gain_one / norm_gains[0].astype(LOW).astype(FULL)

    grad_part, _ = rms_back(input_rows, rms_factor(input_rows), gain_pair[0], grad_normed_one)
    input_grad = grad_residual + grad_part

    per_route = [dot_tn(picks[k], returned) for k in range(TOP)]
    sh_part = sum_relative(jnp.split(sh_part, count))
    mixed = residual + gates[:, :1] * per_route[0] + gates[:, 1:] * per_route[1] + sh_part
    gate_grad = jnp.stack([jnp.sum(grad_out * rows, axis=-1) for rows in per_route], axis=1)
    logit_grad = gates * (gate_grad - jnp.sum(gates * gate_grad, axis=-1, keepdims=True))

    tree = lax.axis_index("wide")
    rows_shared = width // wide
    sh_grads = jnp.concatenate([sh_grad_in[0], sh_grad_out], axis=0)
    sh_grads = sum_halving(
        [block_of(sh_grads, tree ^ m, rows_shared, 1) for m in range(wide)], "wide", wide
    )

    weights = (mixing_in, mixing_out, norm_gains, shared_in, shared_out, expert_in, expert_out)
    means = (
        mixing_in_mean,
        mixing_out_mean,
        norm_gains_mean,
        shared_in_mean,
        shared_out_mean,
        expert_in_mean,
        expert_out_mean,
    )
    squares = (
        mixing_in_square,
        mixing_out_square,
        norm_gains_square,
        shared_in_square,
        shared_out_square,
        expert_in_square,
        expert_out_square,
    )
    gradients = (
        grad_mix_in,
        grad_mix_out,
        jnp.stack([grad_gain_one, grad_gain_two]),
        sh_grads[:2].transpose(1, 0, 2),
        sh_grads[2].T,
        grad_ex_in[None],
        grad_ex_out[None],
    )
    results = [mixed.astype(LOW), input_grad, logit_grad]
    for number in range(7):
        results.extend(
            adam_step(
                weights[number], means[number], squares[number], gradients[number], RATES[number]
            )
        )
    return tuple(results)


def solution(mesh):
    placed = (
        P(("wide", "tensor"), None),
        P(("wide", "tensor"), None),
        P("wide", None),
        P("wide", None),
        P("wide", None),
        P(("wide", "tensor"), None),
        P(("wide", "tensor"), None),
        P(("wide", "tensor"), None),
        P(("wide", "tensor"), None),
        P(("wide", "tensor"), None),
        P(("wide", "tensor"), None),
        P(None, ("wide", "tensor")),
        P(None, ("wide", "tensor")),
        P(None, ("wide", "tensor")),
        P("wide", None, "tensor"),
        P("wide", None, "tensor"),
        P("wide", None, "tensor"),
        P("tensor", "wide"),
        P("tensor", "wide"),
        P("tensor", "wide"),
        P("wide", None, None, "tensor"),
        P("wide", None, None, "tensor"),
        P("wide", None, None, "tensor"),
        P("wide", "tensor", None),
        P("wide", "tensor", None),
        P("wide", "tensor", None),
    )
    return jax.shard_map(
        body,
        mesh=mesh,
        in_specs=placed,
        out_specs=(
            P(("wide", "tensor"), None),
            P(("wide", "tensor"), None),
            P(("wide", "tensor"), None),
            P(("wide", "tensor"), None),
            P(("wide", "tensor"), None),
            P(("wide", "tensor"), None),
            P(("wide", "tensor"), None),
            P(("wide", "tensor"), None),
            P(("wide", "tensor"), None),
            P(None, ("wide", "tensor")),
            P(None, ("wide", "tensor")),
            P(None, ("wide", "tensor")),
            P("wide", None, "tensor"),
            P("wide", None, "tensor"),
            P("wide", None, "tensor"),
            P("tensor", "wide"),
            P("tensor", "wide"),
            P("tensor", "wide"),
            P("wide", None, None, "tensor"),
            P("wide", None, None, "tensor"),
            P("wide", None, None, "tensor"),
            P("wide", "tensor", None),
            P("wide", "tensor", None),
            P("wide", "tensor", None),
        ),
        check_vma=False,
    )
```

```python
import functools
import math

import jax
import jax.numpy as jnp
from jax import lax
from jax.experimental import pallas as pl
from jax.experimental.pallas import tpu as pltpu
from jax.sharding import PartitionSpec as P

HEAD = 64
TOP = 2
TRUNK = 256
SEG = 64
STEP = 5
SEGS = 13


NORM_EPS = 1e-06
BETA_ONE = 0.5
BETA_TWO = 0.5
ADAM_EPS = 1e-08
DECAY = 0.01
RATES = (0.02, 0.15, 0.3, 0.02, 0.012, 0.02, 0.012)

LOW = jnp.bfloat16
FULL = jnp.float32


def dot(a, b):
    return jnp.dot(a, b, preferred_element_type=FULL)


def dot_nt(a, b):
    return lax.dot_general(a, b, (((1,), (1,)), ((), ())), preferred_element_type=FULL)


def dot_tn(a, b):
    return lax.dot_general(a, b, (((0,), (0,)), ((), ())), preferred_element_type=FULL)


def rms_factor(values):
    return lax.rsqrt(jnp.mean(values * values, axis=-1, keepdims=True) + NORM_EPS)


def rms_back(values, factor, gain, grad):
    hat = values * factor
    scaled = grad * gain
    return factor * (scaled - hat * jnp.mean(scaled * hat, axis=-1, keepdims=True)), hat


def rotary_tables(position):
    half = HEAD // 2
    frequency = 10000.0 ** (-jnp.arange(half, dtype=FULL) / half)
    angles = position[:, None] * frequency[None, :]
    return jnp.cos(angles)[:, None, :], jnp.sin(angles)[:, None, :]


def rotate(values, cosine, sine):
    half = values.shape[-1] // 2
    one, two = values[..., :half], values[..., half:]
    return jnp.concatenate([one * cosine - two * sine, two * cosine + one * sine], axis=-1)


def tree_layout(parent_row, places):
    segment = jnp.where(places < TRUNK, 0, 1 + (places - TRUNK) // SEG)
    seg_start = jnp.where(segment == 0, 0, TRUNK + (segment - 1) * SEG)
    matches = segment[:, None] == jnp.arange(SEGS, dtype=jnp.int32)[None, :]
    upward = jnp.sum(jnp.where(matches, parent_row[None, :], 0), axis=1)
    depth_base = jnp.where(upward == 0, TRUNK, TRUNK + SEG)
    position = jnp.where(segment == 0, places, depth_base + places - seg_start)
    return (segment, upward, position)


def allowed_mask(segment, upward, places):
    same_segment = (segment[None, :] == segment[:, None]) & (places[None, :] <= places[:, None])
    ancestor = (segment[:, None] != 0) & (
        (segment[None, :] == 0) | (segment[None, :] == upward[:, None])
    )
    return same_segment | ancestor


def attend_forward(queries, keys, values, allowed):
    scale = 1.0 / math.sqrt(HEAD)
    scores = jnp.einsum("qhd,khd->hqk", queries, keys, preferred_element_type=FULL) * scale
    scores = jnp.where(allowed[None], scores, -1e30)
    row_top = jnp.max(scores, axis=-1, keepdims=True)
    shifted = jnp.exp(scores - row_top)
    row_total = jnp.sum(shifted, axis=-1, keepdims=True)
    weights = (shifted / row_total).astype(LOW)
    attended = jnp.einsum("hqk,khd->qhd", weights, values, preferred_element_type=FULL)
    return attended, row_top + jnp.log(row_total)


def attend_backward(queries, keys, values, allowed, grad_attended, log_totals):
    scale = 1.0 / math.sqrt(HEAD)
    scores = jnp.einsum("qhd,khd->hqk", queries, keys, preferred_element_type=FULL) * scale
    scores = jnp.where(allowed[None], scores, -1e30)
    probs = jnp.exp(scores - log_totals)
    grad_probs = jnp.einsum("qhd,khd->hqk", grad_attended, values, preferred_element_type=FULL)
    inner = jnp.sum(probs * grad_probs, axis=-1, keepdims=True)
    grad_scores = (probs * (grad_probs - inner)).astype(LOW)
    grad_query = jnp.einsum("hqk,khd->qhd", grad_scores, keys, preferred_element_type=FULL) * scale
    grad_key = jnp.einsum("hqk,qhd->khd", grad_scores, queries, preferred_element_type=FULL) * scale
    grad_value = jnp.einsum(
        "hqk,qhd->khd", probs.astype(LOW), grad_attended, preferred_element_type=FULL
    )
    return grad_query, grad_key, grad_value


def branch_rows_kernel(chunks, x_ref, g_ref, *refs):
    weights = refs[:chunks]
    hidden_ref, ggate_ref, gup_ref, grad_ref, xt_ref, gt_ref = refs[chunks:]
    x, g = x_ref[...], g_ref[...]
    xt_ref[...] = x.T
    gt_ref[...] = g.T
    total = None
    for chunk in range(chunks):
        w = weights[chunk]
        size = w.shape[2]
        at = pl.ds(chunk * size, size)
        gate, up, grad_hidden = dot(x, w[0]), dot(x, w[1]), dot(g, w[2])
        sigmoid = 1.0 / (1.0 + jnp.exp(-gate))
        active = gate * sigmoid
        hidden_ref[:, at] = (active * up).astype(LOW)
        ggate = (grad_hidden * up * sigmoid * (1.0 + gate * (1.0 - sigmoid))).astype(LOW)
        gup = (grad_hidden * active).astype(LOW)
        ggate_ref[:, at] = ggate
        gup_ref[:, at] = gup
        part = dot_nt(ggate, w[0]) + dot_nt(gup, w[1])
        total = part if total is None else total + part
    grad_ref[...] = total.astype(LOW)


def branch_rows(x, g, chunks):
    rows, width = x.shape
    size = chunks[0].shape[2]
    hidden = size * len(chunks)
    block = math.gcd(rows, 256)
    row_spec = pl.BlockSpec((block, width), lambda i: (i, 0))
    hidden_spec = pl.BlockSpec((block, hidden), lambda i: (i, 0))
    whole = [
        pl.BlockSpec(w.shape, lambda i: (0, 0, 0), pipeline_mode=pl.Buffered(1)) for w in chunks
    ]
    hidden_type = jax.ShapeDtypeStruct((rows, hidden), LOW)
    turned_spec = pl.BlockSpec((width, block), lambda i: (0, i))
    turned_type = jax.ShapeDtypeStruct((width, rows), LOW)
    return pl.pallas_call(
        functools.partial(branch_rows_kernel, len(chunks)),
        grid=(rows // block,),
        in_specs=[row_spec, row_spec] + whole,
        out_specs=[hidden_spec] * 3 + [row_spec] + [turned_spec] * 2,
        out_shape=[hidden_type] * 3
        + [jax.ShapeDtypeStruct((rows, width), LOW)]
        + [turned_type] * 2,
        compiler_params=pltpu.CompilerParams(vmem_limit_bytes=48 * 1024 * 1024),
        cost_estimate=pl.CostEstimate(
            flops=10 * rows * width * hidden,
            bytes_accessed=6 * (width * hidden + rows * hidden + rows * width),
            transcendentals=rows * hidden,
        ),
        name="branch_rows",
    )(x, g, *chunks)


def branch_out_kernel(chunks, hidden_ref, *refs):
    weights, out_ref = refs[:chunks], refs[chunks]
    total = None
    for chunk in range(chunks):
        w_out = weights[chunk][0]
        size = w_out.shape[1]
        part = dot_nt(hidden_ref[:, pl.ds(chunk * size, size)], w_out)
        total = part if total is None else total + part
    out_ref[...] = total.astype(LOW)


def branch_out(hidden, chunks):
    rows, size = hidden.shape
    width = chunks[0].shape[1]
    block = math.gcd(rows, 256)
    return pl.pallas_call(
        functools.partial(branch_out_kernel, len(chunks)),
        grid=(rows // block,),
        in_specs=[pl.BlockSpec((block, size), lambda i: (i, 0))]
        + [
            pl.BlockSpec(
                (1,) + w.shape[1:], lambda i: (2, 0, 0), pipeline_mode=pl.Buffered(1)
            )
            for w in chunks
        ],
        out_specs=pl.BlockSpec((block, width), lambda i: (i, 0)),
        out_shape=jax.ShapeDtypeStruct((rows, width), LOW),
        compiler_params=pltpu.CompilerParams(vmem_limit_bytes=48 * 1024 * 1024),
        cost_estimate=pl.CostEstimate(
            flops=2 * rows * width * size,
            bytes_accessed=2 * (width * size + rows * size + rows * width),
            transcendentals=0,
        ),
        name="branch_out",
    )(hidden, *chunks)


def branch_grads_kernel(xt_ref, gt_ref, hidden_ref, ggate_ref, gup_ref, grad_ref):
    xt = xt_ref[...]
    grad_ref[0, 0] = dot(xt, ggate_ref[...]).astype(LOW)
    grad_ref[0, 1] = dot(xt, gup_ref[...]).astype(LOW)
    grad_ref[0, 2] = dot(gt_ref[...], hidden_ref[...]).astype(LOW)


def branch_grads(turned, states, first, chunks, size):
    width, rows = turned[0].shape
    block = math.gcd(width, 256)
    turned_spec = pl.BlockSpec((block, rows), lambda j, i: (i, 0))
    hidden_spec = pl.BlockSpec((rows, size), lambda j, i: (0, first + j))
    return pl.pallas_call(
        branch_grads_kernel,
        grid=(chunks, width // block),
        in_specs=[turned_spec] * 2 + [hidden_spec] * 3,
        out_specs=pl.BlockSpec((1, 3, block, size), lambda j, i: (j, 0, i, 0)),
        out_shape=jax.ShapeDtypeStruct((chunks, 3, width, size), LOW),
        compiler_params=pltpu.CompilerParams(vmem_limit_bytes=48 * 1024 * 1024),
        cost_estimate=pl.CostEstimate(
            flops=6 * rows * width * size * chunks,
            bytes_accessed=6 * chunks * (width * size + rows * size + rows * width),
            transcendentals=0,
        ),
        name="branch_grads",
    )(*turned, *states)


def sum_turned_kernel(*refs):
    total = refs[0][0].astype(FULL)
    for ref in refs[1:-1]:
        total = total + ref[0].astype(FULL)
    refs[-1][...] = total.T


def sum_turned(parts):
    _, width, size = parts[0].shape
    block = math.gcd(width, 256)
    return pl.pallas_call(
        sum_turned_kernel,
        grid=(width // block,),
        in_specs=[pl.BlockSpec((1, block, size), lambda i: (2, i, 0))] * len(parts),
        out_specs=pl.BlockSpec((size, block), lambda i: (0, i)),
        out_shape=jax.ShapeDtypeStruct((size, width), FULL),
        name="sum_turned",
    )(*parts)


def adam_step(weight, mean_old, square_old, gradient, rate):
    mean_new = BETA_ONE * mean_old + (1.0 - BETA_ONE) * gradient
    square_new = BETA_TWO * square_old + (1.0 - BETA_TWO) * gradient * gradient
    mean_hat = mean_new / (1.0 - BETA_ONE**STEP)
    square_hat = square_new / (1.0 - BETA_TWO**STEP)
    updated = weight - rate * (mean_hat / (jnp.sqrt(square_hat) + ADAM_EPS) + DECAY * weight)
    return (mean_new, square_new, updated)


def swap(value, axis, mask, count):
    return lax.ppermute(value, axis, [(i, i ^ mask) for i in range(count)])


def after(value, *earlier):
    return lax.optimization_barrier((value,) + earlier)[0]


def by_rank(parts, rank):
    count = len(parts)
    ordered = []
    for place in range(count):
        chosen = parts[place]
        for other in range(1, count):
            chosen = jnp.where(rank == other, parts[place ^ other], chosen)
        ordered.append(chosen)
    return ordered


def gather_relative(value, count):
    if count != 4:
        rank = lax.axis_index("tensor")
        every = lax.all_gather(value, "tensor", axis=0)
        return [lax.dynamic_index_in_dim(every, rank ^ m, 0, False) for m in range(count)]
    far = swap(value, "tensor", 2, count)
    near = swap(value, "tensor", 1, count)
    return [value, near, far, swap(far, "tensor", 1, count)]


def send_relative(parts):
    count = len(parts)
    return [parts[0]] + [swap(parts[m], "tensor", m, count) for m in range(1, count)]


def sum_relative(parts):
    got = send_relative([p.astype(LOW) for p in parts])
    total = parts[0].astype(FULL)
    for part in got[1:]:
        total = total + part.astype(FULL)
    return total


def axis_bit(axis, mask):
    return (lax.axis_index(axis) // mask) % 2


def masks_of(count):
    return [1 << bit for bit in reversed(range(count.bit_length() - 1))]


def gather_doubling(value, axes, *earlier):
    steps = [(axis, mask, size) for axis, size in axes for mask in masks_of(size)]
    rest = value.ndim
    for axis, mask, size in steps:
        sent = after(value, *earlier) if earlier else value
        earlier = ()
        got = swap(sent, axis, mask, size)
        low_half = axis_bit(axis, mask) == 0
        value = jnp.stack([jnp.where(low_half, value, got), jnp.where(low_half, got, value)])
    order = tuple(reversed(range(len(steps))))
    value = value.transpose(order + tuple(len(steps) + dim for dim in range(rest)))
    return value.reshape((-1,) + value.shape[len(steps) :])


def sum_step(value, axis, mask, size, dim, *earlier):
    bit = axis_bit(axis, mask)
    kept = lax.dynamic_index_in_dim(value, bit, dim, False)
    sent = lax.dynamic_index_in_dim(value, 1 - bit, dim, False).astype(LOW)
    if earlier:
        sent = after(sent, *earlier)
    return kept.astype(FULL) + swap(sent, axis, mask, size).astype(FULL)


def sum_wide(value, wide):
    place = lax.axis_index("wide")
    parts = [lax.dynamic_index_in_dim(value, place ^ m, 0, False) for m in range(wide)]
    got = [swap(parts[m].astype(LOW), "wide", m, wide) for m in range(1, wide)]
    total = parts[0].astype(FULL)
    for part in got:
        total = total + part.astype(FULL)
    return total


def block_of(value, place, size, dim=0):
    return lax.dynamic_slice_in_dim(value, place * size, size, dim)


def exchange(value):
    return lax.all_to_all(value, "wide", split_axis=0, concat_axis=0, tiled=True)


def body(
    tokens,
    cotangent,
    gate_logits,
    routes,
    parents,
    mixing_in,
    mixing_in_mean,
    mixing_in_square,
    mixing_out,
    mixing_out_mean,
    mixing_out_square,
    norm_gains,
    norm_gains_mean,
    norm_gains_square,
    shared_in,
    shared_in_mean,
    shared_in_square,
    shared_out,
    shared_out_mean,
    shared_out_square,
    expert_in,
    expert_in_mean,
    expert_in_square,
    expert_out,
    expert_out_mean,
    expert_out_square,
):
    rows_dev, width = tokens.shape
    wide = lax.axis_size("wide")
    count = lax.axis_size("tensor")
    rank = lax.axis_index("tensor")
    tree_length = rows_dev * count
    capacity = 2 * rows_dev * TOP // wide
    slots = wide * capacity
    heads = width // HEAD
    heads_dev = -(-heads // count)
    head_pad = heads_dev * count - heads
    head_width = heads_dev * HEAD
    rows_weight = mixing_in.shape[0]

    cut = mixing_in.astype(LOW).reshape(rows_weight, 3, heads, HEAD)
    cut = jnp.pad(cut, ((0, 0), (0, 0), (0, head_pad), (0, 0)))
    cut = cut.reshape(rows_weight, 3, count, head_width).transpose(2, 0, 1, 3)
    cut = cut.reshape(count, rows_weight, 3 * head_width)
    gain_columns = jnp.broadcast_to(norm_gains.astype(LOW).T[None], (count, rows_weight, 2))
    cut = jnp.concatenate([cut, gain_columns], axis=2)
    own_cut = send_relative(
        [lax.dynamic_index_in_dim(cut, rank ^ m, 0, False) for m in range(count)]
    )
    got = gather_doubling(jnp.stack(by_rank(own_cut, rank)), [("wide", wide)])
    got = got.reshape(width, 3 * head_width + 2)
    w_qkv = got[:, : 3 * head_width]
    gain_pair = got[:, 3 * head_width :].astype(FULL).T

    both = jnp.concatenate([tokens, cotangent], axis=1)
    both = gather_relative(both, count)
    tokens_all = jnp.concatenate(by_rank([part[:, :width] for part in both], rank), axis=0)
    cotangent_rel = jnp.concatenate([part[:, width:] for part in both], axis=0)
    shared_low = jnp.concatenate(
        [shared_in.astype(LOW).transpose(1, 0, 2), shared_out.astype(LOW).T[None]], axis=0
    )
    w_shared = lax.all_gather(shared_low, "wide", axis=1, tiled=True)
    expert_low = jnp.concatenate(
        [expert_in[0].astype(LOW).transpose(1, 0, 2), expert_out.astype(LOW).transpose(0, 2, 1)],
        axis=0,
    )
    if count == 4:
        far = []
        for plane in range(3):
            far.append(
                swap(after(expert_low[plane], far[-1] if far else own_cut[1]), "tensor", 2, count)
            )
        far_low = jnp.stack(far)
        expert_chunks = [expert_low, far_low] + [
            swap(part, "tensor", 1, count) for part in (expert_low, far_low)
        ]
    else:
        far = [own_cut[1]] * 3
        expert_chunks = gather_relative(expert_low, count)
    w_mix_out = gather_doubling(
        mixing_out.astype(LOW), [("wide", wide), ("tensor", count)], own_cut[1]
    )
    w_mix_out = w_mix_out.reshape(width, width)

    own_routes = lax.dynamic_slice_in_dim(routes, rank * rows_dev, rows_dev, 0)
    own_logits = lax.dynamic_slice_in_dim(gate_logits, rank * rows_dev, rows_dev, 0)
    gates = jax.nn.softmax(own_logits, axis=-1)
    flat = own_routes.reshape(-1)
    named = (flat[:, None] == jnp.arange(wide, dtype=jnp.int32)[None, :]).astype(LOW)
    order = jnp.arange(flat.shape[0], dtype=jnp.int32)
    earlier = (order[None, :] < order[:, None]).astype(LOW)
    before = jnp.sum(dot(earlier, named) * named.astype(FULL), axis=1).astype(jnp.int32)
    places = (flat * capacity + before).reshape(rows_dev, TOP)
    slot_ids = jnp.arange(slots, dtype=jnp.int32)
    picks = [(slot_ids[:, None] == places[:, k][None, :]).astype(LOW) for k in range(TOP)]
    pick_any = picks[0] + picks[1]
    grad_out = cotangent.astype(FULL)
    grad_routes = [(gates[:, k : k + 1] * grad_out).astype(LOW) for k in range(TOP)]
    grad_slots = (dot(picks[0], grad_routes[0]) + dot(picks[1], grad_routes[1])).astype(LOW)
    grad_slots = after(grad_slots, own_cut[1])
    expert_grads = exchange(grad_slots.reshape(wide, capacity, width)).reshape(slots, width)

    tree_places = jnp.arange(tree_length, dtype=jnp.int32)
    segment, upward, position = tree_layout(parents[0], tree_places)
    allowed = allowed_mask(segment, upward, tree_places)
    cosine, sine = rotary_tables(position.astype(FULL))
    tree_rows = after(tokens_all, far[0]).astype(FULL)
    normed_one = (tree_rows * rms_factor(tree_rows) * gain_pair[0]).astype(LOW)
    projected = dot(normed_one, w_qkv).reshape(tree_length, 3, heads_dev, HEAD)
    queries = rotate(projected[:, 0], cosine, sine).astype(LOW)
    keys = rotate(projected[:, 1], cosine, sine).astype(LOW)
    values = projected[:, 2].astype(LOW)
    attended, log_totals = attend_forward(queries, keys, values, allowed)
    attended = attended.astype(LOW).reshape(tree_length, head_width)
    attended = after(attended, expert_grads, far[1])
    attended = send_relative([block_of(attended, rank ^ m, rows_dev) for m in range(count)])
    attended_low = jnp.concatenate(by_rank(attended, rank), axis=1)[:, :width]
    input_rows = tokens.astype(FULL)
    residual = input_rows + dot(attended_low, w_mix_out)
    factor_two = rms_factor(residual)
    normed_two = (residual * factor_two * gain_pair[1]).astype(LOW)

    row_slots = dot(pick_any, normed_two).astype(LOW)
    row_slots = after(row_slots, far[2])
    expert_rows = exchange(row_slots.reshape(wide, capacity, width)).reshape(slots, width)
    shared_rows = jnp.concatenate(gather_relative(normed_two, count), axis=0)
    *sh_states, sh_grad_rows, sh_xt, sh_gt = branch_rows(shared_rows, cotangent_rel, [w_shared])
    sh_part = branch_out(sh_states[0], [w_shared])
    sh_sums = jnp.concatenate([sh_grad_rows, sh_part], axis=1)
    sh_sums = sum_relative(jnp.split(sh_sums, count))
    sh_size = sh_states[0].shape[1]
    sh_grads = branch_grads((sh_xt, sh_gt), sh_states, 0, 1, sh_size)
    halves = masks_of(wide)
    sh_grads = sh_grads.reshape((3,) + (2,) * len(halves) + (width // wide, sh_size))
    sh_grads = sum_step(sh_grads, "wide", halves[-1], wide, len(halves))

    *ex_states, ex_grad_rows, ex_xt, ex_gt = branch_rows(expert_rows, expert_grads, expert_chunks)
    back_rows = exchange(ex_grad_rows.reshape(wide, capacity, width)).reshape(slots, width)
    for level in range(len(halves) - 2, 0, -1):
        sh_grads = sum_step(sh_grads, "wide", halves[level], wide, level + 1, ex_grad_rows)
    ex_size = ex_states[0].shape[1] // count
    ex_grads = functools.partial(branch_grads, (ex_xt, ex_gt), ex_states)
    if count == 4:
        ex_sent = swap(ex_grads(2, 2, ex_size), "tensor", 1, count)
        ex_kept = ex_grads(0, 2, ex_size)
    else:
        ex_sent, ex_kept = (), ex_grads(0, count, ex_size)
    out_rows = branch_out(ex_states[0], expert_chunks)
    back_rows, out_rows, ex_kept = lax.optimization_barrier((back_rows, out_rows, ex_kept))
    returned = exchange(out_rows.reshape(wide, capacity, width)).reshape(slots, width)

    grad_normed_two = dot_tn(pick_any, back_rows) + sh_sums[:, :width]
    grad_part, hat_two = rms_back(residual, factor_two, gain_pair[1], grad_normed_two)
    gain_two_part = jnp.sum(grad_normed_two * hat_two, axis=0)
    grad_residual = grad_out + grad_part
    grad_res_low = after(grad_residual.astype(LOW), ex_sent)
    w_mix_pad = jnp.pad(w_mix_out, ((0, head_pad * HEAD), (0, 0)))
    grad_attended = send_relative(
        [
            dot_nt(grad_res_low, block_of(w_mix_pad, rank ^ m, head_width)).astype(LOW)
            for m in range(count)
        ]
    )
    grad_attended = lax.optimization_barrier(grad_attended)
    grad_attended_all = jnp.concatenate(by_rank(grad_attended, rank), axis=0)
    grad_attended_all = grad_attended_all.reshape(tree_length, heads_dev, HEAD)
    grad_mix_out = dot_tn(attended_low, grad_res_low)
    halves_tensor = masks_of(count)
    grad_mix_out = grad_mix_out.reshape(
        (2,) * (len(halves) + len(halves_tensor)) + (rows_weight, width)
    )
    for level in range(len(halves_tensor) - 1, -1, -1):
        grad_mix_out = sum_step(
            grad_mix_out, "tensor", halves_tensor[level], count, len(halves) + level,
            grad_attended[0],
        )
    across = ()
    if count == 4:
        across = ex_kept[1].astype(FULL) + ex_sent[1].astype(FULL)
        across = after(across.astype(LOW), grad_attended[0], grad_mix_out)
        across = [swap(across[0], "tensor", 2, count), across]
    sh_grads = sum_step(sh_grads, "wide", halves[0], wide, 1, grad_attended[0])

    grad_query, grad_key, grad_value = attend_backward(
        queries, keys, values, allowed, grad_attended_all, log_totals
    )
    grad_projected = jnp.stack(
        [rotate(grad_query, cosine, -sine), rotate(grad_key, cosine, -sine), grad_value], axis=1
    )
    grad_projected = grad_projected.astype(LOW).reshape(tree_length, 3 * head_width)
    grad_normed_one = dot_nt(grad_projected, w_qkv).astype(LOW)
    grad_normed_one = sum_relative(
        [block_of(grad_normed_one, rank ^ m, rows_dev) for m in range(count)]
    )
    grad_mix_in = dot_tn(normed_one, grad_projected).astype(LOW)
    grad_mix_in = after(grad_mix_in, *across[:1])
    returned, sh_sums, sh_grads, grad_mix_out, ex_kept, ex_sent, across = lax.optimization_barrier(
        (returned, sh_sums, sh_grads, grad_mix_out, ex_kept, ex_sent, across, grad_projected)
    )[:7]
    for level in range(len(halves) - 1, -1, -1):
        grad_mix_out = sum_step(grad_mix_out, "wide", halves[level], wide, level)
    if count == 4:
        second = swap(after(across[1][1], across[0]), "tensor", 2, count)
        third = swap(after(across[1][2], second), "tensor", 2, count)
        across = jnp.stack([across[0], second, third])
        ex_parts = [ex_kept[0], ex_sent[0], across]
    else:
        ex_parts = send_relative([ex_kept[m] for m in range(count)])
    grad_ex_in = sum(part[:2].astype(FULL) for part in ex_parts).transpose(1, 0, 2)
    grad_ex_out = sum_turned(ex_parts)
    sent = jnp.concatenate([grad_mix_in, gain_two_part.astype(LOW)[:, None]], axis=1)
    got = lax.all_to_all(
        sent.reshape(wide * count, rows_weight, 3 * head_width + 1),
        ("wide", "tensor"),
        split_axis=0,
        concat_axis=0,
        tiled=True,
    )
    got = jnp.sum(got.astype(FULL).reshape(wide, count, rows_weight, -1), axis=0)
    grad_gain_two = jnp.sum(got[:, :, 3 * head_width], axis=0)
    grad_mix_in = got[:, :, : 3 * head_width].reshape(count, rows_weight, 3, head_width)
    grad_mix_in = grad_mix_in.transpose(1, 2, 0, 3).reshape(rows_weight, 3, count * head_width)
    grad_mix_in = grad_mix_in[:, :, :width].reshape(rows_weight, 3 * width)
    grad_gain_one = jnp.sum(mixing_in.astype(LOW).astype(FULL) * grad_mix_in, axis=1)
    grad_gain_one = grad_gain_one / norm_gains[0].astype(LOW).astype(FULL)

    grad_part, _ = rms_back(input_rows, rms_factor(input_rows), gain_pair[0], grad_normed_one)
    input_grad = grad_residual + grad_part

    per_route = [dot_tn(picks[k], returned) for k in range(TOP)]
    mixed = residual + gates[:, :1] * per_route[0] + gates[:, 1:] * per_route[1]
    mixed = mixed + sh_sums[:, width:]
    gate_grad = jnp.stack([jnp.sum(grad_out * rows, axis=-1) for rows in per_route], axis=1)
    logit_grad = gates * (gate_grad - jnp.sum(gates * gate_grad, axis=-1, keepdims=True))

    weights = (mixing_in, mixing_out, norm_gains, shared_in, shared_out, expert_in, expert_out)
    means = (
        mixing_in_mean,
        mixing_out_mean,
        norm_gains_mean,
        shared_in_mean,
        shared_out_mean,
        expert_in_mean,
        expert_out_mean,
    )
    squares = (
        mixing_in_square,
        mixing_out_square,
        norm_gains_square,
        shared_in_square,
        shared_out_square,
        expert_in_square,
        expert_out_square,
    )
    gradients = (
        grad_mix_in,
        grad_mix_out,
        jnp.stack([grad_gain_one, grad_gain_two]),
        sh_grads[:2].transpose(1, 0, 2),
        sh_grads[2].T,
        grad_ex_in[None],
        grad_ex_out[None],
    )
    results = [mixed.astype(LOW), input_grad, logit_grad]
    for number in range(7):
        results.extend(
            adam_step(
                weights[number], means[number], squares[number], gradients[number], RATES[number]
            )
        )
    return tuple(results)


def solution(mesh):
    placed = (
        P(("wide", "tensor"), None),
        P(("wide", "tensor"), None),
        P("wide", None),
        P("wide", None),
        P("wide", None),
        P(("wide", "tensor"), None),
        P(("wide", "tensor"), None),
        P(("wide", "tensor"), None),
        P(("wide", "tensor"), None),
        P(("wide", "tensor"), None),
        P(("wide", "tensor"), None),
        P(None, ("wide", "tensor")),
        P(None, ("wide", "tensor")),
        P(None, ("wide", "tensor")),
        P("wide", None, "tensor"),
        P("wide", None, "tensor"),
        P("wide", None, "tensor"),
        P("tensor", "wide"),
        P("tensor", "wide"),
        P("tensor", "wide"),
        P("wide", None, None, "tensor"),
        P("wide", None, None, "tensor"),
        P("wide", None, None, "tensor"),
        P("wide", "tensor", None),
        P("wide", "tensor", None),
        P("wide", "tensor", None),
    )
    return jax.shard_map(
        body,
        mesh=mesh,
        in_specs=placed,
        out_specs=(
            P(("wide", "tensor"), None),
            P(("wide", "tensor"), None),
            P(("wide", "tensor"), None),
            P(("wide", "tensor"), None),
            P(("wide", "tensor"), None),
            P(("wide", "tensor"), None),
            P(("wide", "tensor"), None),
            P(("wide", "tensor"), None),
            P(("wide", "tensor"), None),
            P(None, ("wide", "tensor")),
            P(None, ("wide", "tensor")),
            P(None, ("wide", "tensor")),
            P("wide", None, "tensor"),
            P("wide", None, "tensor"),
            P("wide", None, "tensor"),
            P("tensor", "wide"),
            P("tensor", "wide"),
            P("tensor", "wide"),
            P("wide", None, None, "tensor"),
            P("wide", None, None, "tensor"),
            P("wide", None, None, "tensor"),
            P("wide", "tensor", None),
            P("wide", "tensor", None),
            P("wide", "tensor", None),
        ),
        check_vma=False,
    )
```

```python
import functools
import math

import jax
import jax.numpy as jnp
from jax import lax
from jax.experimental import pallas as pl
from jax.experimental.pallas import tpu as pltpu
from jax.sharding import PartitionSpec as P

HEAD = 64
TOP = 2
TRUNK = 256
SEG = 64
STEP = 5
SEGS = 13


NORM_EPS = 1e-06
BETA_ONE = 0.5
BETA_TWO = 0.5
ADAM_EPS = 1e-08
DECAY = 0.01
RATES = (0.02, 0.15, 0.3, 0.02, 0.012, 0.02, 0.012)

LOW = jnp.bfloat16
FULL = jnp.float32
SMALL = pl.CostEstimate(flops=1000, bytes_accessed=1000, transcendentals=0)


def dot(a, b):
    return jnp.dot(a, b, preferred_element_type=FULL)


def dot_nt(a, b):
    return lax.dot_general(a, b, (((1,), (1,)), ((), ())), preferred_element_type=FULL)


def dot_tn(a, b):
    return lax.dot_general(a, b, (((0,), (0,)), ((), ())), preferred_element_type=FULL)


def rms_factor(values):
    return lax.rsqrt(jnp.mean(values * values, axis=-1, keepdims=True) + NORM_EPS)


def rms_back(values, factor, gain, grad):
    hat = values * factor
    scaled = grad * gain
    return factor * (scaled - hat * jnp.mean(scaled * hat, axis=-1, keepdims=True)), hat


def rotary_tables(position):
    half = HEAD // 2
    frequency = 10000.0 ** (-jnp.arange(half, dtype=FULL) / half)
    angles = position[:, None] * frequency[None, :]
    return jnp.cos(angles)[:, None, :], jnp.sin(angles)[:, None, :]


def rotate(values, cosine, sine):
    half = values.shape[-1] // 2
    one, two = values[..., :half], values[..., half:]
    return jnp.concatenate([one * cosine - two * sine, two * cosine + one * sine], axis=-1)


def tree_layout(parent_row, places):
    segment = jnp.where(places < TRUNK, 0, 1 + (places - TRUNK) // SEG)
    seg_start = jnp.where(segment == 0, 0, TRUNK + (segment - 1) * SEG)
    matches = segment[:, None] == jnp.arange(SEGS, dtype=jnp.int32)[None, :]
    upward = jnp.sum(jnp.where(matches, parent_row[None, :], 0), axis=1)
    depth_base = jnp.where(upward == 0, TRUNK, TRUNK + SEG)
    position = jnp.where(segment == 0, places, depth_base + places - seg_start)
    return (segment, upward, position)


def allowed_mask(segment, upward, places):
    same_segment = (segment[None, :] == segment[:, None]) & (places[None, :] <= places[:, None])
    ancestor = (segment[:, None] != 0) & (
        (segment[None, :] == 0) | (segment[None, :] == upward[:, None])
    )
    return same_segment | ancestor


def attend_forward(queries, keys, values, allowed):
    scale = 1.0 / math.sqrt(HEAD)
    scores = jnp.einsum("qhd,khd->hqk", queries, keys, preferred_element_type=FULL) * scale
    scores = jnp.where(allowed[None], scores, -1e30)
    row_top = jnp.max(scores, axis=-1, keepdims=True)
    shifted = jnp.exp(scores - row_top)
    row_total = jnp.sum(shifted, axis=-1, keepdims=True)
    weights = (shifted / row_total).astype(LOW)
    attended = jnp.einsum("hqk,khd->qhd", weights, values, preferred_element_type=FULL)
    return attended, row_top + jnp.log(row_total)


def attend_backward(queries, keys, values, allowed, grad_attended, log_totals):
    scale = 1.0 / math.sqrt(HEAD)
    scores = jnp.einsum("qhd,khd->hqk", queries, keys, preferred_element_type=FULL) * scale
    scores = jnp.where(allowed[None], scores, -1e30)
    probs = jnp.exp(scores - log_totals)
    grad_probs = jnp.einsum("qhd,khd->hqk", grad_attended, values, preferred_element_type=FULL)
    inner = jnp.sum(probs * grad_probs, axis=-1, keepdims=True)
    grad_scores = (probs * (grad_probs - inner)).astype(LOW)
    grad_query = jnp.einsum("hqk,khd->qhd", grad_scores, keys, preferred_element_type=FULL) * scale
    grad_key = jnp.einsum("hqk,qhd->khd", grad_scores, queries, preferred_element_type=FULL) * scale
    grad_value = jnp.einsum(
        "hqk,qhd->khd", probs.astype(LOW), grad_attended, preferred_element_type=FULL
    )
    return grad_query, grad_key, grad_value


def branch_rows_kernel(chunks, x_ref, g_ref, *refs):
    weights = refs[:chunks]
    hidden_ref, ggate_ref, gup_ref, grad_ref, xt_ref, gt_ref = refs[chunks:]
    x, g = x_ref[...], g_ref[...]
    xt_ref[...] = x.T
    gt_ref[...] = g.T
    total = None
    for chunk in range(chunks):
        w = weights[chunk]
        size = w.shape[2]
        at = pl.ds(chunk * size, size)
        gate, up, grad_hidden = dot(x, w[0]), dot(x, w[1]), dot(g, w[2])
        sigmoid = 1.0 / (1.0 + jnp.exp(-gate))
        active = gate * sigmoid
        hidden_ref[:, at] = (active * up).astype(LOW)
        ggate = (grad_hidden * up * sigmoid * (1.0 + gate * (1.0 - sigmoid))).astype(LOW)
        gup = (grad_hidden * active).astype(LOW)
        ggate_ref[:, at] = ggate
        gup_ref[:, at] = gup
        part = dot_nt(ggate, w[0]) + dot_nt(gup, w[1])
        total = part if total is None else total + part
    grad_ref[...] = total.astype(LOW)


def branch_rows(x, g, chunks):
    rows, width = x.shape
    size = chunks[0].shape[2]
    hidden = size * len(chunks)
    block = math.gcd(rows, 256)
    row_spec = pl.BlockSpec((block, width), lambda i: (i, 0))
    hidden_spec = pl.BlockSpec((block, hidden), lambda i: (i, 0))
    whole = [
        pl.BlockSpec(w.shape, lambda i: (0, 0, 0), pipeline_mode=pl.Buffered(1)) for w in chunks
    ]
    hidden_type = jax.ShapeDtypeStruct((rows, hidden), LOW)
    turned_spec = pl.BlockSpec((width, block), lambda i: (0, i))
    turned_type = jax.ShapeDtypeStruct((width, rows), LOW)
    return pl.pallas_call(
        functools.partial(branch_rows_kernel, len(chunks)),
        grid=(rows // block,),
        in_specs=[row_spec, row_spec] + whole,
        out_specs=[hidden_spec] * 3 + [row_spec] + [turned_spec] * 2,
        out_shape=[hidden_type] * 3
        + [jax.ShapeDtypeStruct((rows, width), LOW)]
        + [turned_type] * 2,
        compiler_params=pltpu.CompilerParams(vmem_limit_bytes=48 * 1024 * 1024),
        cost_estimate=SMALL,
        name="branch_rows",
    )(x, g, *chunks)


def branch_out_kernel(chunks, hidden_ref, *refs):
    weights, out_ref = refs[:chunks], refs[chunks]
    total = None
    for chunk in range(chunks):
        w_out = weights[chunk][0]
        size = w_out.shape[1]
        part = dot_nt(hidden_ref[:, pl.ds(chunk * size, size)], w_out)
        total = part if total is None else total + part
    out_ref[...] = total.astype(LOW)


def branch_out(hidden, chunks):
    rows, size = hidden.shape
    width = chunks[0].shape[1]
    block = math.gcd(rows, 256)
    return pl.pallas_call(
        functools.partial(branch_out_kernel, len(chunks)),
        grid=(rows // block,),
        in_specs=[pl.BlockSpec((block, size), lambda i: (i, 0))]
        + [
            pl.BlockSpec(
                (1,) + w.shape[1:], lambda i: (2, 0, 0), pipeline_mode=pl.Buffered(1)
            )
            for w in chunks
        ],
        out_specs=pl.BlockSpec((block, width), lambda i: (i, 0)),
        out_shape=jax.ShapeDtypeStruct((rows, width), LOW),
        compiler_params=pltpu.CompilerParams(vmem_limit_bytes=48 * 1024 * 1024),
        cost_estimate=SMALL,
        name="branch_out",
    )(hidden, *chunks)


def branch_grads_kernel(xt_ref, gt_ref, hidden_ref, ggate_ref, gup_ref, grad_ref):
    xt = xt_ref[...]
    grad_ref[0, 0] = dot(xt, ggate_ref[...]).astype(LOW)
    grad_ref[0, 1] = dot(xt, gup_ref[...]).astype(LOW)
    grad_ref[0, 2] = dot(gt_ref[...], hidden_ref[...]).astype(LOW)


def branch_grads(turned, states, first, chunks, size):
    width, rows = turned[0].shape
    block = math.gcd(width, 256)
    turned_spec = pl.BlockSpec((block, rows), lambda j, i: (i, 0))
    hidden_spec = pl.BlockSpec((rows, size), lambda j, i: (0, first + j))
    return pl.pallas_call(
        branch_grads_kernel,
        grid=(chunks, width // block),
        in_specs=[turned_spec] * 2 + [hidden_spec] * 3,
        out_specs=pl.BlockSpec((1, 3, block, size), lambda j, i: (j, 0, i, 0)),
        out_shape=jax.ShapeDtypeStruct((chunks, 3, width, size), LOW),
        compiler_params=pltpu.CompilerParams(vmem_limit_bytes=48 * 1024 * 1024),
        cost_estimate=SMALL,
        name="branch_grads",
    )(*turned, *states)


def adam_step(weight, mean_old, square_old, gradient, rate):
    mean_new = BETA_ONE * mean_old + (1.0 - BETA_ONE) * gradient
    square_new = BETA_TWO * square_old + (1.0 - BETA_TWO) * gradient * gradient
    mean_hat = mean_new / (1.0 - BETA_ONE**STEP)
    square_hat = square_new / (1.0 - BETA_TWO**STEP)
    updated = weight - rate * (mean_hat / (jnp.sqrt(square_hat) + ADAM_EPS) + DECAY * weight)
    return (mean_new, square_new, updated)


def sum_of(refs, plane):
    total = refs[0][plane].astype(FULL)
    for ref in refs[1:]:
        total = total + ref[plane].astype(FULL)
    return total


def adam_in_kernel(count, rate, *refs):
    parts, (w_ref, mean_ref, square_ref), outs = refs[:count], refs[count : count + 3], refs[-4:-1]
    grad_ref = refs[-1]
    _, rows, size = parts[0].shape
    tiles = size // 128
    for half in range(2):
        total = sum_of(parts, half)
        for tile in range(tiles):
            at = pl.ds(2 * tile + half, rows, 2 * tiles)
            grad_ref[at, :] = total[:, tile * 128 : (tile + 1) * 128]
    results = adam_step(w_ref[...], mean_ref[...], square_ref[...], grad_ref[...], rate)
    for ref, value in zip(outs, results):
        ref[...] = value


def adam_in(parts, weight, mean, square, rate):
    _, width, _, size = weight.shape
    tiles = size // 128
    block = math.gcd(width, 128)

    def rows_of(value):
        value = value[0].reshape(width, 2, tiles, 128).transpose(0, 2, 1, 3)
        return value.reshape(width * 2 * tiles, 128)

    spec = pl.BlockSpec((block * 2 * tiles, 128), lambda i: (i, 0))
    outs = pl.pallas_call(
        functools.partial(adam_in_kernel, len(parts), rate),
        grid=(width // block,),
        in_specs=[pl.BlockSpec((2, block, size), lambda i: (0, i, 0))] * len(parts) + [spec] * 3,
        out_specs=[spec] * 3,
        out_shape=[jax.ShapeDtypeStruct((width * 2 * tiles, 128), FULL)] * 3,
        scratch_shapes=[pltpu.VMEM((block * 2 * tiles, 128), FULL)],
        compiler_params=pltpu.CompilerParams(vmem_limit_bytes=48 * 1024 * 1024),
        cost_estimate=SMALL,
        name="adam_in",
    )(*parts, rows_of(weight), rows_of(mean), rows_of(square))
    return [
        out.reshape(width, tiles, 2, 128).transpose(0, 2, 1, 3).reshape(weight.shape)
        for out in outs
    ]


def adam_out_kernel(count, rate, *refs):
    parts, (w_ref, mean_ref, square_ref), outs = refs[:count], refs[count : count + 3], refs[-3:]
    total = sum_of(parts, 0).T
    results = adam_step(w_ref[0], mean_ref[0], square_ref[0], total, rate)
    for ref, value in zip(outs, results):
        ref[0] = value


def adam_out(parts, weight, mean, square, rate):
    _, size, width = weight.shape
    block = math.gcd(width, 128)
    spec = pl.BlockSpec((1, size, block), lambda i: (0, 0, i))
    return pl.pallas_call(
        functools.partial(adam_out_kernel, len(parts), rate),
        grid=(width // block,),
        in_specs=[pl.BlockSpec((1, block, size), lambda i: (2, i, 0))] * len(parts) + [spec] * 3,
        out_specs=[spec] * 3,
        out_shape=[jax.ShapeDtypeStruct(weight.shape, FULL)] * 3,
        compiler_params=pltpu.CompilerParams(vmem_limit_bytes=48 * 1024 * 1024),
        cost_estimate=SMALL,
        name="adam_out",
    )(*parts, weight, mean, square)


def swap(value, axis, mask, count):
    return lax.ppermute(value, axis, [(i, i ^ mask) for i in range(count)])


def after(value, *earlier):
    return lax.optimization_barrier((value,) + earlier)[0]


def by_rank(parts, rank):
    count = len(parts)
    ordered = []
    for place in range(count):
        chosen = parts[place]
        for other in range(1, count):
            chosen = jnp.where(rank == other, parts[place ^ other], chosen)
        ordered.append(chosen)
    return ordered


def gather_relative(value, count):
    if count != 4:
        rank = lax.axis_index("tensor")
        every = lax.all_gather(value, "tensor", axis=0)
        return [lax.dynamic_index_in_dim(every, rank ^ m, 0, False) for m in range(count)]
    far = swap(value, "tensor", 2, count)
    near = swap(value, "tensor", 1, count)
    return [value, near, far, swap(far, "tensor", 1, count)]


def send_relative(parts):
    count = len(parts)
    return [parts[0]] + [swap(parts[m], "tensor", m, count) for m in range(1, count)]


def sum_relative(parts):
    got = send_relative([p.astype(LOW) for p in parts])
    total = parts[0].astype(FULL)
    for part in got[1:]:
        total = total + part.astype(FULL)
    return total


def axis_bit(axis, mask):
    return (lax.axis_index(axis) // mask) % 2


def masks_of(count):
    return [1 << bit for bit in reversed(range(count.bit_length() - 1))]


def gather_doubling(value, axes, *earlier):
    steps = [(axis, mask, size) for axis, size in axes for mask in masks_of(size)]
    rest = value.ndim
    for axis, mask, size in steps:
        sent = after(value, *earlier) if earlier else value
        earlier = ()
        got = swap(sent, axis, mask, size)
        low_half = axis_bit(axis, mask) == 0
        value = jnp.stack([jnp.where(low_half, value, got), jnp.where(low_half, got, value)])
    order = tuple(reversed(range(len(steps))))
    value = value.transpose(order + tuple(len(steps) + dim for dim in range(rest)))
    return value.reshape((-1,) + value.shape[len(steps) :])


def sum_step(value, axis, mask, size, dim, *earlier):
    bit = axis_bit(axis, mask)
    kept = lax.dynamic_index_in_dim(value, bit, dim, False)
    sent = lax.dynamic_index_in_dim(value, 1 - bit, dim, False).astype(LOW)
    if earlier:
        sent = after(sent, *earlier)
    return kept.astype(FULL) + swap(sent, axis, mask, size).astype(FULL)


def sum_wide(value, wide):
    place = lax.axis_index("wide")
    parts = [lax.dynamic_index_in_dim(value, place ^ m, 0, False) for m in range(wide)]
    got = [swap(parts[m].astype(LOW), "wide", m, wide) for m in range(1, wide)]
    total = parts[0].astype(FULL)
    for part in got:
        total = total + part.astype(FULL)
    return total


def block_of(value, place, size, dim=0):
    return lax.dynamic_slice_in_dim(value, place * size, size, dim)


def exchange(value):
    return lax.all_to_all(value, "wide", split_axis=0, concat_axis=0, tiled=True)


def body(
    tokens,
    cotangent,
    gate_logits,
    routes,
    parents,
    mixing_in,
    mixing_in_mean,
    mixing_in_square,
    mixing_out,
    mixing_out_mean,
    mixing_out_square,
    norm_gains,
    norm_gains_mean,
    norm_gains_square,
    shared_in,
    shared_in_mean,
    shared_in_square,
    shared_out,
    shared_out_mean,
    shared_out_square,
    expert_in,
    expert_in_mean,
    expert_in_square,
    expert_out,
    expert_out_mean,
    expert_out_square,
):
    rows_dev, width = tokens.shape
    wide = lax.axis_size("wide")
    count = lax.axis_size("tensor")
    rank = lax.axis_index("tensor")
    tree_length = rows_dev * count
    capacity = 2 * rows_dev * TOP // wide
    slots = wide * capacity
    heads = width // HEAD
    heads_dev = -(-heads // count)
    head_pad = heads_dev * count - heads
    head_width = heads_dev * HEAD
    rows_weight = mixing_in.shape[0]

    cut = mixing_in.astype(LOW).reshape(rows_weight, 3, heads, HEAD)
    cut = jnp.pad(cut, ((0, 0), (0, 0), (0, head_pad), (0, 0)))
    cut = cut.reshape(rows_weight, 3, count, head_width).transpose(2, 0, 1, 3)
    cut = cut.reshape(count, rows_weight, 3 * head_width)
    gain_columns = jnp.broadcast_to(norm_gains.astype(LOW).T[None], (count, rows_weight, 2))
    cut = jnp.concatenate([cut, gain_columns], axis=2)
    sent = jnp.broadcast_to(cut[None], (wide,) + cut.shape).reshape(
        wide * count, rows_weight, 3 * head_width + 2
    )
    got = lax.all_to_all(sent, ("wide", "tensor"), split_axis=0, concat_axis=0, tiled=True)
    got = got.reshape(width, 3 * head_width + 2)
    w_qkv = got[:, : 3 * head_width]
    gain_pair = got[:, 3 * head_width :].astype(FULL).T

    token_parts = gather_relative(tokens, count)
    tokens_all = jnp.concatenate(by_rank(token_parts, rank), axis=0)
    expert_low = jnp.concatenate(
        [expert_in[0].astype(LOW).transpose(1, 0, 2), expert_out.astype(LOW).transpose(0, 2, 1)],
        axis=0,
    )
    expert_chunks = gather_relative(expert_low, count)
    if count == 4:
        expert_chunks = [expert_chunks[m] for m in (0, 2, 1, 3)]
    shared_low = jnp.concatenate(
        [shared_in.astype(LOW).transpose(1, 0, 2), shared_out.astype(LOW).T[None]], axis=0
    )
    w_shared = lax.all_gather(shared_low, "wide", axis=1, tiled=True)
    cotangent_all = lax.all_gather(cotangent, "tensor", axis=0)
    cotangent_rel = jnp.concatenate(
        [lax.dynamic_index_in_dim(cotangent_all, rank ^ m, 0, False) for m in range(count)], axis=0
    )
    w_mix_out = gather_doubling(mixing_out.astype(LOW), [("wide", wide), ("tensor", count)])
    w_mix_out = w_mix_out.reshape(width, width)

    own_routes = lax.dynamic_slice_in_dim(routes, rank * rows_dev, rows_dev, 0)
    own_logits = lax.dynamic_slice_in_dim(gate_logits, rank * rows_dev, rows_dev, 0)
    gates = jax.nn.softmax(own_logits, axis=-1)
    flat = own_routes.reshape(-1)
    named = (flat[:, None] == jnp.arange(wide, dtype=jnp.int32)[None, :]).astype(LOW)
    order = jnp.arange(flat.shape[0], dtype=jnp.int32)
    earlier = (order[None, :] < order[:, None]).astype(LOW)
    before = jnp.sum(dot(earlier, named) * named.astype(FULL), axis=1).astype(jnp.int32)
    places = (flat * capacity + before).reshape(rows_dev, TOP)
    slot_ids = jnp.arange(slots, dtype=jnp.int32)
    picks = [(slot_ids[:, None] == places[:, k][None, :]).astype(LOW) for k in range(TOP)]
    pick_any = picks[0] + picks[1]
    grad_out = cotangent.astype(FULL)
    grad_routes = [(gates[:, k : k + 1] * grad_out).astype(LOW) for k in range(TOP)]
    grad_slots = (dot(picks[0], grad_routes[0]) + dot(picks[1], grad_routes[1])).astype(LOW)
    grad_slots = after(grad_slots, got)
    expert_grads = exchange(grad_slots.reshape(wide, capacity, width)).reshape(slots, width)

    tree_places = jnp.arange(tree_length, dtype=jnp.int32)
    segment, upward, position = tree_layout(parents[0], tree_places)
    allowed = allowed_mask(segment, upward, tree_places)
    cosine, sine = rotary_tables(position.astype(FULL))
    tree_rows = tokens_all.astype(FULL)
    normed_one = (tree_rows * rms_factor(tree_rows) * gain_pair[0]).astype(LOW)
    projected = dot(normed_one, w_qkv).reshape(tree_length, 3, heads_dev, HEAD)
    queries = rotate(projected[:, 0], cosine, sine).astype(LOW)
    keys = rotate(projected[:, 1], cosine, sine).astype(LOW)
    values = projected[:, 2].astype(LOW)
    attended, log_totals = attend_forward(queries, keys, values, allowed)
    attended = attended.astype(LOW).reshape(tree_length, head_width)
    attended = after(attended, expert_chunks[1])
    attended_own = attended
    attended = send_relative([block_of(attended, rank ^ m, rows_dev) for m in range(count)])
    attended_low = jnp.concatenate(by_rank(attended, rank), axis=1)[:, :width]
    input_rows = tokens.astype(FULL)
    residual = input_rows + dot(attended_low, w_mix_out)
    factor_two = rms_factor(residual)
    normed_two = (residual * factor_two * gain_pair[1]).astype(LOW)

    row_slots = dot(pick_any, normed_two).astype(LOW)
    row_slots = after(row_slots, expert_grads)
    expert_rows = exchange(row_slots.reshape(wide, capacity, width)).reshape(slots, width)
    shared_rows = jnp.concatenate(gather_relative(normed_two, count), axis=0)
    *sh_states, sh_grad_rows, sh_xt, sh_gt = branch_rows(shared_rows, cotangent_rel, [w_shared])
    sh_part = branch_out(sh_states[0], [w_shared])
    sh_sums = jnp.concatenate([sh_grad_rows, sh_part], axis=1)
    sh_sums = sum_relative(jnp.split(sh_sums, count))
    sh_size = sh_states[0].shape[1]
    sh_grads = branch_grads((sh_xt, sh_gt), sh_states, 0, 1, sh_size)
    halves = masks_of(wide)
    sh_grads = sh_grads.reshape((3,) + (2,) * len(halves) + (width // wide, sh_size))
    sh_grads = sum_step(sh_grads, "wide", halves[-1], wide, len(halves))

    *ex_states, ex_grad_rows, ex_xt, ex_gt = branch_rows(expert_rows, expert_grads, expert_chunks)
    back_rows = exchange(ex_grad_rows.reshape(wide, capacity, width)).reshape(slots, width)
    for level in range(len(halves) - 2, 0, -1):
        sh_grads = sum_step(sh_grads, "wide", halves[level], wide, level + 1, ex_grad_rows)
    ex_size = ex_states[0].shape[1] // count
    ex_grads = functools.partial(branch_grads, (ex_xt, ex_gt), ex_states)
    if count == 4:
        ex_sent = swap(ex_grads(2, 2, ex_size), "tensor", 1, count)
        ex_kept = ex_grads(0, 2, ex_size)
    else:
        ex_sent, ex_kept = (), ex_grads(0, count, ex_size)
    out_rows = branch_out(ex_states[0], expert_chunks)
    back_rows, out_rows, ex_kept = lax.optimization_barrier((back_rows, out_rows, ex_kept))
    returned = exchange(out_rows.reshape(wide, capacity, width)).reshape(slots, width)

    grad_normed_two = dot_tn(pick_any, back_rows) + sh_sums[:, :width]
    grad_part, hat_two = rms_back(residual, factor_two, gain_pair[1], grad_normed_two)
    gain_two_part = jnp.sum(grad_normed_two * hat_two, axis=0)
    grad_residual = grad_out + grad_part
    grad_res_low = after(grad_residual.astype(LOW), ex_sent)
    w_mix_pad = jnp.pad(w_mix_out, ((0, head_pad * HEAD), (0, 0)))
    grad_res_parts = gather_relative(grad_res_low, count)
    grad_res_all = jnp.concatenate(by_rank(grad_res_parts, rank), axis=0)
    w_mix_own = block_of(w_mix_pad, rank, head_width)
    grad_attended = dot_nt(grad_res_all, w_mix_own).astype(LOW)
    grad_attended = grad_attended.reshape(tree_length, heads_dev, HEAD)
    if head_width == rows_weight * wide:
        grad_mix_out = dot_tn(attended_own, grad_res_all).astype(LOW)
        grad_mix_out = lax.psum_scatter(grad_mix_out, "wide", scatter_dimension=0, tiled=True)
        turns = [(w * count + t, t * wide + w) for w in range(wide) for t in range(count)]
    else:
        grad_mix_out = dot_tn(attended_low, grad_res_low).astype(LOW)
        grad_mix_out = lax.all_to_all(
            grad_mix_out.reshape(wide * count, rows_weight, width),
            ("wide", "tensor"),
            split_axis=0,
            concat_axis=0,
            tiled=True,
        )
        grad_mix_out = jnp.sum(grad_mix_out.astype(FULL), axis=0)
        turns = None
    across = ()
    if count == 4:
        across = ex_kept[1].astype(FULL) + ex_sent[1].astype(FULL)
        across = after(across.astype(LOW), grad_res_all)
        across = swap(across, "tensor", 2, count)
    sh_grads = sum_step(sh_grads, "wide", halves[0], wide, 1, grad_res_all)

    grad_query, grad_key, grad_value = attend_backward(
        queries, keys, values, allowed, grad_attended, log_totals
    )
    grad_projected = jnp.stack(
        [rotate(grad_query, cosine, -sine), rotate(grad_key, cosine, -sine), grad_value], axis=1
    )
    grad_projected = grad_projected.astype(LOW).reshape(tree_length, 3 * head_width)
    grad_normed_one = dot_nt(grad_projected, w_qkv).astype(LOW)
    grad_normed_one = sum_relative(
        [block_of(grad_normed_one, rank ^ m, rows_dev) for m in range(count)]
    )
    grad_mix_in = dot_tn(normed_one, grad_projected).astype(LOW)
    returned, sh_sums, sh_grads, grad_mix_out, ex_kept, ex_sent, across = lax.optimization_barrier(
        (returned, sh_sums, sh_grads, grad_mix_out, ex_kept, ex_sent, across, grad_projected)
    )[:7]
    if turns:
        grad_mix_out = lax.ppermute(grad_mix_out, ("wide", "tensor"), turns)
    grad_mix_out = grad_mix_out.astype(FULL)
    if count == 4:
        ex_parts = [ex_kept[0], ex_sent[0], across]
    else:
        ex_parts = send_relative([ex_kept[m] for m in range(count)])
    sent = jnp.concatenate([grad_mix_in, gain_two_part.astype(LOW)[:, None]], axis=1)
    got = lax.all_to_all(
        sent.reshape(wide * count, rows_weight, 3 * head_width + 1),
        ("wide", "tensor"),
        split_axis=0,
        concat_axis=0,
        tiled=True,
    )
    got = jnp.sum(got.astype(FULL).reshape(wide, count, rows_weight, -1), axis=0)
    grad_gain_two = jnp.sum(got[:, :, 3 * head_width], axis=0)
    grad_mix_in = got[:, :, : 3 * head_width].reshape(count, rows_weight, 3, head_width)
    grad_mix_in = grad_mix_in.transpose(1, 2, 0, 3).reshape(rows_weight, 3, count * head_width)
    grad_mix_in = grad_mix_in[:, :, :width].reshape(rows_weight, 3 * width)
    grad_gain_one = jnp.sum(mixing_in.astype(LOW).astype(FULL) * grad_mix_in, axis=1)
    grad_gain_one = grad_gain_one / norm_gains[0].astype(LOW).astype(FULL)

    grad_part, _ = rms_back(input_rows, rms_factor(input_rows), gain_pair[0], grad_normed_one)
    input_grad = grad_residual + grad_part

    per_route = [dot_tn(picks[k], returned) for k in range(TOP)]
    mixed = residual + gates[:, :1] * per_route[0] + gates[:, 1:] * per_route[1]
    mixed = mixed + sh_sums[:, width:]
    gate_grad = jnp.stack([jnp.sum(grad_out * rows, axis=-1) for rows in per_route], axis=1)
    logit_grad = gates * (gate_grad - jnp.sum(gates * gate_grad, axis=-1, keepdims=True))

    gradients = (
        (mixing_in, mixing_in_mean, mixing_in_square, grad_mix_in),
        (mixing_out, mixing_out_mean, mixing_out_square, grad_mix_out),
        (
            norm_gains,
            norm_gains_mean,
            norm_gains_square,
            jnp.stack([grad_gain_one, grad_gain_two]),
        ),
        (shared_in, shared_in_mean, shared_in_square, sh_grads[:2].transpose(1, 0, 2)),
        (shared_out, shared_out_mean, shared_out_square, sh_grads[2].T),
    )
    results = [mixed.astype(LOW), input_grad, logit_grad]
    for number, (weight, mean, square, gradient) in enumerate(gradients):
        results.extend(adam_step(weight, mean, square, gradient, RATES[number]))
    results.extend(adam_in(ex_parts, expert_in, expert_in_mean, expert_in_square, RATES[5]))
    results.extend(adam_out(ex_parts, expert_out, expert_out_mean, expert_out_square, RATES[6]))
    return tuple(results)


def solution(mesh):
    placed = (
        P(("wide", "tensor"), None),
        P(("wide", "tensor"), None),
        P("wide", None),
        P("wide", None),
        P("wide", None),
        P(("wide", "tensor"), None),
        P(("wide", "tensor"), None),
        P(("wide", "tensor"), None),
        P(("wide", "tensor"), None),
        P(("wide", "tensor"), None),
        P(("wide", "tensor"), None),
        P(None, ("wide", "tensor")),
        P(None, ("wide", "tensor")),
        P(None, ("wide", "tensor")),
        P("wide", None, "tensor"),
        P("wide", None, "tensor"),
        P("wide", None, "tensor"),
        P("tensor", "wide"),
        P("tensor", "wide"),
        P("tensor", "wide"),
        P("wide", None, None, "tensor"),
        P("wide", None, None, "tensor"),
        P("wide", None, None, "tensor"),
        P("wide", "tensor", None),
        P("wide", "tensor", None),
        P("wide", "tensor", None),
    )
    return jax.shard_map(
        body,
        mesh=mesh,
        in_specs=placed,
        out_specs=(
            P(("wide", "tensor"), None),
            P(("wide", "tensor"), None),
            P(("wide", "tensor"), None),
            P(("wide", "tensor"), None),
            P(("wide", "tensor"), None),
            P(("wide", "tensor"), None),
            P(("wide", "tensor"), None),
            P(("wide", "tensor"), None),
            P(("wide", "tensor"), None),
            P(None, ("wide", "tensor")),
            P(None, ("wide", "tensor")),
            P(None, ("wide", "tensor")),
            P("wide", None, "tensor"),
            P("wide", None, "tensor"),
            P("wide", None, "tensor"),
            P("tensor", "wide"),
            P("tensor", "wide"),
            P("tensor", "wide"),
            P("wide", None, None, "tensor"),
            P("wide", None, None, "tensor"),
            P("wide", None, None, "tensor"),
            P("wide", "tensor", None),
            P("wide", "tensor", None),
            P("wide", "tensor", None),
        ),
        check_vma=False,
    )
```

```python
import functools
import math

import jax
import jax.numpy as jnp
from jax import lax
from jax.experimental import pallas as pl
from jax.experimental.pallas import tpu as pltpu
from jax.sharding import PartitionSpec as P

HEAD = 64
TOP = 2
TRUNK = 256
SEG = 64
STEP = 5
SEGS = 13


NORM_EPS = 1e-06
BETA_ONE = 0.5
BETA_TWO = 0.5
ADAM_EPS = 1e-08
DECAY = 0.01
RATES = (0.02, 0.15, 0.3, 0.02, 0.012, 0.02, 0.012)

LOW = jnp.bfloat16
FULL = jnp.float32
SMALL = pl.CostEstimate(flops=1000, bytes_accessed=1000, transcendentals=0)


def dot(a, b):
    return jnp.dot(a, b, preferred_element_type=FULL)


def dot_nt(a, b):
    return lax.dot_general(a, b, (((1,), (1,)), ((), ())), preferred_element_type=FULL)


def dot_tn(a, b):
    return lax.dot_general(a, b, (((0,), (0,)), ((), ())), preferred_element_type=FULL)


def rms_factor(values):
    return lax.rsqrt(jnp.mean(values * values, axis=-1, keepdims=True) + NORM_EPS)


def rms_back(values, factor, gain, grad):
    hat = values * factor
    scaled = grad * gain
    return factor * (scaled - hat * jnp.mean(scaled * hat, axis=-1, keepdims=True)), hat


def rotary_tables(position):
    half = HEAD // 2
    frequency = 10000.0 ** (-jnp.arange(half, dtype=FULL) / half)
    angles = position[:, None] * frequency[None, :]
    return jnp.cos(angles)[:, None, :], jnp.sin(angles)[:, None, :]


def rotate(values, cosine, sine):
    half = values.shape[-1] // 2
    one, two = values[..., :half], values[..., half:]
    return jnp.concatenate([one * cosine - two * sine, two * cosine + one * sine], axis=-1)


def tree_layout(parent_row, places):
    segment = jnp.where(places < TRUNK, 0, 1 + (places - TRUNK) // SEG)
    seg_start = jnp.where(segment == 0, 0, TRUNK + (segment - 1) * SEG)
    matches = segment[:, None] == jnp.arange(SEGS, dtype=jnp.int32)[None, :]
    upward = jnp.sum(jnp.where(matches, parent_row[None, :], 0), axis=1)
    depth_base = jnp.where(upward == 0, TRUNK, TRUNK + SEG)
    position = jnp.where(segment == 0, places, depth_base + places - seg_start)
    return (segment, upward, position)


def allowed_mask(segment, upward, places):
    same_segment = (segment[None, :] == segment[:, None]) & (places[None, :] <= places[:, None])
    ancestor = (segment[:, None] != 0) & (
        (segment[None, :] == 0) | (segment[None, :] == upward[:, None])
    )
    return same_segment | ancestor


def attend_forward(queries, keys, values, allowed):
    scale = 1.0 / math.sqrt(HEAD)
    scores = jnp.einsum("qhd,khd->hqk", queries, keys, preferred_element_type=FULL) * scale
    scores = jnp.where(allowed[None], scores, -1e30)
    row_top = jnp.max(scores, axis=-1, keepdims=True)
    shifted = jnp.exp(scores - row_top)
    row_total = jnp.sum(shifted, axis=-1, keepdims=True)
    weights = (shifted / row_total).astype(LOW)
    attended = jnp.einsum("hqk,khd->qhd", weights, values, preferred_element_type=FULL)
    return attended, row_top + jnp.log(row_total)


def attend_backward(queries, keys, values, allowed, grad_attended, log_totals):
    scale = 1.0 / math.sqrt(HEAD)
    scores = jnp.einsum("qhd,khd->hqk", queries, keys, preferred_element_type=FULL) * scale
    scores = jnp.where(allowed[None], scores, -1e30)
    probs = jnp.exp(scores - log_totals)
    grad_probs = jnp.einsum("qhd,khd->hqk", grad_attended, values, preferred_element_type=FULL)
    inner = jnp.sum(probs * grad_probs, axis=-1, keepdims=True)
    grad_scores = (probs * (grad_probs - inner)).astype(LOW)
    grad_query = jnp.einsum("hqk,khd->qhd", grad_scores, keys, preferred_element_type=FULL) * scale
    grad_key = jnp.einsum("hqk,qhd->khd", grad_scores, queries, preferred_element_type=FULL) * scale
    grad_value = jnp.einsum(
        "hqk,qhd->khd", probs.astype(LOW), grad_attended, preferred_element_type=FULL
    )
    return grad_query, grad_key, grad_value


def branch_rows_kernel(chunks, x_ref, g_ref, *refs):
    weights = refs[:chunks]
    hidden_ref, ggate_ref, gup_ref, grad_ref, xt_ref, gt_ref = refs[chunks:]
    x, g = x_ref[...], g_ref[...]
    xt_ref[...] = x.T
    gt_ref[...] = g.T
    total = None
    for chunk in range(chunks):
        w = weights[chunk]
        size = w.shape[2]
        at = pl.ds(chunk * size, size)
        gate, up, grad_hidden = dot(x, w[0]), dot(x, w[1]), dot(g, w[2])
        sigmoid = 1.0 / (1.0 + jnp.exp(-gate))
        active = gate * sigmoid
        hidden_ref[:, at] = (active * up).astype(LOW)
        ggate = (grad_hidden * up * sigmoid * (1.0 + gate * (1.0 - sigmoid))).astype(LOW)
        gup = (grad_hidden * active).astype(LOW)
        ggate_ref[:, at] = ggate
        gup_ref[:, at] = gup
        part = dot_nt(ggate, w[0]) + dot_nt(gup, w[1])
        total = part if total is None else total + part
    grad_ref[...] = total.astype(LOW)


def branch_rows(x, g, chunks):
    rows, width = x.shape
    size = chunks[0].shape[2]
    hidden = size * len(chunks)
    block = math.gcd(rows, 256)
    row_spec = pl.BlockSpec((block, width), lambda i: (i, 0))
    hidden_spec = pl.BlockSpec((block, hidden), lambda i: (i, 0))
    whole = [
        pl.BlockSpec(w.shape, lambda i: (0, 0, 0), pipeline_mode=pl.Buffered(1)) for w in chunks
    ]
    hidden_type = jax.ShapeDtypeStruct((rows, hidden), LOW)
    turned_spec = pl.BlockSpec((width, block), lambda i: (0, i))
    turned_type = jax.ShapeDtypeStruct((width, rows), LOW)
    return pl.pallas_call(
        functools.partial(branch_rows_kernel, len(chunks)),
        grid=(rows // block,),
        in_specs=[row_spec, row_spec] + whole,
        out_specs=[hidden_spec] * 3 + [row_spec] + [turned_spec] * 2,
        out_shape=[hidden_type] * 3
        + [jax.ShapeDtypeStruct((rows, width), LOW)]
        + [turned_type] * 2,
        compiler_params=pltpu.CompilerParams(vmem_limit_bytes=48 * 1024 * 1024),
        cost_estimate=SMALL,
        name="branch_rows",
    )(x, g, *chunks)


def branch_out_kernel(chunks, hidden_ref, *refs):
    weights, out_ref = refs[:chunks], refs[chunks]
    total = None
    for chunk in range(chunks):
        w_out = weights[chunk][0]
        size = w_out.shape[1]
        part = dot_nt(hidden_ref[:, pl.ds(chunk * size, size)], w_out)
        total = part if total is None else total + part
    out_ref[...] = total.astype(LOW)


def branch_out(hidden, chunks):
    rows, size = hidden.shape
    width = chunks[0].shape[1]
    block = math.gcd(rows, 256)
    return pl.pallas_call(
        functools.partial(branch_out_kernel, len(chunks)),
        grid=(rows // block,),
        in_specs=[pl.BlockSpec((block, size), lambda i: (i, 0))]
        + [
            pl.BlockSpec(
                (1,) + w.shape[1:], lambda i: (2, 0, 0), pipeline_mode=pl.Buffered(1)
            )
            for w in chunks
        ],
        out_specs=pl.BlockSpec((block, width), lambda i: (i, 0)),
        out_shape=jax.ShapeDtypeStruct((rows, width), LOW),
        compiler_params=pltpu.CompilerParams(vmem_limit_bytes=48 * 1024 * 1024),
        cost_estimate=SMALL,
        name="branch_out",
    )(hidden, *chunks)


def branch_grads_kernel(xt_ref, gt_ref, hidden_ref, ggate_ref, gup_ref, grad_ref):
    xt = xt_ref[...]
    grad_ref[0, 0] = dot(xt, ggate_ref[...]).astype(LOW)
    grad_ref[0, 1] = dot(xt, gup_ref[...]).astype(LOW)
    grad_ref[0, 2] = dot(gt_ref[...], hidden_ref[...]).astype(LOW)


def branch_grads(turned, states, first, chunks, size):
    width, rows = turned[0].shape
    block = math.gcd(width, 256)
    turned_spec = pl.BlockSpec((block, rows), lambda j, i: (i, 0))
    hidden_spec = pl.BlockSpec((rows, size), lambda j, i: (0, first + j))
    return pl.pallas_call(
        branch_grads_kernel,
        grid=(chunks, width // block),
        in_specs=[turned_spec] * 2 + [hidden_spec] * 3,
        out_specs=pl.BlockSpec((1, 3, block, size), lambda j, i: (j, 0, i, 0)),
        out_shape=jax.ShapeDtypeStruct((chunks, 3, width, size), LOW),
        compiler_params=pltpu.CompilerParams(vmem_limit_bytes=48 * 1024 * 1024),
        cost_estimate=SMALL,
        name="branch_grads",
    )(*turned, *states)


def adam_step(weight, mean_old, square_old, gradient, rate):
    mean_new = BETA_ONE * mean_old + (1.0 - BETA_ONE) * gradient
    square_new = BETA_TWO * square_old + (1.0 - BETA_TWO) * gradient * gradient
    mean_hat = mean_new / (1.0 - BETA_ONE**STEP)
    square_hat = square_new / (1.0 - BETA_TWO**STEP)
    updated = weight - rate * (mean_hat / (jnp.sqrt(square_hat) + ADAM_EPS) + DECAY * weight)
    return (mean_new, square_new, updated)


def sum_of(refs, plane):
    total = refs[0][plane].astype(FULL)
    for ref in refs[1:]:
        total = total + ref[plane].astype(FULL)
    return total


def adam_in_kernel(count, rate, *refs):
    parts, (w_ref, mean_ref, square_ref), outs = refs[:count], refs[count : count + 3], refs[-4:-1]
    grad_ref = refs[-1]
    _, rows, size = parts[0].shape
    tiles = size // 128
    for half in range(2):
        total = sum_of(parts, half)
        for tile in range(tiles):
            at = pl.ds(2 * tile + half, rows, 2 * tiles)
            grad_ref[at, :] = total[:, tile * 128 : (tile + 1) * 128]
    results = adam_step(w_ref[...], mean_ref[...], square_ref[...], grad_ref[...], rate)
    for ref, value in zip(outs, results):
        ref[...] = value


def adam_in(parts, weight, mean, square, rate):
    _, width, _, size = weight.shape
    tiles = size // 128
    block = math.gcd(width, 128)

    def rows_of(value):
        value = value[0].reshape(width, 2, tiles, 128).transpose(0, 2, 1, 3)
        return value.reshape(width * 2 * tiles, 128)

    spec = pl.BlockSpec((block * 2 * tiles, 128), lambda i: (i, 0))
    outs = pl.pallas_call(
        functools.partial(adam_in_kernel, len(parts), rate),
        grid=(width // block,),
        in_specs=[pl.BlockSpec((2, block, size), lambda i: (0, i, 0))] * len(parts) + [spec] * 3,
        out_specs=[spec] * 3,
        out_shape=[jax.ShapeDtypeStruct((width * 2 * tiles, 128), FULL)] * 3,
        scratch_shapes=[pltpu.VMEM((block * 2 * tiles, 128), FULL)],
        compiler_params=pltpu.CompilerParams(vmem_limit_bytes=48 * 1024 * 1024),
        cost_estimate=SMALL,
        name="adam_in",
    )(*parts, rows_of(weight), rows_of(mean), rows_of(square))
    return [
        out.reshape(width, tiles, 2, 128).transpose(0, 2, 1, 3).reshape(weight.shape)
        for out in outs
    ]


def adam_out_kernel(count, rate, *refs):
    parts, (w_ref, mean_ref, square_ref), outs = refs[:count], refs[count : count + 3], refs[-3:]
    total = sum_of(parts, 0).T
    results = adam_step(w_ref[0], mean_ref[0], square_ref[0], total, rate)
    for ref, value in zip(outs, results):
        ref[0] = value


def adam_out(parts, weight, mean, square, rate):
    _, size, width = weight.shape
    block = math.gcd(width, 128)
    spec = pl.BlockSpec((1, size, block), lambda i: (0, 0, i))
    return pl.pallas_call(
        functools.partial(adam_out_kernel, len(parts), rate),
        grid=(width // block,),
        in_specs=[pl.BlockSpec((1, block, size), lambda i: (2, i, 0))] * len(parts) + [spec] * 3,
        out_specs=[spec] * 3,
        out_shape=[jax.ShapeDtypeStruct(weight.shape, FULL)] * 3,
        compiler_params=pltpu.CompilerParams(vmem_limit_bytes=48 * 1024 * 1024),
        cost_estimate=SMALL,
        name="adam_out",
    )(*parts, weight, mean, square)


def swap(value, axis, mask, count):
    return lax.ppermute(value, axis, [(i, i ^ mask) for i in range(count)])


def after(value, *earlier):
    return lax.optimization_barrier((value,) + earlier)[0]


def by_rank(parts, rank):
    count = len(parts)
    ordered = []
    for place in range(count):
        chosen = parts[place]
        for other in range(1, count):
            chosen = jnp.where(rank == other, parts[place ^ other], chosen)
        ordered.append(chosen)
    return ordered


def gather_relative(value, count):
    if count != 4:
        rank = lax.axis_index("tensor")
        every = lax.all_gather(value, "tensor", axis=0)
        return [lax.dynamic_index_in_dim(every, rank ^ m, 0, False) for m in range(count)]
    far = swap(value, "tensor", 2, count)
    near = swap(value, "tensor", 1, count)
    return [value, near, far, swap(far, "tensor", 1, count)]


def send_relative(parts):
    count = len(parts)
    return [parts[0]] + [swap(parts[m], "tensor", m, count) for m in range(1, count)]


def sum_relative(parts):
    got = send_relative([p.astype(LOW) for p in parts])
    total = parts[0].astype(FULL)
    for part in got[1:]:
        total = total + part.astype(FULL)
    return total


def block_of(value, place, size, dim=0):
    return lax.dynamic_slice_in_dim(value, place * size, size, dim)


def exchange(value):
    return lax.all_to_all(value, "wide", split_axis=0, concat_axis=0, tiled=True)


def body(
    tokens,
    cotangent,
    gate_logits,
    routes,
    parents,
    mixing_in,
    mixing_in_mean,
    mixing_in_square,
    mixing_out,
    mixing_out_mean,
    mixing_out_square,
    norm_gains,
    norm_gains_mean,
    norm_gains_square,
    shared_in,
    shared_in_mean,
    shared_in_square,
    shared_out,
    shared_out_mean,
    shared_out_square,
    expert_in,
    expert_in_mean,
    expert_in_square,
    expert_out,
    expert_out_mean,
    expert_out_square,
):
    rows_dev, width = tokens.shape
    wide = lax.axis_size("wide")
    count = lax.axis_size("tensor")
    rank = lax.axis_index("tensor")
    tree_length = rows_dev * count
    capacity = 2 * rows_dev * TOP // wide
    slots = wide * capacity
    heads = width // HEAD
    heads_dev = -(-heads // count)
    head_pad = heads_dev * count - heads
    head_width = heads_dev * HEAD
    rows_weight = mixing_in.shape[0]

    cut = mixing_in.astype(LOW).reshape(rows_weight, 3, heads, HEAD)
    cut = jnp.pad(cut, ((0, 0), (0, 0), (0, head_pad), (0, 0)))
    cut = cut.reshape(rows_weight, 3, count, head_width).transpose(2, 0, 1, 3)
    cut = cut.reshape(count, rows_weight, 3 * head_width)
    gain_columns = jnp.broadcast_to(norm_gains.astype(LOW).T[None], (count, rows_weight, 2))
    cut = jnp.concatenate([cut, gain_columns], axis=2)
    sent = jnp.broadcast_to(cut[None], (wide,) + cut.shape).reshape(
        wide * count, rows_weight, 3 * head_width + 2
    )
    got = lax.all_to_all(sent, ("wide", "tensor"), split_axis=0, concat_axis=0, tiled=True)
    got = got.reshape(width, 3 * head_width + 2)
    w_qkv = got[:, : 3 * head_width]
    gain_pair = got[:, 3 * head_width :].astype(FULL).T

    token_parts = gather_relative(tokens, count)
    tokens_all = jnp.concatenate(by_rank(token_parts, rank), axis=0)
    expert_low = jnp.concatenate(
        [expert_in[0].astype(LOW).transpose(1, 0, 2), expert_out.astype(LOW).transpose(0, 2, 1)],
        axis=0,
    )
    expert_chunks = gather_relative(expert_low, count)
    if count == 4:
        expert_chunks = [expert_chunks[m] for m in (0, 2, 1, 3)]
    shared_low = jnp.concatenate(
        [shared_in.astype(LOW).transpose(1, 0, 2), shared_out.astype(LOW).T[None]], axis=0
    )
    w_mix_out = lax.all_gather(mixing_out.astype(LOW), ("wide", "tensor"), axis=0, tiled=True)
    shared_low = after(shared_low, w_mix_out)
    w_shared = lax.all_gather(shared_low, "wide", axis=1, tiled=True)

    own_routes = lax.dynamic_slice_in_dim(routes, rank * rows_dev, rows_dev, 0)
    own_logits = lax.dynamic_slice_in_dim(gate_logits, rank * rows_dev, rows_dev, 0)
    gates = jax.nn.softmax(own_logits, axis=-1)
    flat = own_routes.reshape(-1)
    named = (flat[:, None] == jnp.arange(wide, dtype=jnp.int32)[None, :]).astype(LOW)
    order = jnp.arange(flat.shape[0], dtype=jnp.int32)
    earlier = (order[None, :] < order[:, None]).astype(LOW)
    before = jnp.sum(dot(earlier, named) * named.astype(FULL), axis=1).astype(jnp.int32)
    places = (flat * capacity + before).reshape(rows_dev, TOP)
    slot_ids = jnp.arange(slots, dtype=jnp.int32)
    picks = [(slot_ids[:, None] == places[:, k][None, :]).astype(LOW) for k in range(TOP)]
    pick_any = picks[0] + picks[1]
    grad_out = cotangent.astype(FULL)
    grad_routes = [(gates[:, k : k + 1] * grad_out).astype(LOW) for k in range(TOP)]
    grad_slots = (dot(picks[0], grad_routes[0]) + dot(picks[1], grad_routes[1])).astype(LOW)
    grad_slots = after(grad_slots, got)
    expert_grads = exchange(grad_slots.reshape(wide, capacity, width)).reshape(slots, width)

    tree_places = jnp.arange(tree_length, dtype=jnp.int32)
    segment, upward, position = tree_layout(parents[0], tree_places)
    allowed = allowed_mask(segment, upward, tree_places)
    cosine, sine = rotary_tables(position.astype(FULL))
    tree_rows = tokens_all.astype(FULL)
    normed_one = (tree_rows * rms_factor(tree_rows) * gain_pair[0]).astype(LOW)
    projected = dot(normed_one, w_qkv).reshape(tree_length, 3, heads_dev, HEAD)
    queries = rotate(projected[:, 0], cosine, sine).astype(LOW)
    keys = rotate(projected[:, 1], cosine, sine).astype(LOW)
    values = projected[:, 2].astype(LOW)
    attended, log_totals = attend_forward(queries, keys, values, allowed)
    attended = attended.astype(LOW).reshape(tree_length, head_width)
    attended_own = attended
    attended = send_relative([block_of(attended, rank ^ m, rows_dev) for m in range(count)])
    attended_low = jnp.concatenate(by_rank(attended, rank), axis=1)[:, :width]
    attended_low = after(attended_low, expert_chunks[1])
    input_rows = tokens.astype(FULL)
    residual = input_rows + dot(attended_low, w_mix_out)
    factor_two = rms_factor(residual)
    normed_two = (residual * factor_two * gain_pair[1]).astype(LOW)

    row_slots = dot(pick_any, normed_two).astype(LOW)
    row_slots = after(row_slots, expert_grads)
    expert_rows = exchange(row_slots.reshape(wide, capacity, width)).reshape(slots, width)
    shared_rows = jnp.concatenate(gather_relative(normed_two, count), axis=0)
    cotangent_late = after(cotangent, normed_two)
    cotangent_rel = jnp.concatenate(gather_relative(cotangent_late, count), axis=0)

    *ex_states, ex_grad_rows, ex_xt, ex_gt = branch_rows(expert_rows, expert_grads, expert_chunks)
    back_rows = exchange(ex_grad_rows.reshape(wide, capacity, width)).reshape(slots, width)
    shared_rows = after(shared_rows, ex_grad_rows)
    *sh_states, sh_grad_rows, sh_xt, sh_gt = branch_rows(shared_rows, cotangent_rel, [w_shared])
    sh_part = branch_out(sh_states[0], [w_shared])
    sh_sums = jnp.concatenate([sh_grad_rows, sh_part], axis=1)
    sh_sums = sum_relative(jnp.split(sh_sums, count))
    sh_size = sh_states[0].shape[1]
    sh_grads = branch_grads((sh_xt, sh_gt), sh_states, 0, 1, sh_size)
    rows_shared = width // wide
    sh_grads = sh_grads.reshape(3, wide, rows_shared, sh_size).transpose(1, 0, 2, 3)
    ex_size = ex_states[0].shape[1] // count
    ex_grads = functools.partial(branch_grads, (ex_xt, ex_gt), ex_states)
    if count == 4:
        ex_sent = swap(ex_grads(2, 2, ex_size), "tensor", 1, count)
        ex_kept = ex_grads(0, 2, ex_size)
    else:
        ex_sent, ex_kept = (), ex_grads(0, count, ex_size)
    out_rows = branch_out(ex_states[0], expert_chunks)
    back_rows, out_rows, ex_kept, sh_grads = lax.optimization_barrier(
        (back_rows, out_rows, ex_kept, sh_grads)
    )
    returned = exchange(out_rows.reshape(wide, capacity, width)).reshape(slots, width)

    grad_normed_two = dot_tn(pick_any, back_rows) + sh_sums[:, :width]
    grad_part, hat_two = rms_back(residual, factor_two, gain_pair[1], grad_normed_two)
    gain_two_part = jnp.sum(grad_normed_two * hat_two, axis=0)
    grad_residual = grad_out + grad_part
    grad_res_low = grad_residual.astype(LOW)
    w_mix_pad = jnp.pad(w_mix_out, ((0, head_pad * HEAD), (0, 0)))
    grad_res_parts = gather_relative(grad_res_low, count)
    grad_res_all = jnp.concatenate(by_rank(grad_res_parts, rank), axis=0)
    w_mix_own = block_of(w_mix_pad, rank, head_width)
    grad_attended = dot_nt(grad_res_all, w_mix_own).astype(LOW)
    grad_attended = grad_attended.reshape(tree_length, heads_dev, HEAD)
    if head_width == rows_weight * wide:
        grad_mix_out = dot_tn(attended_own, grad_res_all).astype(LOW)
        lines = rows_weight * width // sh_size
        sums = jnp.concatenate(
            [
                sh_grads.reshape(wide, 3 * rows_shared, sh_size),
                grad_mix_out.reshape(wide, lines, sh_size),
            ],
            axis=1,
        )
        grad_attended, sums = lax.optimization_barrier((grad_attended, sums))
        sums = lax.psum_scatter(sums, "wide", scatter_dimension=0, tiled=True)[0]
        turns = [(w * count + t, t * wide + w) for w in range(wide) for t in range(count)]
    else:
        grad_mix_out = dot_tn(attended_low, grad_res_low).astype(LOW)
        sums = lax.all_to_all(
            grad_mix_out.reshape(wide * count, rows_weight, width),
            ("wide", "tensor"),
            split_axis=0,
            concat_axis=0,
            tiled=True,
        )
        sh_grads = lax.psum_scatter(sh_grads, "wide", scatter_dimension=0, tiled=True)
        turns = None
    across = ()
    if count == 4:
        across = ex_kept[1].astype(FULL) + ex_sent[1].astype(FULL)
        across, grad_attended = lax.optimization_barrier((across.astype(LOW), grad_attended))
        across = swap(across, "tensor", 2, count)

    grad_query, grad_key, grad_value = attend_backward(
        queries, keys, values, allowed, grad_attended, log_totals
    )
    grad_projected = jnp.stack(
        [rotate(grad_query, cosine, -sine), rotate(grad_key, cosine, -sine), grad_value], axis=1
    )
    grad_projected = grad_projected.astype(LOW).reshape(tree_length, 3 * head_width)
    grad_normed_one = dot_nt(grad_projected, w_qkv).astype(LOW)
    grad_normed_one = sum_relative(
        [block_of(grad_normed_one, rank ^ m, rows_dev) for m in range(count)]
    )
    grad_mix_in = dot_tn(normed_one, grad_projected).astype(LOW)
    returned, sh_sums, sh_grads, sums, ex_kept, ex_sent, across = lax.optimization_barrier(
        (returned, sh_sums, sh_grads, sums, ex_kept, ex_sent, across, grad_projected)
    )[:7]
    if turns:
        sh_grads = sums[: 3 * rows_shared].reshape(3, rows_shared, sh_size).astype(FULL)
        grad_mix_out = sums[3 * rows_shared :].reshape(rows_weight, width)
        grad_mix_out = lax.ppermute(grad_mix_out, ("wide", "tensor"), turns).astype(FULL)
    else:
        sh_grads = sh_grads[0].astype(FULL)
        grad_mix_out = jnp.sum(sums.astype(FULL), axis=0)
    if count == 4:
        ex_parts = [ex_kept[0], ex_sent[0], across]
    else:
        ex_parts = send_relative([ex_kept[m] for m in range(count)])
    grad_mix_in = after(grad_mix_in, returned)
    sent = jnp.concatenate([grad_mix_in, gain_two_part.astype(LOW)[:, None]], axis=1)
    got = lax.all_to_all(
        sent.reshape(wide * count, rows_weight, 3 * head_width + 1),
        ("wide", "tensor"),
        split_axis=0,
        concat_axis=0,
        tiled=True,
    )
    got = jnp.sum(got.astype(FULL).reshape(wide, count, rows_weight, -1), axis=0)
    grad_gain_two = jnp.sum(got[:, :, 3 * head_width], axis=0)
    grad_mix_in = got[:, :, : 3 * head_width].reshape(count, rows_weight, 3, head_width)
    grad_mix_in = grad_mix_in.transpose(1, 2, 0, 3).reshape(rows_weight, 3, count * head_width)
    grad_mix_in = grad_mix_in[:, :, :width].reshape(rows_weight, 3 * width)
    grad_gain_one = jnp.sum(mixing_in.astype(LOW).astype(FULL) * grad_mix_in, axis=1)
    grad_gain_one = grad_gain_one / norm_gains[0].astype(LOW).astype(FULL)

    grad_part, _ = rms_back(input_rows, rms_factor(input_rows), gain_pair[0], grad_normed_one)
    input_grad = grad_residual + grad_part

    per_route = [dot_tn(picks[k], returned) for k in range(TOP)]
    mixed = residual + gates[:, :1] * per_route[0] + gates[:, 1:] * per_route[1]
    mixed = mixed + sh_sums[:, width:]
    gate_grad = jnp.stack([jnp.sum(grad_out * rows, axis=-1) for rows in per_route], axis=1)
    logit_grad = gates * (gate_grad - jnp.sum(gates * gate_grad, axis=-1, keepdims=True))

    gradients = (
        (mixing_in, mixing_in_mean, mixing_in_square, grad_mix_in),
        (mixing_out, mixing_out_mean, mixing_out_square, grad_mix_out),
        (
            norm_gains,
            norm_gains_mean,
            norm_gains_square,
            jnp.stack([grad_gain_one, grad_gain_two]),
        ),
        (shared_in, shared_in_mean, shared_in_square, sh_grads[:2].transpose(1, 0, 2)),
        (shared_out, shared_out_mean, shared_out_square, sh_grads[2].T),
    )
    results = [mixed.astype(LOW), input_grad, logit_grad]
    for number, (weight, mean, square, gradient) in enumerate(gradients):
        results.extend(adam_step(weight, mean, square, gradient, RATES[number]))
    results.extend(adam_in(ex_parts, expert_in, expert_in_mean, expert_in_square, RATES[5]))
    results.extend(adam_out(ex_parts, expert_out, expert_out_mean, expert_out_square, RATES[6]))
    return tuple(results)


def solution(mesh):
    placed = (
        P(("wide", "tensor"), None),
        P(("wide", "tensor"), None),
        P("wide", None),
        P("wide", None),
        P("wide", None),
        P(("wide", "tensor"), None),
        P(("wide", "tensor"), None),
        P(("wide", "tensor"), None),
        P(("wide", "tensor"), None),
        P(("wide", "tensor"), None),
        P(("wide", "tensor"), None),
        P(None, ("wide", "tensor")),
        P(None, ("wide", "tensor")),
        P(None, ("wide", "tensor")),
        P("wide", None, "tensor"),
        P("wide", None, "tensor"),
        P("wide", None, "tensor"),
        P("tensor", "wide"),
        P("tensor", "wide"),
        P("tensor", "wide"),
        P("wide", None, None, "tensor"),
        P("wide", None, None, "tensor"),
        P("wide", None, None, "tensor"),
        P("wide", "tensor", None),
        P("wide", "tensor", None),
        P("wide", "tensor", None),
    )
    return jax.shard_map(
        body,
        mesh=mesh,
        in_specs=placed,
        out_specs=(
            P(("wide", "tensor"), None),
            P(("wide", "tensor"), None),
            P(("wide", "tensor"), None),
            P(("wide", "tensor"), None),
            P(("wide", "tensor"), None),
            P(("wide", "tensor"), None),
            P(("wide", "tensor"), None),
            P(("wide", "tensor"), None),
            P(("wide", "tensor"), None),
            P(None, ("wide", "tensor")),
            P(None, ("wide", "tensor")),
            P(None, ("wide", "tensor")),
            P("wide", None, "tensor"),
            P("wide", None, "tensor"),
            P("wide", None, "tensor"),
            P("tensor", "wide"),
            P("tensor", "wide"),
            P("tensor", "wide"),
            P("wide", None, None, "tensor"),
            P("wide", None, None, "tensor"),
            P("wide", None, None, "tensor"),
            P("wide", "tensor", None),
            P("wide", "tensor", None),
            P("wide", "tensor", None),
        ),
        check_vma=False,
    )
```

```python
import functools
import math

import jax
import jax.numpy as jnp
from jax import lax
from jax.experimental import pallas as pl
from jax.experimental.pallas import tpu as pltpu
from jax.sharding import PartitionSpec as P

HEAD = 64
TOP = 2
TRUNK = 256
SEG = 64
STEP = 5
SEGS = 13


NORM_EPS = 1e-06
BETA_ONE = 0.5
BETA_TWO = 0.5
ADAM_EPS = 1e-08
DECAY = 0.01
RATES = (0.02, 0.15, 0.3, 0.02, 0.012, 0.02, 0.012)

LOW = jnp.bfloat16
FULL = jnp.float32
SMALL = pl.CostEstimate(flops=1000, bytes_accessed=1000, transcendentals=0)


def dot(a, b):
    return jnp.dot(a, b, preferred_element_type=FULL)


def dot_nt(a, b):
    return lax.dot_general(a, b, (((1,), (1,)), ((), ())), preferred_element_type=FULL)


def dot_tn(a, b):
    return lax.dot_general(a, b, (((0,), (0,)), ((), ())), preferred_element_type=FULL)


def rms_factor(values):
    return lax.rsqrt(jnp.mean(values * values, axis=-1, keepdims=True) + NORM_EPS)


def rms_back(values, factor, gain, grad):
    hat = values * factor
    scaled = grad * gain
    return factor * (scaled - hat * jnp.mean(scaled * hat, axis=-1, keepdims=True)), hat


def rotary_tables(position):
    half = HEAD // 2
    frequency = 10000.0 ** (-jnp.arange(half, dtype=FULL) / half)
    angles = position[:, None] * frequency[None, :]
    return jnp.cos(angles)[:, None, :], jnp.sin(angles)[:, None, :]


def rotate(values, cosine, sine):
    half = values.shape[-1] // 2
    one, two = values[..., :half], values[..., half:]
    return jnp.concatenate([one * cosine - two * sine, two * cosine + one * sine], axis=-1)


def tree_layout(parent_row, places):
    segment = jnp.where(places < TRUNK, 0, 1 + (places - TRUNK) // SEG)
    seg_start = jnp.where(segment == 0, 0, TRUNK + (segment - 1) * SEG)
    matches = segment[:, None] == jnp.arange(SEGS, dtype=jnp.int32)[None, :]
    upward = jnp.sum(jnp.where(matches, parent_row[None, :], 0), axis=1)
    depth_base = jnp.where(upward == 0, TRUNK, TRUNK + SEG)
    position = jnp.where(segment == 0, places, depth_base + places - seg_start)
    return (segment, upward, position)


def allowed_mask(segment, upward, places):
    same_segment = (segment[None, :] == segment[:, None]) & (places[None, :] <= places[:, None])
    ancestor = (segment[:, None] != 0) & (
        (segment[None, :] == 0) | (segment[None, :] == upward[:, None])
    )
    return same_segment | ancestor


def attend_forward(queries, keys, values, allowed):
    scale = 1.0 / math.sqrt(HEAD)
    scores = jnp.einsum("qhd,khd->hqk", queries, keys, preferred_element_type=FULL) * scale
    scores = jnp.where(allowed[None], scores, -1e30)
    row_top = jnp.max(scores, axis=-1, keepdims=True)
    shifted = jnp.exp(scores - row_top)
    row_total = jnp.sum(shifted, axis=-1, keepdims=True)
    weights = (shifted / row_total).astype(LOW)
    attended = jnp.einsum("hqk,khd->qhd", weights, values, preferred_element_type=FULL)
    return attended, row_top + jnp.log(row_total)


def attend_backward(queries, keys, values, allowed, grad_attended, log_totals):
    scale = 1.0 / math.sqrt(HEAD)
    scores = jnp.einsum("qhd,khd->hqk", queries, keys, preferred_element_type=FULL) * scale
    scores = jnp.where(allowed[None], scores, -1e30)
    probs = jnp.exp(scores - log_totals)
    grad_probs = jnp.einsum("qhd,khd->hqk", grad_attended, values, preferred_element_type=FULL)
    inner = jnp.sum(probs * grad_probs, axis=-1, keepdims=True)
    grad_scores = (probs * (grad_probs - inner)).astype(LOW)
    grad_query = jnp.einsum("hqk,khd->qhd", grad_scores, keys, preferred_element_type=FULL) * scale
    grad_key = jnp.einsum("hqk,qhd->khd", grad_scores, queries, preferred_element_type=FULL) * scale
    grad_value = jnp.einsum(
        "hqk,qhd->khd", probs.astype(LOW), grad_attended, preferred_element_type=FULL
    )
    return grad_query, grad_key, grad_value


def branch_rows_kernel(chunks, x_ref, g_ref, *refs):
    weights = refs[:chunks]
    hidden_ref, ggate_ref, gup_ref, grad_ref, xt_ref, gt_ref = refs[chunks:]
    x, g = x_ref[...], g_ref[...]
    xt_ref[...] = x.T
    gt_ref[...] = g.T
    total = None
    for chunk in range(chunks):
        w = weights[chunk]
        size = w.shape[2]
        at = pl.ds(chunk * size, size)
        gate, up, grad_hidden = dot(x, w[0]), dot(x, w[1]), dot(g, w[2])
        sigmoid = 1.0 / (1.0 + jnp.exp(-gate))
        active = gate * sigmoid
        hidden_ref[:, at] = (active * up).astype(LOW)
        ggate = (grad_hidden * up * sigmoid * (1.0 + gate * (1.0 - sigmoid))).astype(LOW)
        gup = (grad_hidden * active).astype(LOW)
        ggate_ref[:, at] = ggate
        gup_ref[:, at] = gup
        part = dot_nt(ggate, w[0]) + dot_nt(gup, w[1])
        total = part if total is None else total + part
    grad_ref[...] = total.astype(LOW)


def branch_rows(x, g, chunks):
    rows, width = x.shape
    size = chunks[0].shape[2]
    hidden = size * len(chunks)
    block = math.gcd(rows, 256)
    row_spec = pl.BlockSpec((block, width), lambda i: (i, 0))
    hidden_spec = pl.BlockSpec((block, hidden), lambda i: (i, 0))
    whole = [
        pl.BlockSpec(w.shape, lambda i: (0, 0, 0), pipeline_mode=pl.Buffered(1)) for w in chunks
    ]
    hidden_type = jax.ShapeDtypeStruct((rows, hidden), LOW)
    turned_spec = pl.BlockSpec((width, block), lambda i: (0, i))
    turned_type = jax.ShapeDtypeStruct((width, rows), LOW)
    return pl.pallas_call(
        functools.partial(branch_rows_kernel, len(chunks)),
        grid=(rows // block,),
        in_specs=[row_spec, row_spec] + whole,
        out_specs=[hidden_spec] * 3 + [row_spec] + [turned_spec] * 2,
        out_shape=[hidden_type] * 3
        + [jax.ShapeDtypeStruct((rows, width), LOW)]
        + [turned_type] * 2,
        compiler_params=pltpu.CompilerParams(vmem_limit_bytes=48 * 1024 * 1024),
        cost_estimate=SMALL,
        name="branch_rows",
    )(x, g, *chunks)


def branch_out_kernel(chunks, hidden_ref, *refs):
    weights, out_ref = refs[:chunks], refs[chunks]
    total = None
    for chunk in range(chunks):
        w_out = weights[chunk][0]
        size = w_out.shape[1]
        part = dot_nt(hidden_ref[:, pl.ds(chunk * size, size)], w_out)
        total = part if total is None else total + part
    out_ref[...] = total.astype(LOW)


def branch_out(hidden, chunks):
    rows, size = hidden.shape
    width = chunks[0].shape[1]
    block = math.gcd(rows, 256)
    return pl.pallas_call(
        functools.partial(branch_out_kernel, len(chunks)),
        grid=(rows // block,),
        in_specs=[pl.BlockSpec((block, size), lambda i: (i, 0))]
        + [
            pl.BlockSpec(
                (1,) + w.shape[1:], lambda i: (2, 0, 0), pipeline_mode=pl.Buffered(1)
            )
            for w in chunks
        ],
        out_specs=pl.BlockSpec((block, width), lambda i: (i, 0)),
        out_shape=jax.ShapeDtypeStruct((rows, width), LOW),
        compiler_params=pltpu.CompilerParams(vmem_limit_bytes=48 * 1024 * 1024),
        cost_estimate=SMALL,
        name="branch_out",
    )(hidden, *chunks)


def branch_grads_kernel(xt_ref, gt_ref, hidden_ref, ggate_ref, gup_ref, grad_ref):
    xt = xt_ref[...]
    grad_ref[0, 0] = dot(xt, ggate_ref[...]).astype(LOW)
    grad_ref[0, 1] = dot(xt, gup_ref[...]).astype(LOW)
    grad_ref[0, 2] = dot(gt_ref[...], hidden_ref[...]).astype(LOW)


def branch_grads(turned, states, first, chunks, size):
    width, rows = turned[0].shape
    block = math.gcd(width, 256)
    turned_spec = pl.BlockSpec((block, rows), lambda j, i: (i, 0))
    hidden_spec = pl.BlockSpec((rows, size), lambda j, i: (0, first + j))
    return pl.pallas_call(
        branch_grads_kernel,
        grid=(chunks, width // block),
        in_specs=[turned_spec] * 2 + [hidden_spec] * 3,
        out_specs=pl.BlockSpec((1, 3, block, size), lambda j, i: (j, 0, i, 0)),
        out_shape=jax.ShapeDtypeStruct((chunks, 3, width, size), LOW),
        compiler_params=pltpu.CompilerParams(vmem_limit_bytes=48 * 1024 * 1024),
        cost_estimate=SMALL,
        name="branch_grads",
    )(*turned, *states)


def adam_step(weight, mean_old, square_old, gradient, rate):
    mean_new = BETA_ONE * mean_old + (1.0 - BETA_ONE) * gradient
    square_new = BETA_TWO * square_old + (1.0 - BETA_TWO) * gradient * gradient
    mean_hat = mean_new / (1.0 - BETA_ONE**STEP)
    square_hat = square_new / (1.0 - BETA_TWO**STEP)
    updated = weight - rate * (mean_hat / (jnp.sqrt(square_hat) + ADAM_EPS) + DECAY * weight)
    return (mean_new, square_new, updated)


def shared_grads_kernel(xt_ref, gt_ref, hidden_ref, ggate_ref, gup_ref, grad_ref):
    groups, _, rows, _ = grad_ref.shape
    for plane, (turned, state) in enumerate(
        ((xt_ref, ggate_ref), (xt_ref, gup_ref), (gt_ref, hidden_ref))
    ):
        grad = dot(turned[...], state[...])
        for group in range(groups):
            grad_ref[group, plane] = grad[group * rows : (group + 1) * rows].astype(LOW)


def shared_grads(turned, states, wide):
    width, rows = turned[0].shape
    size = states[0].shape[1]
    share = width // wide
    groups = max(g for g in range(1, wide + 1) if wide % g == 0 and g * share <= 384)
    turned_spec = pl.BlockSpec((groups * share, rows), lambda i: (i, 0))
    return pl.pallas_call(
        shared_grads_kernel,
        grid=(wide // groups,),
        in_specs=[turned_spec] * 2 + [pl.BlockSpec((rows, size), lambda i: (0, 0))] * 3,
        out_specs=pl.BlockSpec((groups, 3, share, size), lambda i: (i, 0, 0, 0)),
        out_shape=jax.ShapeDtypeStruct((wide, 3, share, size), LOW),
        compiler_params=pltpu.CompilerParams(vmem_limit_bytes=48 * 1024 * 1024),
        cost_estimate=SMALL,
        name="shared_grads",
    )(*turned, *states)


def sum_of(refs, plane):
    total = refs[0][0, plane].astype(FULL)
    for ref in refs[1:]:
        total = total + ref[0, plane].astype(FULL)
    return total


def adam_in_kernel(count, rate, *refs):
    parts, (w_ref, mean_ref, square_ref), outs = refs[:count], refs[count : count + 3], refs[-4:-1]
    grad_ref = refs[-1]
    _, _, rows, size = parts[0].shape
    tiles = size // 128
    for half in range(2):
        total = sum_of(parts, half)
        for tile in range(tiles):
            at = pl.ds(2 * tile + half, rows, 2 * tiles)
            grad_ref[at, :] = total[:, tile * 128 : (tile + 1) * 128]
    results = adam_step(w_ref[...], mean_ref[...], square_ref[...], grad_ref[...], rate)
    for ref, value in zip(outs, results):
        ref[...] = value


def adam_in(parts, weight, mean, square, rate):
    _, width, _, size = weight.shape
    tiles = size // 128
    block = math.gcd(width, 128)

    def rows_of(value):
        value = value[0].reshape(width, 2, tiles, 128).transpose(0, 2, 1, 3)
        return value.reshape(width * 2 * tiles, 128)

    spec = pl.BlockSpec((block * 2 * tiles, 128), lambda i: (i, 0))
    outs = pl.pallas_call(
        functools.partial(adam_in_kernel, len(parts), rate),
        grid=(width // block,),
        in_specs=[pl.BlockSpec((1, 2, block, size), lambda i: (0, 0, i, 0))] * len(parts) + [spec] * 3,
        out_specs=[spec] * 3,
        out_shape=[jax.ShapeDtypeStruct((width * 2 * tiles, 128), FULL)] * 3,
        scratch_shapes=[pltpu.VMEM((block * 2 * tiles, 128), FULL)],
        compiler_params=pltpu.CompilerParams(vmem_limit_bytes=48 * 1024 * 1024),
        cost_estimate=SMALL,
        name="adam_in",
    )(*parts, rows_of(weight), rows_of(mean), rows_of(square))
    return [
        out.reshape(width, tiles, 2, 128).transpose(0, 2, 1, 3).reshape(weight.shape)
        for out in outs
    ]


def adam_out_kernel(count, rate, *refs):
    parts, (w_ref, mean_ref, square_ref), outs = refs[:count], refs[count : count + 3], refs[-3:]
    total = sum_of(parts, 0).T
    results = adam_step(w_ref[0], mean_ref[0], square_ref[0], total, rate)
    for ref, value in zip(outs, results):
        ref[0] = value


def adam_out(parts, weight, mean, square, rate):
    _, size, width = weight.shape
    block = math.gcd(width, 128)
    spec = pl.BlockSpec((1, size, block), lambda i: (0, 0, i))
    return pl.pallas_call(
        functools.partial(adam_out_kernel, len(parts), rate),
        grid=(width // block,),
        in_specs=[pl.BlockSpec((1, 1, block, size), lambda i: (0, 2, i, 0))] * len(parts) + [spec] * 3,
        out_specs=[spec] * 3,
        out_shape=[jax.ShapeDtypeStruct(weight.shape, FULL)] * 3,
        compiler_params=pltpu.CompilerParams(vmem_limit_bytes=48 * 1024 * 1024),
        cost_estimate=SMALL,
        name="adam_out",
    )(*parts, weight, mean, square)


def swap(value, axis, mask, count):
    return lax.ppermute(value, axis, [(i, i ^ mask) for i in range(count)])


def after(value, *earlier):
    return lax.optimization_barrier((value,) + earlier)[0]


def by_rank(parts, rank):
    count = len(parts)
    ordered = []
    for place in range(count):
        chosen = parts[place]
        for other in range(1, count):
            chosen = jnp.where(rank == other, parts[place ^ other], chosen)
        ordered.append(chosen)
    return ordered


def gather_relative(value, count):
    if count != 4:
        rank = lax.axis_index("tensor")
        every = lax.all_gather(value, "tensor", axis=0)
        return [lax.dynamic_index_in_dim(every, rank ^ m, 0, False) for m in range(count)]
    far = swap(value, "tensor", 2, count)
    near = swap(value, "tensor", 1, count)
    return [value, near, far, swap(far, "tensor", 1, count)]


def send_relative(parts):
    count = len(parts)
    return [parts[0]] + [swap(parts[m], "tensor", m, count) for m in range(1, count)]


def sum_relative(parts):
    got = send_relative([p.astype(LOW) for p in parts])
    total = parts[0].astype(FULL)
    for part in got[1:]:
        total = total + part.astype(FULL)
    return total


def sum_wide(value, wide):
    place = lax.axis_index("wide")
    parts = [lax.dynamic_index_in_dim(value, place ^ m, 0, False) for m in range(wide)]
    got = [swap(parts[m], "wide", m, wide) for m in range(1, wide)]
    total = parts[0].astype(FULL)
    for part in got:
        total = total + part.astype(FULL)
    return total


def masks_of(count):
    return [1 << bit for bit in reversed(range(count.bit_length() - 1))]


def gather_doubling(value, wide, count):
    steps = [("tensor", mask, count) for mask in masks_of(count)]
    steps += [("wide", mask, wide) for mask in masks_of(wide)]
    rest, first = value.ndim, None
    for axis, mask, size in steps:
        got = swap(value, axis, mask, size)
        first = got if first is None else first
        low_half = (lax.axis_index(axis) // mask) % 2 == 0
        value = jnp.stack([jnp.where(low_half, value, got), jnp.where(low_half, got, value)])
    ranked = sorted(range(len(steps)), key=lambda n: (steps[n][0] == "tensor", -steps[n][1]))
    order = tuple(len(steps) - 1 - n for n in ranked)
    value = value.transpose(order + tuple(len(steps) + dim for dim in range(rest)))
    return value.reshape((-1,) + value.shape[len(steps) :]), first


def block_of(value, place, size, dim=0):
    return lax.dynamic_slice_in_dim(value, place * size, size, dim)


def exchange(value):
    return lax.all_to_all(value, "wide", split_axis=0, concat_axis=0, tiled=True)


def body(
    tokens,
    cotangent,
    gate_logits,
    routes,
    parents,
    mixing_in,
    mixing_in_mean,
    mixing_in_square,
    mixing_out,
    mixing_out_mean,
    mixing_out_square,
    norm_gains,
    norm_gains_mean,
    norm_gains_square,
    shared_in,
    shared_in_mean,
    shared_in_square,
    shared_out,
    shared_out_mean,
    shared_out_square,
    expert_in,
    expert_in_mean,
    expert_in_square,
    expert_out,
    expert_out_mean,
    expert_out_square,
):
    rows_dev, width = tokens.shape
    wide = lax.axis_size("wide")
    count = lax.axis_size("tensor")
    rank = lax.axis_index("tensor")
    tree_length = rows_dev * count
    capacity = 2 * rows_dev * TOP // wide
    slots = wide * capacity
    heads = width // HEAD
    heads_dev = -(-heads // count)
    head_pad = heads_dev * count - heads
    head_width = heads_dev * HEAD
    rows_weight = mixing_in.shape[0]

    token_parts = gather_relative(tokens, count)
    tokens_all = jnp.concatenate(by_rank(token_parts, rank), axis=0)
    w_mix_out, first = gather_doubling(mixing_out.astype(LOW), wide, count)
    w_mix_out = w_mix_out.reshape(width, width)
    shared_low = jnp.concatenate(
        [shared_in.astype(LOW).transpose(1, 0, 2), shared_out.astype(LOW).T[None]], axis=0
    )
    w_shared = lax.all_gather(shared_low, "wide", axis=1, tiled=True)
    expert_low = jnp.concatenate(
        [expert_in[0].astype(LOW).transpose(1, 0, 2), expert_out.astype(LOW).transpose(0, 2, 1)],
        axis=0,
    )
    expert_low = after(expert_low, first)
    expert_chunks = gather_relative(expert_low, count)
    if count == 4:
        expert_chunks = [expert_chunks[m] for m in (0, 2, 1, 3)]

    cut = mixing_in.astype(LOW).reshape(rows_weight, 3, heads, HEAD)
    cut = jnp.pad(cut, ((0, 0), (0, 0), (0, head_pad), (0, 0)))
    cut = cut.reshape(rows_weight, 3, count, head_width).transpose(2, 0, 1, 3)
    cut = cut.reshape(count, rows_weight, 3 * head_width)
    gain_columns = jnp.broadcast_to(norm_gains.astype(LOW).T[None], (count, rows_weight, 2))
    cut = jnp.concatenate([cut, gain_columns], axis=2)
    sent = jnp.broadcast_to(cut[None], (wide,) + cut.shape).reshape(
        wide * count, rows_weight, 3 * head_width + 2
    )
    sent = after(sent, expert_low, shared_low)
    got = lax.all_to_all(sent, ("wide", "tensor"), split_axis=0, concat_axis=0, tiled=True)
    got = got.reshape(width, 3 * head_width + 2)
    w_qkv = got[:, : 3 * head_width]
    gain_pair = got[:, 3 * head_width :].astype(FULL).T

    own_routes = lax.dynamic_slice_in_dim(routes, rank * rows_dev, rows_dev, 0)
    own_logits = lax.dynamic_slice_in_dim(gate_logits, rank * rows_dev, rows_dev, 0)
    gates = jax.nn.softmax(own_logits, axis=-1)
    flat = own_routes.reshape(-1)
    named = (flat[:, None] == jnp.arange(wide, dtype=jnp.int32)[None, :]).astype(LOW)
    order = jnp.arange(flat.shape[0], dtype=jnp.int32)
    earlier = (order[None, :] < order[:, None]).astype(LOW)
    before = jnp.sum(dot(earlier, named) * named.astype(FULL), axis=1).astype(jnp.int32)
    places = (flat * capacity + before).reshape(rows_dev, TOP)
    slot_ids = jnp.arange(slots, dtype=jnp.int32)
    picks = [(slot_ids[:, None] == places[:, k][None, :]).astype(LOW) for k in range(TOP)]
    pick_any = picks[0] + picks[1]
    grad_out = cotangent.astype(FULL)
    grad_routes = [(gates[:, k : k + 1] * grad_out).astype(LOW) for k in range(TOP)]
    grad_slots = (dot(picks[0], grad_routes[0]) + dot(picks[1], grad_routes[1])).astype(LOW)
    grad_slots = after(grad_slots, got)
    expert_grads = exchange(grad_slots.reshape(wide, capacity, width)).reshape(slots, width)

    tree_places = jnp.arange(tree_length, dtype=jnp.int32)
    segment, upward, position = tree_layout(parents[0], tree_places)
    allowed = allowed_mask(segment, upward, tree_places)
    cosine, sine = rotary_tables(position.astype(FULL))
    tree_rows = tokens_all.astype(FULL)
    normed_one = (tree_rows * rms_factor(tree_rows) * gain_pair[0]).astype(LOW)
    projected = dot(normed_one, w_qkv).reshape(tree_length, 3, heads_dev, HEAD)
    queries = rotate(projected[:, 0], cosine, sine).astype(LOW)
    keys = rotate(projected[:, 1], cosine, sine).astype(LOW)
    values = projected[:, 2].astype(LOW)
    attended, log_totals = attend_forward(queries, keys, values, allowed)
    attended = attended.astype(LOW).reshape(tree_length, head_width)
    attended_own = attended
    attended = send_relative([block_of(attended, rank ^ m, rows_dev) for m in range(count)])
    attended_low = jnp.concatenate(by_rank(attended, rank), axis=1)[:, :width]
    attended_low = after(attended_low, expert_chunks[1])
    input_rows = tokens.astype(FULL)
    residual = input_rows + dot(attended_low, w_mix_out)
    factor_two = rms_factor(residual)
    normed_two = (residual * factor_two * gain_pair[1]).astype(LOW)

    row_slots = dot(pick_any, normed_two).astype(LOW)
    row_slots = after(row_slots, expert_grads)
    expert_rows = exchange(row_slots.reshape(wide, capacity, width)).reshape(slots, width)
    shared_rows = jnp.concatenate(gather_relative(normed_two, count), axis=0)
    cotangent_late = after(cotangent, expert_chunks[1])
    cotangent_rel = jnp.concatenate(gather_relative(cotangent_late, count), axis=0)
    *sh_states, sh_grad_rows, sh_xt, sh_gt = branch_rows(shared_rows, cotangent_rel, [w_shared])
    sh_part = branch_out(sh_states[0], [w_shared])
    sh_sums = jnp.concatenate([sh_grad_rows, sh_part], axis=1)
    sh_grads = shared_grads((sh_xt, sh_gt), sh_states, wide)
    expert_rows, sh_sums, sh_grads = lax.optimization_barrier((expert_rows, sh_sums, sh_grads))
    sh_sums = sum_relative(jnp.split(sh_sums, count))
    sh_grads = lax.psum_scatter(sh_grads, "wide", scatter_dimension=0, tiled=True)

    *ex_states, ex_grad_rows, ex_xt, ex_gt = branch_rows(expert_rows, expert_grads, expert_chunks)
    back_rows = exchange(ex_grad_rows.reshape(wide, capacity, width)).reshape(slots, width)
    ex_size = ex_states[0].shape[1] // count
    ex_grads = functools.partial(branch_grads, (ex_xt, ex_gt), ex_states)
    if count == 4:
        ex_sent = swap(ex_grads(2, 2, ex_size), "tensor", 1, count)
        ex_kept = ex_grads(0, 2, ex_size)
    else:
        ex_sent, ex_kept = (), ex_grads(0, count, ex_size)
    out_rows = branch_out(ex_states[0], expert_chunks)
    back_rows, out_rows, ex_kept = lax.optimization_barrier((back_rows, out_rows, ex_kept))
    returned = exchange(out_rows.reshape(wide, capacity, width)).reshape(slots, width)

    grad_normed_two = dot_tn(pick_any, back_rows) + sh_sums[:, :width]
    grad_part, hat_two = rms_back(residual, factor_two, gain_pair[1], grad_normed_two)
    gain_two_part = jnp.sum(grad_normed_two * hat_two, axis=0)
    grad_residual = grad_out + grad_part
    grad_res_low = grad_residual.astype(LOW)
    w_mix_pad = jnp.pad(w_mix_out, ((0, head_pad * HEAD), (0, 0)))
    grad_res_parts = gather_relative(grad_res_low, count)
    grad_res_all = jnp.concatenate(by_rank(grad_res_parts, rank), axis=0)
    w_mix_own = block_of(w_mix_pad, rank, head_width)
    grad_attended = dot_nt(grad_res_all, w_mix_own).astype(LOW)
    grad_attended = grad_attended.reshape(tree_length, heads_dev, HEAD)
    if head_width == rows_weight * wide:
        grad_mix_out = dot_tn(attended_own, grad_res_all).astype(LOW)
        grad_attended, grad_mix_out = lax.optimization_barrier((grad_attended, grad_mix_out))
        sums = grad_mix_out.reshape(wide, rows_weight, width)
        turns = [(w * count + t, t * wide + w) for w in range(wide) for t in range(count)]
    else:
        grad_mix_out = dot_tn(attended_low, grad_res_low).astype(LOW)
        sums = lax.all_to_all(
            grad_mix_out.reshape(wide * count, rows_weight, width),
            ("wide", "tensor"),
            split_axis=0,
            concat_axis=0,
            tiled=True,
        )
        turns = None
    across = ()
    if count == 4:
        across = ex_kept[1].astype(FULL) + ex_sent[1].astype(FULL)
        across, grad_attended = lax.optimization_barrier((across.astype(LOW), grad_attended))
        across = swap(across, "tensor", 2, count)

    grad_query, grad_key, grad_value = attend_backward(
        queries, keys, values, allowed, grad_attended, log_totals
    )
    grad_projected = jnp.stack(
        [rotate(grad_query, cosine, -sine), rotate(grad_key, cosine, -sine), grad_value], axis=1
    )
    grad_projected = grad_projected.astype(LOW).reshape(tree_length, 3 * head_width)
    grad_normed_one = dot_nt(grad_projected, w_qkv).astype(LOW)
    grad_normed_one = sum_relative(
        [block_of(grad_normed_one, rank ^ m, rows_dev) for m in range(count)]
    )
    grad_mix_in = dot_tn(normed_one, grad_projected).astype(LOW)
    grad_mix_in = after(grad_mix_in, returned)
    returned, sh_sums, sh_grads, sums = [
        after(value, grad_projected) for value in (returned, sh_sums, sh_grads, sums)
    ]
    sh_grads = sh_grads[0].astype(FULL)
    if turns:
        grad_mix_out = lax.ppermute(
            sum_wide(sums, wide).astype(LOW), ("wide", "tensor"), turns
        ).astype(FULL)
    else:
        grad_mix_out = jnp.sum(sums.astype(FULL), axis=0)
    if count == 4:
        ex_parts = [ex_kept, ex_sent, after(across, grad_projected)[None]]
    else:
        ex_parts = [part[None] for part in send_relative([ex_kept[m] for m in range(count)])]
    sent = jnp.concatenate([grad_mix_in, gain_two_part.astype(LOW)[:, None]], axis=1)
    got = lax.all_to_all(
        sent.reshape(wide * count, rows_weight, 3 * head_width + 1),
        ("wide", "tensor"),
        split_axis=0,
        concat_axis=0,
        tiled=True,
    )
    got = jnp.sum(got.astype(FULL).reshape(wide, count, rows_weight, -1), axis=0)
    grad_gain_two = jnp.sum(got[:, :, 3 * head_width], axis=0)
    grad_mix_in = got[:, :, : 3 * head_width].reshape(count, rows_weight, 3, head_width)
    grad_mix_in = grad_mix_in.transpose(1, 2, 0, 3).reshape(rows_weight, 3, count * head_width)
    grad_mix_in = grad_mix_in[:, :, :width].reshape(rows_weight, 3 * width)
    grad_gain_one = jnp.sum(mixing_in.astype(LOW).astype(FULL) * grad_mix_in, axis=1)
    grad_gain_one = grad_gain_one / norm_gains[0].astype(LOW).astype(FULL)

    grad_part, _ = rms_back(input_rows, rms_factor(input_rows), gain_pair[0], grad_normed_one)
    input_grad = grad_residual + grad_part

    per_route = [dot_tn(picks[k], returned) for k in range(TOP)]
    mixed = residual + gates[:, :1] * per_route[0] + gates[:, 1:] * per_route[1]
    mixed = mixed + sh_sums[:, width:]
    gate_grad = jnp.stack([jnp.sum(grad_out * rows, axis=-1) for rows in per_route], axis=1)
    logit_grad = gates * (gate_grad - jnp.sum(gates * gate_grad, axis=-1, keepdims=True))

    gradients = (
        (mixing_in, mixing_in_mean, mixing_in_square, grad_mix_in),
        (mixing_out, mixing_out_mean, mixing_out_square, grad_mix_out),
        (
            norm_gains,
            norm_gains_mean,
            norm_gains_square,
            jnp.stack([grad_gain_one, grad_gain_two]),
        ),
        (shared_in, shared_in_mean, shared_in_square, sh_grads[:2].transpose(1, 0, 2)),
        (shared_out, shared_out_mean, shared_out_square, sh_grads[2].T),
    )
    results = [mixed.astype(LOW), input_grad, logit_grad]
    for number, (weight, mean, square, gradient) in enumerate(gradients):
        results.extend(adam_step(weight, mean, square, gradient, RATES[number]))
    results.extend(adam_in(ex_parts, expert_in, expert_in_mean, expert_in_square, RATES[5]))
    results.extend(adam_out(ex_parts, expert_out, expert_out_mean, expert_out_square, RATES[6]))
    return tuple(results)


def solution(mesh):
    placed = (
        P(("wide", "tensor"), None),
        P(("wide", "tensor"), None),
        P("wide", None),
        P("wide", None),
        P("wide", None),
        P(("wide", "tensor"), None),
        P(("wide", "tensor"), None),
        P(("wide", "tensor"), None),
        P(("wide", "tensor"), None),
        P(("wide", "tensor"), None),
        P(("wide", "tensor"), None),
        P(None, ("wide", "tensor")),
        P(None, ("wide", "tensor")),
        P(None, ("wide", "tensor")),
        P("wide", None, "tensor"),
        P("wide", None, "tensor"),
        P("wide", None, "tensor"),
        P("tensor", "wide"),
        P("tensor", "wide"),
        P("tensor", "wide"),
        P("wide", None, None, "tensor"),
        P("wide", None, None, "tensor"),
        P("wide", None, None, "tensor"),
        P("wide", "tensor", None),
        P("wide", "tensor", None),
        P("wide", "tensor", None),
    )
    return jax.shard_map(
        body,
        mesh=mesh,
        in_specs=placed,
        out_specs=(
            P(("wide", "tensor"), None),
            P(("wide", "tensor"), None),
            P(("wide", "tensor"), None),
            P(("wide", "tensor"), None),
            P(("wide", "tensor"), None),
            P(("wide", "tensor"), None),
            P(("wide", "tensor"), None),
            P(("wide", "tensor"), None),
            P(("wide", "tensor"), None),
            P(None, ("wide", "tensor")),
            P(None, ("wide", "tensor")),
            P(None, ("wide", "tensor")),
            P("wide", None, "tensor"),
            P("wide", None, "tensor"),
            P("wide", None, "tensor"),
            P("tensor", "wide"),
            P("tensor", "wide"),
            P("tensor", "wide"),
            P("wide", None, None, "tensor"),
            P("wide", None, None, "tensor"),
            P("wide", None, None, "tensor"),
            P("wide", "tensor", None),
            P("wide", "tensor", None),
            P("wide", "tensor", None),
        ),
        check_vma=False,
    )
```

```python
import functools
import math

import jax
import jax.numpy as jnp
from jax import lax
from jax.experimental import pallas as pl
from jax.experimental.pallas import tpu as pltpu
from jax.sharding import PartitionSpec as P

HEAD = 64
TOP = 2
TRUNK = 256
SEG = 64
STEP = 5
SEGS = 13


NORM_EPS = 1e-06
BETA_ONE = 0.5
BETA_TWO = 0.5
ADAM_EPS = 1e-08
DECAY = 0.01
RATES = (0.02, 0.15, 0.3, 0.02, 0.012, 0.02, 0.012)

LOW = jnp.bfloat16
FULL = jnp.float32
SMALL = pl.CostEstimate(flops=1000, bytes_accessed=1000, transcendentals=0)


def dot(a, b):
    return jnp.dot(a, b, preferred_element_type=FULL)


def dot_nt(a, b):
    return lax.dot_general(a, b, (((1,), (1,)), ((), ())), preferred_element_type=FULL)


def dot_tn(a, b):
    return lax.dot_general(a, b, (((0,), (0,)), ((), ())), preferred_element_type=FULL)


def rms_factor(values):
    return lax.rsqrt(jnp.mean(values * values, axis=-1, keepdims=True) + NORM_EPS)


def rms_back(values, factor, gain, grad):
    hat = values * factor
    scaled = grad * gain
    return factor * (scaled - hat * jnp.mean(scaled * hat, axis=-1, keepdims=True)), hat


def rotary_tables(position):
    half = HEAD // 2
    frequency = 10000.0 ** (-jnp.arange(half, dtype=FULL) / half)
    angles = position[:, None] * frequency[None, :]
    return jnp.cos(angles)[:, None, :], jnp.sin(angles)[:, None, :]


def rotate(values, cosine, sine):
    half = values.shape[-1] // 2
    one, two = values[..., :half], values[..., half:]
    return jnp.concatenate([one * cosine - two * sine, two * cosine + one * sine], axis=-1)


def tree_layout(parent_row, places):
    segment = jnp.where(places < TRUNK, 0, 1 + (places - TRUNK) // SEG)
    seg_start = jnp.where(segment == 0, 0, TRUNK + (segment - 1) * SEG)
    matches = segment[:, None] == jnp.arange(SEGS, dtype=jnp.int32)[None, :]
    upward = jnp.sum(jnp.where(matches, parent_row[None, :], 0), axis=1)
    depth_base = jnp.where(upward == 0, TRUNK, TRUNK + SEG)
    position = jnp.where(segment == 0, places, depth_base + places - seg_start)
    return (segment, upward, position)


def allowed_mask(segment, upward, places):
    same_segment = (segment[None, :] == segment[:, None]) & (places[None, :] <= places[:, None])
    ancestor = (segment[:, None] != 0) & (
        (segment[None, :] == 0) | (segment[None, :] == upward[:, None])
    )
    return same_segment | ancestor


def attend_forward(queries, keys, values, allowed):
    scale = 1.0 / math.sqrt(HEAD)
    scores = jnp.einsum("qhd,khd->hqk", queries, keys, preferred_element_type=FULL) * scale
    scores = jnp.where(allowed[None], scores, -1e30)
    row_top = jnp.max(scores, axis=-1, keepdims=True)
    shifted = jnp.exp(scores - row_top)
    row_total = jnp.sum(shifted, axis=-1, keepdims=True)
    weights = (shifted / row_total).astype(LOW)
    attended = jnp.einsum("hqk,khd->qhd", weights, values, preferred_element_type=FULL)
    return attended, row_top + jnp.log(row_total)


def attend_backward(queries, keys, values, allowed, grad_attended, log_totals):
    scale = 1.0 / math.sqrt(HEAD)
    scores = jnp.einsum("qhd,khd->hqk", queries, keys, preferred_element_type=FULL) * scale
    scores = jnp.where(allowed[None], scores, -1e30)
    probs = jnp.exp(scores - log_totals)
    grad_probs = jnp.einsum("qhd,khd->hqk", grad_attended, values, preferred_element_type=FULL)
    inner = jnp.sum(probs * grad_probs, axis=-1, keepdims=True)
    grad_scores = (probs * (grad_probs - inner)).astype(LOW)
    grad_query = jnp.einsum("hqk,khd->qhd", grad_scores, keys, preferred_element_type=FULL) * scale
    grad_key = jnp.einsum("hqk,qhd->khd", grad_scores, queries, preferred_element_type=FULL) * scale
    grad_value = jnp.einsum(
        "hqk,qhd->khd", probs.astype(LOW), grad_attended, preferred_element_type=FULL
    )
    return grad_query, grad_key, grad_value


def branch_rows_kernel(chunks, x_ref, g_ref, *refs):
    weights = refs[:chunks]
    hidden_ref, ggate_ref, gup_ref, grad_ref, xt_ref, gt_ref = refs[chunks:]
    x, g = x_ref[...], g_ref[...]
    xt_ref[...] = x.T
    gt_ref[...] = g.T
    total = None
    for chunk in range(chunks):
        w = weights[chunk]
        size = w.shape[2]
        at = pl.ds(chunk * size, size)
        gate, up, grad_hidden = dot(x, w[0]), dot(x, w[1]), dot(g, w[2])
        sigmoid = 1.0 / (1.0 + jnp.exp(-gate))
        active = gate * sigmoid
        hidden_ref[:, at] = (active * up).astype(LOW)
        ggate = (grad_hidden * up * sigmoid * (1.0 + gate * (1.0 - sigmoid))).astype(LOW)
        gup = (grad_hidden * active).astype(LOW)
        ggate_ref[:, at] = ggate
        gup_ref[:, at] = gup
        part = dot_nt(ggate, w[0]) + dot_nt(gup, w[1])
        total = part if total is None else total + part
    grad_ref[...] = total.astype(LOW)


def branch_rows(x, g, chunks):
    rows, width = x.shape
    size = chunks[0].shape[2]
    hidden = size * len(chunks)
    block = math.gcd(rows, 256)
    row_spec = pl.BlockSpec((block, width), lambda i: (i, 0))
    hidden_spec = pl.BlockSpec((block, hidden), lambda i: (i, 0))
    whole = [
        pl.BlockSpec(w.shape, lambda i: (0, 0, 0), pipeline_mode=pl.Buffered(1)) for w in chunks
    ]
    hidden_type = jax.ShapeDtypeStruct((rows, hidden), LOW)
    turned_spec = pl.BlockSpec((width, block), lambda i: (0, i))
    turned_type = jax.ShapeDtypeStruct((width, rows), LOW)
    return pl.pallas_call(
        functools.partial(branch_rows_kernel, len(chunks)),
        grid=(rows // block,),
        in_specs=[row_spec, row_spec] + whole,
        out_specs=[hidden_spec] * 3 + [row_spec] + [turned_spec] * 2,
        out_shape=[hidden_type] * 3
        + [jax.ShapeDtypeStruct((rows, width), LOW)]
        + [turned_type] * 2,
        compiler_params=pltpu.CompilerParams(vmem_limit_bytes=48 * 1024 * 1024),
        cost_estimate=SMALL,
        name="branch_rows",
    )(x, g, *chunks)


def branch_out_kernel(chunks, hidden_ref, *refs):
    weights, out_ref = refs[:chunks], refs[chunks]
    total = None
    for chunk in range(chunks):
        w_out = weights[chunk][0]
        size = w_out.shape[1]
        part = dot_nt(hidden_ref[:, pl.ds(chunk * size, size)], w_out)
        total = part if total is None else total + part
    out_ref[...] = total.astype(LOW)


def branch_out(hidden, chunks):
    rows, size = hidden.shape
    width = chunks[0].shape[1]
    block = math.gcd(rows, 256)
    return pl.pallas_call(
        functools.partial(branch_out_kernel, len(chunks)),
        grid=(rows // block,),
        in_specs=[pl.BlockSpec((block, size), lambda i: (i, 0))]
        + [
            pl.BlockSpec(
                (1,) + w.shape[1:], lambda i: (2, 0, 0), pipeline_mode=pl.Buffered(1)
            )
            for w in chunks
        ],
        out_specs=pl.BlockSpec((block, width), lambda i: (i, 0)),
        out_shape=jax.ShapeDtypeStruct((rows, width), LOW),
        compiler_params=pltpu.CompilerParams(vmem_limit_bytes=48 * 1024 * 1024),
        cost_estimate=SMALL,
        name="branch_out",
    )(hidden, *chunks)


def branch_grads_kernel(xt_ref, gt_ref, hidden_ref, ggate_ref, gup_ref, grad_ref):
    xt = xt_ref[...]
    grad_ref[0, 0] = dot(xt, ggate_ref[...]).astype(LOW)
    grad_ref[0, 1] = dot(xt, gup_ref[...]).astype(LOW)
    grad_ref[0, 2] = dot(gt_ref[...], hidden_ref[...]).astype(LOW)


def branch_grads(turned, states, first, chunks, size):
    width, rows = turned[0].shape
    block = math.gcd(width, 256)
    turned_spec = pl.BlockSpec((block, rows), lambda j, i: (i, 0))
    hidden_spec = pl.BlockSpec((rows, size), lambda j, i: (0, first + j))
    return pl.pallas_call(
        branch_grads_kernel,
        grid=(chunks, width // block),
        in_specs=[turned_spec] * 2 + [hidden_spec] * 3,
        out_specs=pl.BlockSpec((1, 3, block, size), lambda j, i: (j, 0, i, 0)),
        out_shape=jax.ShapeDtypeStruct((chunks, 3, width, size), LOW),
        compiler_params=pltpu.CompilerParams(vmem_limit_bytes=48 * 1024 * 1024),
        cost_estimate=SMALL,
        name="branch_grads",
    )(*turned, *states)


def adam_step(weight, mean_old, square_old, gradient, rate):
    mean_new = BETA_ONE * mean_old + (1.0 - BETA_ONE) * gradient
    square_new = BETA_TWO * square_old + (1.0 - BETA_TWO) * gradient * gradient
    mean_hat = mean_new / (1.0 - BETA_ONE**STEP)
    square_hat = square_new / (1.0 - BETA_TWO**STEP)
    updated = weight - rate * (mean_hat / (jnp.sqrt(square_hat) + ADAM_EPS) + DECAY * weight)
    return (mean_new, square_new, updated)


def shared_grads_kernel(xt_ref, gt_ref, hidden_ref, ggate_ref, gup_ref, grad_ref):
    groups, _, rows, _ = grad_ref.shape
    for plane, (turned, state) in enumerate(
        ((xt_ref, ggate_ref), (xt_ref, gup_ref), (gt_ref, hidden_ref))
    ):
        grad = dot(turned[...], state[...])
        for group in range(groups):
            grad_ref[group, plane] = grad[group * rows : (group + 1) * rows].astype(LOW)


def shared_grads(turned, states, wide):
    width, rows = turned[0].shape
    size = states[0].shape[1]
    share = width // wide
    groups = max(g for g in range(1, wide + 1) if wide % g == 0 and g * share <= 384)
    turned_spec = pl.BlockSpec((groups * share, rows), lambda i: (i, 0))
    return pl.pallas_call(
        shared_grads_kernel,
        grid=(wide // groups,),
        in_specs=[turned_spec] * 2 + [pl.BlockSpec((rows, size), lambda i: (0, 0))] * 3,
        out_specs=pl.BlockSpec((groups, 3, share, size), lambda i: (i, 0, 0, 0)),
        out_shape=jax.ShapeDtypeStruct((wide, 3, share, size), LOW),
        compiler_params=pltpu.CompilerParams(vmem_limit_bytes=48 * 1024 * 1024),
        cost_estimate=SMALL,
        name="shared_grads",
    )(*turned, *states)


def sum_of(refs, plane):
    total = refs[0][0, plane].astype(FULL)
    for ref in refs[1:]:
        total = total + ref[0, plane].astype(FULL)
    return total


def adam_in_kernel(count, rate, *refs):
    parts, (w_ref, mean_ref, square_ref), outs = refs[:count], refs[count : count + 3], refs[-4:-1]
    grad_ref = refs[-1]
    _, _, rows, size = parts[0].shape
    tiles = size // 128
    for half in range(2):
        total = sum_of(parts, half)
        for tile in range(tiles):
            at = pl.ds(2 * tile + half, rows, 2 * tiles)
            grad_ref[at, :] = total[:, tile * 128 : (tile + 1) * 128]
    results = adam_step(w_ref[...], mean_ref[...], square_ref[...], grad_ref[...], rate)
    for ref, value in zip(outs, results):
        ref[...] = value


def adam_in(parts, weight, mean, square, rate):
    _, width, _, size = weight.shape
    tiles = size // 128
    block = math.gcd(width, 128)

    def rows_of(value):
        value = value[0].reshape(width, 2, tiles, 128).transpose(0, 2, 1, 3)
        return value.reshape(width * 2 * tiles, 128)

    spec = pl.BlockSpec((block * 2 * tiles, 128), lambda i: (i, 0))
    outs = pl.pallas_call(
        functools.partial(adam_in_kernel, len(parts), rate),
        grid=(width // block,),
        in_specs=[pl.BlockSpec((1, 2, block, size), lambda i: (0, 0, i, 0))] * len(parts) + [spec] * 3,
        out_specs=[spec] * 3,
        out_shape=[jax.ShapeDtypeStruct((width * 2 * tiles, 128), FULL)] * 3,
        scratch_shapes=[pltpu.VMEM((block * 2 * tiles, 128), FULL)],
        compiler_params=pltpu.CompilerParams(vmem_limit_bytes=48 * 1024 * 1024),
        cost_estimate=SMALL,
        name="adam_in",
    )(*parts, rows_of(weight), rows_of(mean), rows_of(square))
    return [
        out.reshape(width, tiles, 2, 128).transpose(0, 2, 1, 3).reshape(weight.shape)
        for out in outs
    ]


def adam_out_kernel(count, rate, *refs):
    parts, (w_ref, mean_ref, square_ref), outs = refs[:count], refs[count : count + 3], refs[-3:]
    total = sum_of(parts, 0).T
    results = adam_step(w_ref[0], mean_ref[0], square_ref[0], total, rate)
    for ref, value in zip(outs, results):
        ref[0] = value


def adam_out(parts, weight, mean, square, rate):
    _, size, width = weight.shape
    block = math.gcd(width, 128)
    spec = pl.BlockSpec((1, size, block), lambda i: (0, 0, i))
    last = [
        pl.BlockSpec((1, 1, block, size), functools.partial(lambda n, i: (0, n, i, 0), p.shape[1] - 1))
        for p in parts
    ]
    return pl.pallas_call(
        functools.partial(adam_out_kernel, len(parts), rate),
        grid=(width // block,),
        in_specs=last + [spec] * 3,
        out_specs=[spec] * 3,
        out_shape=[jax.ShapeDtypeStruct(weight.shape, FULL)] * 3,
        compiler_params=pltpu.CompilerParams(vmem_limit_bytes=48 * 1024 * 1024),
        cost_estimate=SMALL,
        name="adam_out",
    )(*parts, weight, mean, square)


def swap(value, axis, mask, count):
    return lax.ppermute(value, axis, [(i, i ^ mask) for i in range(count)])


def after(value, *earlier):
    return lax.optimization_barrier((value,) + earlier)[0]


def by_rank(parts, rank):
    count = len(parts)
    ordered = []
    for place in range(count):
        chosen = parts[place]
        for other in range(1, count):
            chosen = jnp.where(rank == other, parts[place ^ other], chosen)
        ordered.append(chosen)
    return ordered


def gather_relative(value, count):
    if count != 4:
        rank = lax.axis_index("tensor")
        every = lax.all_gather(value, "tensor", axis=0)
        return [lax.dynamic_index_in_dim(every, rank ^ m, 0, False) for m in range(count)]
    far = swap(value, "tensor", 2, count)
    near = swap(value, "tensor", 1, count)
    return [value, near, far, swap(far, "tensor", 1, count)]


def send_relative(parts):
    count = len(parts)
    return [parts[0]] + [swap(parts[m], "tensor", m, count) for m in range(1, count)]


def sum_relative(parts):
    got = send_relative([p.astype(LOW) for p in parts])
    total = parts[0].astype(FULL)
    for part in got[1:]:
        total = total + part.astype(FULL)
    return total


def masks_of(count):
    return [1 << bit for bit in reversed(range(count.bit_length() - 1))]


def sum_step(value, axis, mask, size, dim, *earlier):
    bit = (lax.axis_index(axis) // mask) % 2
    kept = lax.dynamic_index_in_dim(value, bit, dim, False)
    sent = lax.dynamic_index_in_dim(value, 1 - bit, dim, False).astype(LOW)
    if earlier:
        sent = after(sent, *earlier)
    return kept.astype(FULL), swap(sent, axis, mask, size)


def block_of(value, place, size, dim=0):
    return lax.dynamic_slice_in_dim(value, place * size, size, dim)


def exchange(value):
    return lax.all_to_all(value, "wide", split_axis=0, concat_axis=0, tiled=True)


def body(
    tokens,
    cotangent,
    gate_logits,
    routes,
    parents,
    mixing_in,
    mixing_in_mean,
    mixing_in_square,
    mixing_out,
    mixing_out_mean,
    mixing_out_square,
    norm_gains,
    norm_gains_mean,
    norm_gains_square,
    shared_in,
    shared_in_mean,
    shared_in_square,
    shared_out,
    shared_out_mean,
    shared_out_square,
    expert_in,
    expert_in_mean,
    expert_in_square,
    expert_out,
    expert_out_mean,
    expert_out_square,
):
    rows_dev, width = tokens.shape
    wide = lax.axis_size("wide")
    count = lax.axis_size("tensor")
    rank = lax.axis_index("tensor")
    tree_length = rows_dev * count
    capacity = 2 * rows_dev * TOP // wide
    slots = wide * capacity
    heads = width // HEAD
    heads_dev = -(-heads // count)
    head_pad = heads_dev * count - heads
    head_width = heads_dev * HEAD
    rows_weight = mixing_in.shape[0]

    token_parts = gather_relative(tokens, count)
    tokens_all = jnp.concatenate(by_rank(token_parts, rank), axis=0)
    shared_low = jnp.concatenate(
        [shared_in.astype(LOW).transpose(1, 0, 2), shared_out.astype(LOW).T[None]], axis=0
    )
    w_shared = lax.all_gather(shared_low, "wide", axis=1, tiled=True)
    expert_low = jnp.concatenate(
        [expert_in[0].astype(LOW).transpose(1, 0, 2), expert_out.astype(LOW).transpose(0, 2, 1)],
        axis=0,
    )
    expert_chunks = gather_relative(expert_low, count)
    if count == 4:
        expert_chunks = [expert_chunks[m] for m in (0, 2, 1, 3)]

    cut = mixing_in.astype(LOW).reshape(rows_weight, 3, heads, HEAD)
    cut = jnp.pad(cut, ((0, 0), (0, 0), (0, head_pad), (0, 0)))
    cut = cut.reshape(rows_weight, 3, count, head_width).transpose(2, 0, 1, 3)
    cut = cut.reshape(count, rows_weight, 3 * head_width)
    gain_columns = jnp.broadcast_to(norm_gains.astype(LOW).T[None], (count, rows_weight, 2))
    out_rows = jnp.broadcast_to(mixing_out.astype(LOW)[None], (count, rows_weight, width))
    cut = jnp.concatenate([out_rows, cut, gain_columns], axis=2)
    sent = jnp.broadcast_to(cut[None], (wide,) + cut.shape).reshape(
        wide * count, rows_weight, width + 3 * head_width + 2
    )
    got = lax.all_to_all(sent, ("wide", "tensor"), split_axis=0, concat_axis=0, tiled=True)
    got = got.reshape(width, width + 3 * head_width + 2)
    w_mix_out = got[:, :width]
    w_qkv = got[:, width : width + 3 * head_width]
    gain_pair = got[:, width + 3 * head_width :].astype(FULL).T

    own_routes = lax.dynamic_slice_in_dim(routes, rank * rows_dev, rows_dev, 0)
    own_logits = lax.dynamic_slice_in_dim(gate_logits, rank * rows_dev, rows_dev, 0)
    gates = jax.nn.softmax(own_logits, axis=-1)
    flat = own_routes.reshape(-1)
    named = (flat[:, None] == jnp.arange(wide, dtype=jnp.int32)[None, :]).astype(LOW)
    order = jnp.arange(flat.shape[0], dtype=jnp.int32)
    earlier = (order[None, :] < order[:, None]).astype(LOW)
    before = jnp.sum(dot(earlier, named) * named.astype(FULL), axis=1).astype(jnp.int32)
    places = (flat * capacity + before).reshape(rows_dev, TOP)
    slot_ids = jnp.arange(slots, dtype=jnp.int32)
    picks = [(slot_ids[:, None] == places[:, k][None, :]).astype(LOW) for k in range(TOP)]
    pick_any = picks[0] + picks[1]
    grad_out = cotangent.astype(FULL)
    grad_routes = [(gates[:, k : k + 1] * grad_out).astype(LOW) for k in range(TOP)]
    grad_slots = (dot(picks[0], grad_routes[0]) + dot(picks[1], grad_routes[1])).astype(LOW)
    grad_slots = after(grad_slots, got)
    expert_grads = exchange(grad_slots.reshape(wide, capacity, width)).reshape(slots, width)

    tree_places = jnp.arange(tree_length, dtype=jnp.int32)
    segment, upward, position = tree_layout(parents[0], tree_places)
    allowed = allowed_mask(segment, upward, tree_places)
    cosine, sine = rotary_tables(position.astype(FULL))
    tree_rows = tokens_all.astype(FULL)
    normed_one = (tree_rows * rms_factor(tree_rows) * gain_pair[0]).astype(LOW)
    projected = dot(normed_one, w_qkv).reshape(tree_length, 3, heads_dev, HEAD)
    queries = rotate(projected[:, 0], cosine, sine).astype(LOW)
    keys = rotate(projected[:, 1], cosine, sine).astype(LOW)
    values = projected[:, 2].astype(LOW)
    attended, log_totals = attend_forward(queries, keys, values, allowed)
    attended = attended.astype(LOW).reshape(tree_length, head_width)
    attended_own = attended
    attended = send_relative([block_of(attended, rank ^ m, rows_dev) for m in range(count)])
    attended_low = jnp.concatenate(by_rank(attended, rank), axis=1)[:, :width]
    attended_low = after(attended_low, expert_chunks[1])
    input_rows = tokens.astype(FULL)
    residual = input_rows + dot(attended_low, w_mix_out)
    factor_two = rms_factor(residual)
    normed_two = (residual * factor_two * gain_pair[1]).astype(LOW)

    row_slots = dot(pick_any, normed_two).astype(LOW)
    row_slots = after(row_slots, expert_grads)
    expert_rows = exchange(row_slots.reshape(wide, capacity, width)).reshape(slots, width)
    shared_rows = jnp.concatenate(gather_relative(normed_two, count), axis=0)
    cotangent_late = after(cotangent, expert_chunks[1])
    cotangent_rel = jnp.concatenate(gather_relative(cotangent_late, count), axis=0)
    *sh_states, sh_grad_rows, sh_xt, sh_gt = branch_rows(shared_rows, cotangent_rel, [w_shared])
    sh_part = branch_out(sh_states[0], [w_shared])
    halves = masks_of(wide)
    sh_grads = shared_grads((sh_xt, sh_gt), sh_states, wide)
    sh_grads = sh_grads.reshape((2,) * len(halves) + sh_grads.shape[1:])
    sh_grads = sum(sum_step(sh_grads, "wide", halves[-1], wide, len(halves) - 1))
    sh_grad_rows = sum_relative(jnp.split(sh_grad_rows, count))
    expert_rows, sh_part, sh_grad_rows = lax.optimization_barrier(
        (expert_rows, sh_part, sh_grad_rows)
    )

    *ex_states, ex_grad_rows, ex_xt, ex_gt = branch_rows(expert_rows, expert_grads, expert_chunks)
    back_rows = exchange(ex_grad_rows.reshape(wide, capacity, width)).reshape(slots, width)
    ex_size = ex_states[0].shape[1] // count
    ex_grads = functools.partial(branch_grads, (ex_xt, ex_gt), ex_states)
    if count == 4:
        ex_sent = swap(ex_grads(2, 2, ex_size), "tensor", 1, count)
        ex_kept = ex_grads(0, 2, ex_size)
    else:
        ex_sent, ex_kept = (), ex_grads(0, count, ex_size)
    out_rows = branch_out(ex_states[0], expert_chunks)
    sh_part = sum_relative(jnp.split(after(sh_part, ex_grad_rows), count))
    for level in range(len(halves) - 2, 0, -1):
        sh_grads = sum(sum_step(sh_grads, "wide", halves[level], wide, level, ex_grad_rows))
    back_rows, out_rows, ex_kept, sh_part = lax.optimization_barrier(
        (back_rows, out_rows, ex_kept, sh_part)
    )
    returned = exchange(out_rows.reshape(wide, capacity, width)).reshape(slots, width)

    grad_normed_two = dot_tn(pick_any, back_rows) + sh_grad_rows
    grad_part, hat_two = rms_back(residual, factor_two, gain_pair[1], grad_normed_two)
    gain_two_part = jnp.sum(grad_normed_two * hat_two, axis=0)
    grad_residual = grad_out + grad_part
    grad_res_low = grad_residual.astype(LOW)
    w_mix_pad = jnp.pad(w_mix_out, ((0, head_pad * HEAD), (0, 0)))
    grad_res_parts = gather_relative(grad_res_low, count)
    grad_res_all = jnp.concatenate(by_rank(grad_res_parts, rank), axis=0)
    w_mix_own = block_of(w_mix_pad, rank, head_width)
    grad_attended = dot_nt(grad_res_all, w_mix_own).astype(LOW)
    grad_attended = grad_attended.reshape(tree_length, heads_dev, HEAD)
    if head_width == rows_weight * wide:
        grad_mix_out = dot_tn(attended_own, grad_res_all).astype(LOW)
        grad_attended, grad_mix_out = lax.optimization_barrier((grad_attended, grad_mix_out))
        sums = lax.psum_scatter(grad_mix_out, "wide", scatter_dimension=0, tiled=True)
        turns = [(w * count + t, t * wide + w) for w in range(wide) for t in range(count)]
    else:
        grad_mix_out = dot_tn(attended_low, grad_res_low).astype(LOW)
        sums = lax.all_to_all(
            grad_mix_out.reshape(wide * count, rows_weight, width),
            ("wide", "tensor"),
            split_axis=0,
            concat_axis=0,
            tiled=True,
        )
        turns = None
    sh_kept, sh_got = sum_step(sh_grads, "wide", halves[0], wide, 0, grad_res_all)
    across = ()
    if count == 4:
        across = ex_kept[1].astype(FULL) + ex_sent[1].astype(FULL)
        across = across.astype(LOW)
        across_in, across_out, grad_attended = lax.optimization_barrier(
            (across[:2], across[2:], grad_attended)
        )
        across_in = swap(across_in, "tensor", 2, count)
        across_out = swap(after(across_out, across_in), "tensor", 2, count)
        across = (across_in,)

    grad_query, grad_key, grad_value = attend_backward(
        queries, keys, values, allowed, grad_attended, log_totals
    )
    grad_projected = jnp.stack(
        [rotate(grad_query, cosine, -sine), rotate(grad_key, cosine, -sine), grad_value], axis=1
    )
    grad_projected = grad_projected.astype(LOW).reshape(tree_length, 3 * head_width)
    grad_normed_one = dot_nt(grad_projected, w_qkv).astype(LOW)
    grad_normed_one = sum_relative(
        [block_of(grad_normed_one, rank ^ m, rows_dev) for m in range(count)]
    )
    grad_mix_in = dot_tn(normed_one, grad_projected).astype(LOW)
    grad_mix_in = after(grad_mix_in, returned, *across)
    returned = after(returned, grad_projected)
    if count == 4:
        in_parts = [ex_kept, ex_sent, across_in[None]]
        out_parts = [ex_kept, ex_sent, after(across_out, grad_projected)[None]]
    else:
        in_parts = [part[None] for part in send_relative([ex_kept[m] for m in range(count)])]
        out_parts = in_parts
    sent = jnp.concatenate([grad_mix_in, gain_two_part.astype(LOW)[:, None]], axis=1)
    got = lax.all_to_all(
        sent.reshape(wide * count, rows_weight, 3 * head_width + 1),
        ("wide", "tensor"),
        split_axis=0,
        concat_axis=0,
        tiled=True,
    )
    sh_got, sums = [after(value, got) for value in (sh_got, sums)]
    sh_grads = sh_kept + sh_got
    if turns:
        grad_mix_out = lax.ppermute(sums, ("wide", "tensor"), turns).astype(FULL)
    else:
        grad_mix_out = jnp.sum(sums.astype(FULL), axis=0)
    got = jnp.sum(got.astype(FULL).reshape(wide, count, rows_weight, -1), axis=0)
    grad_gain_two = jnp.sum(got[:, :, 3 * head_width], axis=0)
    grad_mix_in = got[:, :, : 3 * head_width].reshape(count, rows_weight, 3, head_width)
    grad_mix_in = grad_mix_in.transpose(1, 2, 0, 3).reshape(rows_weight, 3, count * head_width)
    grad_mix_in = grad_mix_in[:, :, :width].reshape(rows_weight, 3 * width)
    grad_gain_one = jnp.sum(mixing_in.astype(LOW).astype(FULL) * grad_mix_in, axis=1)
    grad_gain_one = grad_gain_one / norm_gains[0].astype(LOW).astype(FULL)

    grad_part, _ = rms_back(input_rows, rms_factor(input_rows), gain_pair[0], grad_normed_one)
    input_grad = grad_residual + grad_part

    per_route = [dot_tn(picks[k], returned) for k in range(TOP)]
    mixed = residual + gates[:, :1] * per_route[0] + gates[:, 1:] * per_route[1]
    mixed = mixed + sh_part
    gate_grad = jnp.stack([jnp.sum(grad_out * rows, axis=-1) for rows in per_route], axis=1)
    logit_grad = gates * (gate_grad - jnp.sum(gates * gate_grad, axis=-1, keepdims=True))

    gradients = (
        (mixing_in, mixing_in_mean, mixing_in_square, grad_mix_in),
        (mixing_out, mixing_out_mean, mixing_out_square, grad_mix_out),
        (
            norm_gains,
            norm_gains_mean,
            norm_gains_square,
            jnp.stack([grad_gain_one, grad_gain_two]),
        ),
        (shared_in, shared_in_mean, shared_in_square, sh_grads[:2].transpose(1, 0, 2)),
        (shared_out, shared_out_mean, shared_out_square, sh_grads[2].T),
    )
    results = [mixed.astype(LOW), input_grad, logit_grad]
    for number, (weight, mean, square, gradient) in enumerate(gradients):
        results.extend(adam_step(weight, mean, square, gradient, RATES[number]))
    results.extend(adam_in(in_parts, expert_in, expert_in_mean, expert_in_square, RATES[5]))
    results.extend(adam_out(out_parts, expert_out, expert_out_mean, expert_out_square, RATES[6]))
    return tuple(results)


def solution(mesh):
    placed = (
        P(("wide", "tensor"), None),
        P(("wide", "tensor"), None),
        P("wide", None),
        P("wide", None),
        P("wide", None),
        P(("wide", "tensor"), None),
        P(("wide", "tensor"), None),
        P(("wide", "tensor"), None),
        P(("wide", "tensor"), None),
        P(("wide", "tensor"), None),
        P(("wide", "tensor"), None),
        P(None, ("wide", "tensor")),
        P(None, ("wide", "tensor")),
        P(None, ("wide", "tensor")),
        P("wide", None, "tensor"),
        P("wide", None, "tensor"),
        P("wide", None, "tensor"),
        P("tensor", "wide"),
        P("tensor", "wide"),
        P("tensor", "wide"),
        P("wide", None, None, "tensor"),
        P("wide", None, None, "tensor"),
        P("wide", None, None, "tensor"),
        P("wide", "tensor", None),
        P("wide", "tensor", None),
        P("wide", "tensor", None),
    )
    return jax.shard_map(
        body,
        mesh=mesh,
        in_specs=placed,
        out_specs=(
            P(("wide", "tensor"), None),
            P(("wide", "tensor"), None),
            P(("wide", "tensor"), None),
            P(("wide", "tensor"), None),
            P(("wide", "tensor"), None),
            P(("wide", "tensor"), None),
            P(("wide", "tensor"), None),
            P(("wide", "tensor"), None),
            P(("wide", "tensor"), None),
            P(None, ("wide", "tensor")),
            P(None, ("wide", "tensor")),
            P(None, ("wide", "tensor")),
            P("wide", None, "tensor"),
            P("wide", None, "tensor"),
            P("wide", None, "tensor"),
            P("tensor", "wide"),
            P("tensor", "wide"),
            P("tensor", "wide"),
            P("wide", None, None, "tensor"),
            P("wide", None, None, "tensor"),
            P("wide", None, None, "tensor"),
            P("wide", "tensor", None),
            P("wide", "tensor", None),
            P("wide", "tensor", None),
        ),
        check_vma=False,
    )
```

```python
import functools
import math

import jax
import jax.numpy as jnp
from jax import lax
from jax.experimental import pallas as pl
from jax.experimental.pallas import tpu as pltpu
from jax.sharding import PartitionSpec as P

HEAD = 64
TOP = 2
TRUNK = 256
SEG = 64
STEP = 5
SEGS = 13


NORM_EPS = 1e-06
BETA_ONE = 0.5
BETA_TWO = 0.5
ADAM_EPS = 1e-08
DECAY = 0.01
RATES = (0.02, 0.15, 0.3, 0.02, 0.012, 0.02, 0.012)

LOW = jnp.bfloat16
FULL = jnp.float32
SMALL = pl.CostEstimate(flops=1000, bytes_accessed=1000, transcendentals=0)


def dot(a, b):
    return jnp.dot(a, b, preferred_element_type=FULL)


def dot_nt(a, b):
    return lax.dot_general(a, b, (((1,), (1,)), ((), ())), preferred_element_type=FULL)


def dot_tn(a, b):
    return lax.dot_general(a, b, (((0,), (0,)), ((), ())), preferred_element_type=FULL)


def rms_factor(values):
    return lax.rsqrt(jnp.mean(values * values, axis=-1, keepdims=True) + NORM_EPS)


def rms_back(values, factor, gain, grad):
    hat = values * factor
    scaled = grad * gain
    return factor * (scaled - hat * jnp.mean(scaled * hat, axis=-1, keepdims=True)), hat


def rotary_tables(position):
    half = HEAD // 2
    frequency = 10000.0 ** (-jnp.arange(half, dtype=FULL) / half)
    angles = position[:, None] * frequency[None, :]
    return jnp.cos(angles)[:, None, :], jnp.sin(angles)[:, None, :]


def rotate(values, cosine, sine):
    half = values.shape[-1] // 2
    one, two = values[..., :half], values[..., half:]
    return jnp.concatenate([one * cosine - two * sine, two * cosine + one * sine], axis=-1)


def tree_layout(parent_row, places):
    segment = jnp.where(places < TRUNK, 0, 1 + (places - TRUNK) // SEG)
    seg_start = jnp.where(segment == 0, 0, TRUNK + (segment - 1) * SEG)
    matches = segment[:, None] == jnp.arange(SEGS, dtype=jnp.int32)[None, :]
    upward = jnp.sum(jnp.where(matches, parent_row[None, :], 0), axis=1)
    depth_base = jnp.where(upward == 0, TRUNK, TRUNK + SEG)
    position = jnp.where(segment == 0, places, depth_base + places - seg_start)
    return (segment, upward, position)


def allowed_mask(segment, upward, places):
    same_segment = (segment[None, :] == segment[:, None]) & (places[None, :] <= places[:, None])
    ancestor = (segment[:, None] != 0) & (
        (segment[None, :] == 0) | (segment[None, :] == upward[:, None])
    )
    return same_segment | ancestor


def attend_forward(queries, keys, values, allowed):
    scale = 1.0 / math.sqrt(HEAD)
    scores = jnp.einsum("qhd,khd->hqk", queries, keys, preferred_element_type=FULL) * scale
    scores = jnp.where(allowed[None], scores, -1e30)
    row_top = jnp.max(scores, axis=-1, keepdims=True)
    shifted = jnp.exp(scores - row_top)
    row_total = jnp.sum(shifted, axis=-1, keepdims=True)
    weights = (shifted / row_total).astype(LOW)
    attended = jnp.einsum("hqk,khd->qhd", weights, values, preferred_element_type=FULL)
    return attended, row_top + jnp.log(row_total)


def attend_backward(queries, keys, values, allowed, grad_attended, log_totals):
    scale = 1.0 / math.sqrt(HEAD)
    scores = jnp.einsum("qhd,khd->hqk", queries, keys, preferred_element_type=FULL) * scale
    scores = jnp.where(allowed[None], scores, -1e30)
    probs = jnp.exp(scores - log_totals)
    grad_probs = jnp.einsum("qhd,khd->hqk", grad_attended, values, preferred_element_type=FULL)
    inner = jnp.sum(probs * grad_probs, axis=-1, keepdims=True)
    grad_scores = (probs * (grad_probs - inner)).astype(LOW)
    grad_query = jnp.einsum("hqk,khd->qhd", grad_scores, keys, preferred_element_type=FULL) * scale
    grad_key = jnp.einsum("hqk,qhd->khd", grad_scores, queries, preferred_element_type=FULL) * scale
    grad_value = jnp.einsum(
        "hqk,qhd->khd", probs.astype(LOW), grad_attended, preferred_element_type=FULL
    )
    return grad_query, grad_key, grad_value


def branch_rows_kernel(chunks, x_ref, g_ref, *refs):
    weights = refs[:chunks]
    hidden_ref, ggate_ref, gup_ref, grad_ref, xt_ref, gt_ref = refs[chunks:]
    x, g = x_ref[...], g_ref[...]
    xt_ref[...] = x.T
    gt_ref[...] = g.T
    total = None
    for chunk in range(chunks):
        w = weights[chunk]
        size = w.shape[2]
        at = pl.ds(chunk * size, size)
        gate, up, grad_hidden = dot(x, w[0]), dot(x, w[1]), dot(g, w[2])
        sigmoid = 1.0 / (1.0 + jnp.exp(-gate))
        active = gate * sigmoid
        hidden_ref[:, at] = (active * up).astype(LOW)
        ggate = (grad_hidden * up * sigmoid * (1.0 + gate * (1.0 - sigmoid))).astype(LOW)
        gup = (grad_hidden * active).astype(LOW)
        ggate_ref[:, at] = ggate
        gup_ref[:, at] = gup
        part = dot_nt(ggate, w[0]) + dot_nt(gup, w[1])
        total = part if total is None else total + part
    grad_ref[...] = total.astype(LOW)


def branch_rows(x, g, chunks):
    rows, width = x.shape
    size = chunks[0].shape[2]
    hidden = size * len(chunks)
    block = math.gcd(rows, 256)
    row_spec = pl.BlockSpec((block, width), lambda i: (i, 0))
    hidden_spec = pl.BlockSpec((block, hidden), lambda i: (i, 0))
    whole = [
        pl.BlockSpec(w.shape, lambda i: (0, 0, 0), pipeline_mode=pl.Buffered(1)) for w in chunks
    ]
    hidden_type = jax.ShapeDtypeStruct((rows, hidden), LOW)
    turned_spec = pl.BlockSpec((width, block), lambda i: (0, i))
    turned_type = jax.ShapeDtypeStruct((width, rows), LOW)
    return pl.pallas_call(
        functools.partial(branch_rows_kernel, len(chunks)),
        grid=(rows // block,),
        in_specs=[row_spec, row_spec] + whole,
        out_specs=[hidden_spec] * 3 + [row_spec] + [turned_spec] * 2,
        out_shape=[hidden_type] * 3
        + [jax.ShapeDtypeStruct((rows, width), LOW)]
        + [turned_type] * 2,
        compiler_params=pltpu.CompilerParams(vmem_limit_bytes=48 * 1024 * 1024),
        cost_estimate=SMALL,
        name="branch_rows",
    )(x, g, *chunks)


def branch_out_kernel(chunks, hidden_ref, *refs):
    weights, out_ref = refs[:chunks], refs[chunks]
    total = None
    for chunk in range(chunks):
        w_out = weights[chunk][0]
        size = w_out.shape[1]
        part = dot_nt(hidden_ref[:, pl.ds(chunk * size, size)], w_out)
        total = part if total is None else total + part
    out_ref[...] = total.astype(LOW)


def branch_out(hidden, chunks):
    rows, size = hidden.shape
    width = chunks[0].shape[1]
    block = math.gcd(rows, 256)
    return pl.pallas_call(
        functools.partial(branch_out_kernel, len(chunks)),
        grid=(rows // block,),
        in_specs=[pl.BlockSpec((block, size), lambda i: (i, 0))]
        + [
            pl.BlockSpec(
                (1,) + w.shape[1:], lambda i: (2, 0, 0), pipeline_mode=pl.Buffered(1)
            )
            for w in chunks
        ],
        out_specs=pl.BlockSpec((block, width), lambda i: (i, 0)),
        out_shape=jax.ShapeDtypeStruct((rows, width), LOW),
        compiler_params=pltpu.CompilerParams(vmem_limit_bytes=48 * 1024 * 1024),
        cost_estimate=SMALL,
        name="branch_out",
    )(hidden, *chunks)


def branch_grads_kernel(xt_ref, gt_ref, hidden_ref, ggate_ref, gup_ref, grad_ref):
    xt = xt_ref[...]
    grad_ref[0, 0] = dot(xt, ggate_ref[...]).astype(LOW)
    grad_ref[0, 1] = dot(xt, gup_ref[...]).astype(LOW)
    grad_ref[0, 2] = dot(gt_ref[...], hidden_ref[...]).astype(LOW)


def branch_grads(turned, states, first, chunks, size):
    width, rows = turned[0].shape
    block = math.gcd(width, 256)
    turned_spec = pl.BlockSpec((block, rows), lambda j, i: (i, 0))
    hidden_spec = pl.BlockSpec((rows, size), lambda j, i: (0, first + j))
    return pl.pallas_call(
        branch_grads_kernel,
        grid=(chunks, width // block),
        in_specs=[turned_spec] * 2 + [hidden_spec] * 3,
        out_specs=pl.BlockSpec((1, 3, block, size), lambda j, i: (j, 0, i, 0)),
        out_shape=jax.ShapeDtypeStruct((chunks, 3, width, size), LOW),
        compiler_params=pltpu.CompilerParams(vmem_limit_bytes=48 * 1024 * 1024),
        cost_estimate=SMALL,
        name="branch_grads",
    )(*turned, *states)


def adam_step(weight, mean_old, square_old, gradient, rate):
    mean_new = BETA_ONE * mean_old + (1.0 - BETA_ONE) * gradient
    square_new = BETA_TWO * square_old + (1.0 - BETA_TWO) * gradient * gradient
    mean_hat = mean_new / (1.0 - BETA_ONE**STEP)
    square_hat = square_new / (1.0 - BETA_TWO**STEP)
    updated = weight - rate * (mean_hat / (jnp.sqrt(square_hat) + ADAM_EPS) + DECAY * weight)
    return (mean_new, square_new, updated)


def shared_grads_kernel(xt_ref, gt_ref, hidden_ref, ggate_ref, gup_ref, grad_ref):
    groups, _, rows, _ = grad_ref.shape
    for plane, (turned, state) in enumerate(
        ((xt_ref, ggate_ref), (xt_ref, gup_ref), (gt_ref, hidden_ref))
    ):
        grad = dot(turned[...], state[...])
        for group in range(groups):
            grad_ref[group, plane] = grad[group * rows : (group + 1) * rows].astype(LOW)


def shared_grads(turned, states, wide):
    width, rows = turned[0].shape
    size = states[0].shape[1]
    share = width // wide
    groups = max(g for g in range(1, wide + 1) if wide % g == 0 and g * share <= 384)
    turned_spec = pl.BlockSpec((groups * share, rows), lambda i: (i, 0))
    return pl.pallas_call(
        shared_grads_kernel,
        grid=(wide // groups,),
        in_specs=[turned_spec] * 2 + [pl.BlockSpec((rows, size), lambda i: (0, 0))] * 3,
        out_specs=pl.BlockSpec((groups, 3, share, size), lambda i: (i, 0, 0, 0)),
        out_shape=jax.ShapeDtypeStruct((wide, 3, share, size), LOW),
        compiler_params=pltpu.CompilerParams(vmem_limit_bytes=48 * 1024 * 1024),
        cost_estimate=SMALL,
        name="shared_grads",
    )(*turned, *states)


def sum_of(refs, plane):
    total = refs[0][0, plane].astype(FULL)
    for ref in refs[1:]:
        total = total + ref[0, plane].astype(FULL)
    return total


def adam_in_kernel(count, rate, *refs):
    parts, (w_ref, mean_ref, square_ref), outs = refs[:count], refs[count : count + 3], refs[-4:-1]
    grad_ref = refs[-1]
    _, _, rows, size = parts[0].shape
    tiles = size // 128
    for half in range(2):
        total = sum_of(parts, half)
        for tile in range(tiles):
            at = pl.ds(2 * tile + half, rows, 2 * tiles)
            grad_ref[at, :] = total[:, tile * 128 : (tile + 1) * 128]
    results = adam_step(w_ref[...], mean_ref[...], square_ref[...], grad_ref[...], rate)
    for ref, value in zip(outs, results):
        ref[...] = value


def adam_in(parts, weight, mean, square, rate):
    _, width, _, size = weight.shape
    tiles = size // 128
    block = math.gcd(width, 128)

    def rows_of(value):
        value = value[0].reshape(width, 2, tiles, 128).transpose(0, 2, 1, 3)
        return value.reshape(width * 2 * tiles, 128)

    spec = pl.BlockSpec((block * 2 * tiles, 128), lambda i: (i, 0))
    outs = pl.pallas_call(
        functools.partial(adam_in_kernel, len(parts), rate),
        grid=(width // block,),
        in_specs=[pl.BlockSpec((1, 2, block, size), lambda i: (0, 0, i, 0))] * len(parts) + [spec] * 3,
        out_specs=[spec] * 3,
        out_shape=[jax.ShapeDtypeStruct((width * 2 * tiles, 128), FULL)] * 3,
        scratch_shapes=[pltpu.VMEM((block * 2 * tiles, 128), FULL)],
        compiler_params=pltpu.CompilerParams(vmem_limit_bytes=48 * 1024 * 1024),
        cost_estimate=SMALL,
        name="adam_in",
    )(*parts, rows_of(weight), rows_of(mean), rows_of(square))
    return [
        out.reshape(width, tiles, 2, 128).transpose(0, 2, 1, 3).reshape(weight.shape)
        for out in outs
    ]


def adam_out_kernel(count, rate, *refs):
    parts, (w_ref, mean_ref, square_ref), outs = refs[:count], refs[count : count + 3], refs[-3:]
    total = sum_of(parts, 0).T
    results = adam_step(w_ref[0], mean_ref[0], square_ref[0], total, rate)
    for ref, value in zip(outs, results):
        ref[0] = value


def adam_out(parts, weight, mean, square, rate):
    _, size, width = weight.shape
    block = math.gcd(width, 128)
    spec = pl.BlockSpec((1, size, block), lambda i: (0, 0, i))
    last = [
        pl.BlockSpec((1, 1, block, size), functools.partial(lambda n, i: (0, n, i, 0), p.shape[1] - 1))
        for p in parts
    ]
    return pl.pallas_call(
        functools.partial(adam_out_kernel, len(parts), rate),
        grid=(width // block,),
        in_specs=last + [spec] * 3,
        out_specs=[spec] * 3,
        out_shape=[jax.ShapeDtypeStruct(weight.shape, FULL)] * 3,
        compiler_params=pltpu.CompilerParams(vmem_limit_bytes=48 * 1024 * 1024),
        cost_estimate=SMALL,
        name="adam_out",
    )(*parts, weight, mean, square)


def swap(value, axis, mask, count):
    return lax.ppermute(value, axis, [(i, i ^ mask) for i in range(count)])


def after(value, *earlier):
    return lax.optimization_barrier((value,) + earlier)[0]


def by_rank(parts, rank):
    count = len(parts)
    ordered = []
    for place in range(count):
        chosen = parts[place]
        for other in range(1, count):
            chosen = jnp.where(rank == other, parts[place ^ other], chosen)
        ordered.append(chosen)
    return ordered


def gather_relative(value, count):
    if count != 4:
        rank = lax.axis_index("tensor")
        every = lax.all_gather(value, "tensor", axis=0)
        return [lax.dynamic_index_in_dim(every, rank ^ m, 0, False) for m in range(count)]
    far = swap(value, "tensor", 2, count)
    near = swap(value, "tensor", 1, count)
    return [value, near, far, swap(far, "tensor", 1, count)]


def send_relative(parts):
    count = len(parts)
    return [parts[0]] + [swap(parts[m], "tensor", m, count) for m in range(1, count)]


def sum_relative(parts):
    got = send_relative([p.astype(LOW) for p in parts])
    total = parts[0].astype(FULL)
    for part in got[1:]:
        total = total + part.astype(FULL)
    return total


def block_of(value, place, size, dim=0):
    return lax.dynamic_slice_in_dim(value, place * size, size, dim)


def exchange(value):
    return lax.all_to_all(value, "wide", split_axis=0, concat_axis=0, tiled=True)


def body(
    tokens,
    cotangent,
    gate_logits,
    routes,
    parents,
    mixing_in,
    mixing_in_mean,
    mixing_in_square,
    mixing_out,
    mixing_out_mean,
    mixing_out_square,
    norm_gains,
    norm_gains_mean,
    norm_gains_square,
    shared_in,
    shared_in_mean,
    shared_in_square,
    shared_out,
    shared_out_mean,
    shared_out_square,
    expert_in,
    expert_in_mean,
    expert_in_square,
    expert_out,
    expert_out_mean,
    expert_out_square,
):
    rows_dev, width = tokens.shape
    wide = lax.axis_size("wide")
    count = lax.axis_size("tensor")
    rank = lax.axis_index("tensor")
    tree_length = rows_dev * count
    capacity = 2 * rows_dev * TOP // wide
    slots = wide * capacity
    heads = width // HEAD
    heads_dev = -(-heads // count)
    head_pad = heads_dev * count - heads
    head_width = heads_dev * HEAD
    rows_weight = mixing_in.shape[0]

    cut = mixing_in.astype(LOW).reshape(rows_weight, 3, heads, HEAD)
    cut = jnp.pad(cut, ((0, 0), (0, 0), (0, head_pad), (0, 0)))
    cut = cut.reshape(rows_weight, 3, count, head_width).transpose(2, 0, 1, 3)
    cut = cut.reshape(count, rows_weight, 3 * head_width)
    gain_columns = jnp.broadcast_to(norm_gains.astype(LOW).T[None], (count, rows_weight, 2))
    cut = jnp.concatenate([cut, gain_columns], axis=2)
    sent = jnp.broadcast_to(cut[None], (wide,) + cut.shape).reshape(
        wide * count, rows_weight, 3 * head_width + 2
    )
    got = lax.all_to_all(sent, ("wide", "tensor"), split_axis=0, concat_axis=0, tiled=True)
    got = got.reshape(width, 3 * head_width + 2)
    w_qkv = got[:, : 3 * head_width]
    gain_pair = got[:, 3 * head_width :].astype(FULL).T

    token_parts = gather_relative(tokens, count)
    tokens_all = jnp.concatenate(by_rank(token_parts, rank), axis=0)
    expert_low = jnp.concatenate(
        [expert_in[0].astype(LOW).transpose(1, 0, 2), expert_out.astype(LOW).transpose(0, 2, 1)],
        axis=0,
    )
    expert_chunks = gather_relative(expert_low, count)
    if count == 4:
        expert_chunks = [expert_chunks[m] for m in (0, 2, 1, 3)]
    shared_low = jnp.concatenate(
        [shared_in.astype(LOW).transpose(1, 0, 2), shared_out.astype(LOW).T[None]], axis=0
    )
    w_mix_out = lax.all_gather(mixing_out.astype(LOW), ("wide", "tensor"), axis=0, tiled=True)
    shared_low = after(shared_low, w_mix_out)
    w_shared = lax.all_gather(shared_low, "wide", axis=1, tiled=True)

    own_routes = lax.dynamic_slice_in_dim(routes, rank * rows_dev, rows_dev, 0)
    own_logits = lax.dynamic_slice_in_dim(gate_logits, rank * rows_dev, rows_dev, 0)
    gates = jax.nn.softmax(own_logits, axis=-1)
    flat = own_routes.reshape(-1)
    named = (flat[:, None] == jnp.arange(wide, dtype=jnp.int32)[None, :]).astype(LOW)
    order = jnp.arange(flat.shape[0], dtype=jnp.int32)
    earlier = (order[None, :] < order[:, None]).astype(LOW)
    before = jnp.sum(dot(earlier, named) * named.astype(FULL), axis=1).astype(jnp.int32)
    places = (flat * capacity + before).reshape(rows_dev, TOP)
    slot_ids = jnp.arange(slots, dtype=jnp.int32)
    picks = [(slot_ids[:, None] == places[:, k][None, :]).astype(LOW) for k in range(TOP)]
    pick_any = picks[0] + picks[1]
    grad_out = cotangent.astype(FULL)
    grad_routes = [(gates[:, k : k + 1] * grad_out).astype(LOW) for k in range(TOP)]
    grad_slots = (dot(picks[0], grad_routes[0]) + dot(picks[1], grad_routes[1])).astype(LOW)
    grad_slots = after(grad_slots, got)
    expert_grads = exchange(grad_slots.reshape(wide, capacity, width)).reshape(slots, width)

    tree_places = jnp.arange(tree_length, dtype=jnp.int32)
    segment, upward, position = tree_layout(parents[0], tree_places)
    allowed = allowed_mask(segment, upward, tree_places)
    cosine, sine = rotary_tables(position.astype(FULL))
    tree_rows = tokens_all.astype(FULL)
    normed_one = (tree_rows * rms_factor(tree_rows) * gain_pair[0]).astype(LOW)
    projected = dot(normed_one, w_qkv).reshape(tree_length, 3, heads_dev, HEAD)
    queries = rotate(projected[:, 0], cosine, sine).astype(LOW)
    keys = rotate(projected[:, 1], cosine, sine).astype(LOW)
    values = projected[:, 2].astype(LOW)
    attended, log_totals = attend_forward(queries, keys, values, allowed)
    attended = attended.astype(LOW).reshape(tree_length, head_width)
    attended_own = attended
    attended = send_relative([block_of(attended, rank ^ m, rows_dev) for m in range(count)])
    attended_low = jnp.concatenate(by_rank(attended, rank), axis=1)[:, :width]
    attended_low = after(attended_low, expert_chunks[1])
    input_rows = tokens.astype(FULL)
    residual = input_rows + dot(attended_low, w_mix_out)
    factor_two = rms_factor(residual)
    normed_two = (residual * factor_two * gain_pair[1]).astype(LOW)

    row_slots = dot(pick_any, normed_two).astype(LOW)
    row_slots = after(row_slots, expert_grads)
    expert_rows = exchange(row_slots.reshape(wide, capacity, width)).reshape(slots, width)
    shared_rows = jnp.concatenate(gather_relative(normed_two, count), axis=0)
    cotangent_late = after(cotangent, normed_two)
    cotangent_rel = jnp.concatenate(gather_relative(cotangent_late, count), axis=0)
    expert_rows, shared_rows, cotangent_rel = lax.optimization_barrier(
        (expert_rows, shared_rows, cotangent_rel)
    )

    *ex_states, ex_grad_rows, ex_xt, ex_gt = branch_rows(expert_rows, expert_grads, expert_chunks)
    back_rows = exchange(ex_grad_rows.reshape(wide, capacity, width)).reshape(slots, width)
    shared_rows = after(shared_rows, ex_grad_rows)
    *sh_states, sh_grad_rows, sh_xt, sh_gt = branch_rows(shared_rows, cotangent_rel, [w_shared])
    ex_states = list(after(tuple(ex_states), sh_grad_rows))
    sh_grad_rows = sum_relative(jnp.split(sh_grad_rows, count))
    sh_part = branch_out(sh_states[0], [w_shared])
    sh_part = sum_relative(jnp.split(sh_part, count))
    sh_size = sh_states[0].shape[1]
    sh_grads = shared_grads((sh_xt, sh_gt), sh_states, wide)
    rows_shared = width // wide
    ex_size = ex_states[0].shape[1] // count
    ex_grads = functools.partial(branch_grads, (ex_xt, ex_gt), ex_states)
    if count == 4:
        ex_sent = swap(ex_grads(2, 2, ex_size), "tensor", 1, count)
        ex_kept = ex_grads(0, 2, ex_size)
    else:
        ex_sent, ex_kept = (), ex_grads(0, count, ex_size)
    out_rows = branch_out(ex_states[0], expert_chunks)
    back_rows, out_rows, ex_kept, sh_grads, sh_part = lax.optimization_barrier(
        (back_rows, out_rows, ex_kept, sh_grads, sh_part)
    )
    returned = exchange(out_rows.reshape(wide, capacity, width)).reshape(slots, width)

    grad_normed_two = dot_tn(pick_any, back_rows) + sh_grad_rows
    grad_part, hat_two = rms_back(residual, factor_two, gain_pair[1], grad_normed_two)
    gain_two_part = jnp.sum(grad_normed_two * hat_two, axis=0)
    grad_residual = grad_out + grad_part
    grad_res_low = grad_residual.astype(LOW)
    w_mix_pad = jnp.pad(w_mix_out, ((0, head_pad * HEAD), (0, 0)))
    grad_res_parts = gather_relative(grad_res_low, count)
    grad_res_all = jnp.concatenate(by_rank(grad_res_parts, rank), axis=0)
    w_mix_own = block_of(w_mix_pad, rank, head_width)
    grad_attended = dot_nt(grad_res_all, w_mix_own).astype(LOW)
    grad_attended = grad_attended.reshape(tree_length, heads_dev, HEAD)
    if head_width == rows_weight * wide:
        grad_mix_out = dot_tn(attended_own, grad_res_all).astype(LOW)
        lines = rows_weight * width // sh_size
        sums = jnp.concatenate(
            [
                sh_grads.reshape(wide, 3 * rows_shared, sh_size),
                grad_mix_out.reshape(wide, lines, sh_size),
            ],
            axis=1,
        )
        grad_attended, sums = lax.optimization_barrier((grad_attended, sums))
        sums = lax.psum_scatter(sums, "wide", scatter_dimension=0, tiled=True)[0]
        turns = [(w * count + t, t * wide + w) for w in range(wide) for t in range(count)]
    else:
        grad_mix_out = dot_tn(attended_low, grad_res_low).astype(LOW)
        sums = lax.all_to_all(
            grad_mix_out.reshape(wide * count, rows_weight, width),
            ("wide", "tensor"),
            split_axis=0,
            concat_axis=0,
            tiled=True,
        )
        sh_grads = lax.psum_scatter(sh_grads, "wide", scatter_dimension=0, tiled=True)
        turns = None
    across = ()
    if count == 4:
        across = ex_kept[1].astype(FULL) + ex_sent[1].astype(FULL)
        across = across.astype(LOW)
        across_in, across_out, grad_attended = lax.optimization_barrier(
            (across[:2], across[2:], grad_attended)
        )
        across_in = swap(across_in, "tensor", 2, count)
        across_out = swap(after(across_out, across_in), "tensor", 2, count)
        across = (across_in,)

    grad_query, grad_key, grad_value = attend_backward(
        queries, keys, values, allowed, grad_attended, log_totals
    )
    grad_projected = jnp.stack(
        [rotate(grad_query, cosine, -sine), rotate(grad_key, cosine, -sine), grad_value], axis=1
    )
    grad_projected = grad_projected.astype(LOW).reshape(tree_length, 3 * head_width)
    grad_normed_one = dot_nt(grad_projected, w_qkv).astype(LOW)
    row_grads = send_relative(
        [block_of(grad_normed_one, rank ^ m, rows_dev) for m in range(count)]
    )
    grad_mix_in = dot_tn(normed_one, grad_projected).astype(LOW)
    grad_mix_in = after(grad_mix_in, returned, *across)
    if count == 4:
        in_parts = [ex_kept, ex_sent, across_in[None]]
        out_parts = [ex_kept, ex_sent, after(across_out, grad_projected)[None]]
    else:
        in_parts = [part[None] for part in send_relative([ex_kept[m] for m in range(count)])]
        out_parts = in_parts
    returned = after(returned, grad_projected)
    sent = jnp.concatenate([grad_mix_in, gain_two_part.astype(LOW)[:, None]], axis=1)
    got = lax.all_to_all(
        sent.reshape(wide * count, rows_weight, 3 * head_width + 1),
        ("wide", "tensor"),
        split_axis=0,
        concat_axis=0,
        tiled=True,
    )
    row_grads, sums, sh_grads = after((row_grads, sums, sh_grads), got)
    grad_normed_one = sum(part.astype(FULL) for part in row_grads)
    if turns:
        sh_grads = sums[: 3 * rows_shared].reshape(3, rows_shared, sh_size).astype(FULL)
        grad_mix_out = sums[3 * rows_shared :].reshape(rows_weight, width)
        grad_mix_out = lax.ppermute(grad_mix_out, ("wide", "tensor"), turns).astype(FULL)
    else:
        sh_grads = sh_grads[0].astype(FULL)
        grad_mix_out = jnp.sum(sums.astype(FULL), axis=0)
    got = jnp.sum(got.astype(FULL).reshape(wide, count, rows_weight, -1), axis=0)
    grad_gain_two = jnp.sum(got[:, :, 3 * head_width], axis=0)
    grad_mix_in = got[:, :, : 3 * head_width].reshape(count, rows_weight, 3, head_width)
    grad_mix_in = grad_mix_in.transpose(1, 2, 0, 3).reshape(rows_weight, 3, count * head_width)
    grad_mix_in = grad_mix_in[:, :, :width].reshape(rows_weight, 3 * width)
    grad_gain_one = jnp.sum(mixing_in.astype(LOW).astype(FULL) * grad_mix_in, axis=1)
    grad_gain_one = grad_gain_one / norm_gains[0].astype(LOW).astype(FULL)

    grad_part, _ = rms_back(input_rows, rms_factor(input_rows), gain_pair[0], grad_normed_one)
    input_grad = grad_residual + grad_part

    per_route = [dot_tn(picks[k], returned) for k in range(TOP)]
    mixed = residual + gates[:, :1] * per_route[0] + gates[:, 1:] * per_route[1]
    mixed = mixed + sh_part
    gate_grad = jnp.stack([jnp.sum(grad_out * rows, axis=-1) for rows in per_route], axis=1)
    logit_grad = gates * (gate_grad - jnp.sum(gates * gate_grad, axis=-1, keepdims=True))

    gradients = (
        (mixing_in, mixing_in_mean, mixing_in_square, grad_mix_in),
        (mixing_out, mixing_out_mean, mixing_out_square, grad_mix_out),
        (
            norm_gains,
            norm_gains_mean,
            norm_gains_square,
            jnp.stack([grad_gain_one, grad_gain_two]),
        ),
        (shared_in, shared_in_mean, shared_in_square, sh_grads[:2].transpose(1, 0, 2)),
        (shared_out, shared_out_mean, shared_out_square, sh_grads[2].T),
    )
    results = [mixed.astype(LOW), input_grad, logit_grad]
    for number, (weight, mean, square, gradient) in enumerate(gradients):
        results.extend(adam_step(weight, mean, square, gradient, RATES[number]))
    results.extend(adam_in(in_parts, expert_in, expert_in_mean, expert_in_square, RATES[5]))
    results.extend(adam_out(out_parts, expert_out, expert_out_mean, expert_out_square, RATES[6]))
    return tuple(results)


def solution(mesh):
    placed = (
        P(("wide", "tensor"), None),
        P(("wide", "tensor"), None),
        P("wide", None),
        P("wide", None),
        P("wide", None),
        P(("wide", "tensor"), None),
        P(("wide", "tensor"), None),
        P(("wide", "tensor"), None),
        P(("wide", "tensor"), None),
        P(("wide", "tensor"), None),
        P(("wide", "tensor"), None),
        P(None, ("wide", "tensor")),
        P(None, ("wide", "tensor")),
        P(None, ("wide", "tensor")),
        P("wide", None, "tensor"),
        P("wide", None, "tensor"),
        P("wide", None, "tensor"),
        P("tensor", "wide"),
        P("tensor", "wide"),
        P("tensor", "wide"),
        P("wide", None, None, "tensor"),
        P("wide", None, None, "tensor"),
        P("wide", None, None, "tensor"),
        P("wide", "tensor", None),
        P("wide", "tensor", None),
        P("wide", "tensor", None),
    )
    return jax.shard_map(
        body,
        mesh=mesh,
        in_specs=placed,
        out_specs=(
            P(("wide", "tensor"), None),
            P(("wide", "tensor"), None),
            P(("wide", "tensor"), None),
            P(("wide", "tensor"), None),
            P(("wide", "tensor"), None),
            P(("wide", "tensor"), None),
            P(("wide", "tensor"), None),
            P(("wide", "tensor"), None),
            P(("wide", "tensor"), None),
            P(None, ("wide", "tensor")),
            P(None, ("wide", "tensor")),
            P(None, ("wide", "tensor")),
            P("wide", None, "tensor"),
            P("wide", None, "tensor"),
            P("wide", None, "tensor"),
            P("tensor", "wide"),
            P("tensor", "wide"),
            P("tensor", "wide"),
            P("wide", None, None, "tensor"),
            P("wide", None, None, "tensor"),
            P("wide", None, None, "tensor"),
            P("wide", "tensor", None),
            P("wide", "tensor", None),
            P("wide", "tensor", None),
        ),
        check_vma=False,
    )
```

```python
import functools
import math

import jax
import jax.numpy as jnp
from jax import lax
from jax.experimental import pallas as pl
from jax.experimental.pallas import tpu as pltpu
from jax.sharding import PartitionSpec as P

HEAD = 64
TOP = 2
TRUNK = 256
SEG = 64
STEP = 5
SEGS = 13


NORM_EPS = 1e-06
BETA_ONE = 0.5
BETA_TWO = 0.5
ADAM_EPS = 1e-08
DECAY = 0.01
RATES = (0.02, 0.15, 0.3, 0.02, 0.012, 0.02, 0.012)

LOW = jnp.bfloat16
FULL = jnp.float32
SMALL = pl.CostEstimate(flops=1000, bytes_accessed=1000, transcendentals=0)


def dot(a, b):
    return jnp.dot(a, b, preferred_element_type=FULL)


def dot_nt(a, b):
    return lax.dot_general(a, b, (((1,), (1,)), ((), ())), preferred_element_type=FULL)


def dot_tn(a, b):
    return lax.dot_general(a, b, (((0,), (0,)), ((), ())), preferred_element_type=FULL)


def rms_factor(values):
    return lax.rsqrt(jnp.mean(values * values, axis=-1, keepdims=True) + NORM_EPS)


def rms_back(values, factor, gain, grad):
    hat = values * factor
    scaled = grad * gain
    return factor * (scaled - hat * jnp.mean(scaled * hat, axis=-1, keepdims=True)), hat


def rotary_tables(position):
    half = HEAD // 2
    frequency = 10000.0 ** (-jnp.arange(half, dtype=FULL) / half)
    angles = position[:, None] * frequency[None, :]
    return jnp.cos(angles)[:, None, :], jnp.sin(angles)[:, None, :]


def rotate(values, cosine, sine):
    half = values.shape[-1] // 2
    one, two = values[..., :half], values[..., half:]
    return jnp.concatenate([one * cosine - two * sine, two * cosine + one * sine], axis=-1)


def tree_layout(parent_row, places):
    segment = jnp.where(places < TRUNK, 0, 1 + (places - TRUNK) // SEG)
    seg_start = jnp.where(segment == 0, 0, TRUNK + (segment - 1) * SEG)
    matches = segment[:, None] == jnp.arange(SEGS, dtype=jnp.int32)[None, :]
    upward = jnp.sum(jnp.where(matches, parent_row[None, :], 0), axis=1)
    depth_base = jnp.where(upward == 0, TRUNK, TRUNK + SEG)
    position = jnp.where(segment == 0, places, depth_base + places - seg_start)
    return (segment, upward, position)


def allowed_mask(segment, upward, places):
    same_segment = (segment[None, :] == segment[:, None]) & (places[None, :] <= places[:, None])
    ancestor = (segment[:, None] != 0) & (
        (segment[None, :] == 0) | (segment[None, :] == upward[:, None])
    )
    return same_segment | ancestor


def attend_forward(queries, keys, values, allowed):
    scale = 1.0 / math.sqrt(HEAD)
    scores = jnp.einsum("qhd,khd->hqk", queries, keys, preferred_element_type=FULL) * scale
    scores = jnp.where(allowed[None], scores, -1e30)
    row_top = jnp.max(scores, axis=-1, keepdims=True)
    shifted = jnp.exp(scores - row_top)
    row_total = jnp.sum(shifted, axis=-1, keepdims=True)
    weights = (shifted / row_total).astype(LOW)
    attended = jnp.einsum("hqk,khd->qhd", weights, values, preferred_element_type=FULL)
    return attended, row_top + jnp.log(row_total)


def attend_backward(queries, keys, values, allowed, grad_attended, log_totals):
    scale = 1.0 / math.sqrt(HEAD)
    scores = jnp.einsum("qhd,khd->hqk", queries, keys, preferred_element_type=FULL) * scale
    scores = jnp.where(allowed[None], scores, -1e30)
    probs = jnp.exp(scores - log_totals)
    grad_probs = jnp.einsum("qhd,khd->hqk", grad_attended, values, preferred_element_type=FULL)
    inner = jnp.sum(probs * grad_probs, axis=-1, keepdims=True)
    grad_scores = (probs * (grad_probs - inner)).astype(LOW)
    grad_query = jnp.einsum("hqk,khd->qhd", grad_scores, keys, preferred_element_type=FULL) * scale
    grad_key = jnp.einsum("hqk,qhd->khd", grad_scores, queries, preferred_element_type=FULL) * scale
    grad_value = jnp.einsum(
        "hqk,qhd->khd", probs.astype(LOW), grad_attended, preferred_element_type=FULL
    )
    return grad_query, grad_key, grad_value


def branch_rows_kernel(chunks, x_ref, g_ref, *refs):
    weights = refs[:chunks]
    hidden_ref, ggate_ref, gup_ref, grad_ref, xt_ref, gt_ref = refs[chunks:]
    x, g = x_ref[...], g_ref[...]
    xt_ref[...] = x.T
    gt_ref[...] = g.T
    total = None
    for chunk in range(chunks):
        w = weights[chunk]
        size = w.shape[2]
        at = pl.ds(chunk * size, size)
        gate, up, grad_hidden = dot(x, w[0]), dot(x, w[1]), dot(g, w[2])
        sigmoid = 1.0 / (1.0 + jnp.exp(-gate))
        active = gate * sigmoid
        hidden_ref[:, at] = (active * up).astype(LOW)
        ggate = (grad_hidden * up * sigmoid * (1.0 + gate * (1.0 - sigmoid))).astype(LOW)
        gup = (grad_hidden * active).astype(LOW)
        ggate_ref[:, at] = ggate
        gup_ref[:, at] = gup
        part = dot_nt(ggate, w[0]) + dot_nt(gup, w[1])
        total = part if total is None else total + part
    grad_ref[...] = total.astype(LOW)


def branch_rows(x, g, chunks):
    rows, width = x.shape
    size = chunks[0].shape[2]
    hidden = size * len(chunks)
    block = math.gcd(rows, 256)
    row_spec = pl.BlockSpec((block, width), lambda i: (i, 0))
    hidden_spec = pl.BlockSpec((block, hidden), lambda i: (i, 0))
    whole = [
        pl.BlockSpec(w.shape, lambda i: (0, 0, 0), pipeline_mode=pl.Buffered(1)) for w in chunks
    ]
    hidden_type = jax.ShapeDtypeStruct((rows, hidden), LOW)
    turned_spec = pl.BlockSpec((width, block), lambda i: (0, i))
    turned_type = jax.ShapeDtypeStruct((width, rows), LOW)
    return pl.pallas_call(
        functools.partial(branch_rows_kernel, len(chunks)),
        grid=(rows // block,),
        in_specs=[row_spec, row_spec] + whole,
        out_specs=[hidden_spec] * 3 + [row_spec] + [turned_spec] * 2,
        out_shape=[hidden_type] * 3
        + [jax.ShapeDtypeStruct((rows, width), LOW)]
        + [turned_type] * 2,
        compiler_params=pltpu.CompilerParams(vmem_limit_bytes=48 * 1024 * 1024),
        cost_estimate=SMALL,
        name="branch_rows",
    )(x, g, *chunks)


def branch_out_kernel(chunks, hidden_ref, *refs):
    weights, out_ref = refs[:chunks], refs[chunks]
    total = None
    for chunk in range(chunks):
        w_out = weights[chunk][0]
        size = w_out.shape[1]
        part = dot_nt(hidden_ref[:, pl.ds(chunk * size, size)], w_out)
        total = part if total is None else total + part
    out_ref[...] = total.astype(LOW)


def branch_out(hidden, chunks):
    rows, size = hidden.shape
    width = chunks[0].shape[1]
    block = math.gcd(rows, 256)
    return pl.pallas_call(
        functools.partial(branch_out_kernel, len(chunks)),
        grid=(rows // block,),
        in_specs=[pl.BlockSpec((block, size), lambda i: (i, 0))]
        + [
            pl.BlockSpec(
                (1,) + w.shape[1:], lambda i: (2, 0, 0), pipeline_mode=pl.Buffered(1)
            )
            for w in chunks
        ],
        out_specs=pl.BlockSpec((block, width), lambda i: (i, 0)),
        out_shape=jax.ShapeDtypeStruct((rows, width), LOW),
        compiler_params=pltpu.CompilerParams(vmem_limit_bytes=48 * 1024 * 1024),
        cost_estimate=SMALL,
        name="branch_out",
    )(hidden, *chunks)


def branch_grads_kernel(xt_ref, gt_ref, hidden_ref, ggate_ref, gup_ref, grad_ref):
    xt = xt_ref[...]
    grad_ref[0, 0] = dot(xt, ggate_ref[...]).astype(LOW)
    grad_ref[0, 1] = dot(xt, gup_ref[...]).astype(LOW)
    grad_ref[0, 2] = dot(gt_ref[...], hidden_ref[...]).astype(LOW)


def branch_grads(turned, states, first, chunks, size):
    width, rows = turned[0].shape
    block = math.gcd(width, 256)
    turned_spec = pl.BlockSpec((block, rows), lambda j, i: (i, 0))
    hidden_spec = pl.BlockSpec((rows, size), lambda j, i: (0, first + j))
    return pl.pallas_call(
        branch_grads_kernel,
        grid=(chunks, width // block),
        in_specs=[turned_spec] * 2 + [hidden_spec] * 3,
        out_specs=pl.BlockSpec((1, 3, block, size), lambda j, i: (j, 0, i, 0)),
        out_shape=jax.ShapeDtypeStruct((chunks, 3, width, size), LOW),
        compiler_params=pltpu.CompilerParams(vmem_limit_bytes=48 * 1024 * 1024),
        cost_estimate=SMALL,
        name="branch_grads",
    )(*turned, *states)


def adam_step(weight, mean_old, square_old, gradient, rate):
    mean_new = BETA_ONE * mean_old + (1.0 - BETA_ONE) * gradient
    square_new = BETA_TWO * square_old + (1.0 - BETA_TWO) * gradient * gradient
    mean_hat = mean_new / (1.0 - BETA_ONE**STEP)
    square_hat = square_new / (1.0 - BETA_TWO**STEP)
    updated = weight - rate * (mean_hat / (jnp.sqrt(square_hat) + ADAM_EPS) + DECAY * weight)
    return (mean_new, square_new, updated)


def shared_grads_kernel(xt_ref, gt_ref, hidden_ref, ggate_ref, gup_ref, grad_ref):
    groups, _, rows, _ = grad_ref.shape
    for plane, (turned, state) in enumerate(
        ((xt_ref, ggate_ref), (xt_ref, gup_ref), (gt_ref, hidden_ref))
    ):
        grad = dot(turned[...], state[...])
        for group in range(groups):
            grad_ref[group, plane] = grad[group * rows : (group + 1) * rows].astype(LOW)


def shared_grads(turned, states, wide):
    width, rows = turned[0].shape
    size = states[0].shape[1]
    share = width // wide
    groups = max(g for g in range(1, wide + 1) if wide % g == 0 and g * share <= 384)
    turned_spec = pl.BlockSpec((groups * share, rows), lambda i: (i, 0))
    return pl.pallas_call(
        shared_grads_kernel,
        grid=(wide // groups,),
        in_specs=[turned_spec] * 2 + [pl.BlockSpec((rows, size), lambda i: (0, 0))] * 3,
        out_specs=pl.BlockSpec((groups, 3, share, size), lambda i: (i, 0, 0, 0)),
        out_shape=jax.ShapeDtypeStruct((wide, 3, share, size), LOW),
        compiler_params=pltpu.CompilerParams(vmem_limit_bytes=48 * 1024 * 1024),
        cost_estimate=SMALL,
        name="shared_grads",
    )(*turned, *states)


def sum_of(refs, plane):
    total = refs[0][0, plane].astype(FULL)
    for ref in refs[1:]:
        total = total + ref[0, plane].astype(FULL)
    return total


def adam_in_kernel(count, rate, *refs):
    parts, (w_ref, mean_ref, square_ref), outs = refs[:count], refs[count : count + 3], refs[-4:-1]
    grad_ref = refs[-1]
    _, _, rows, size = parts[0].shape
    tiles = size // 128
    for half in range(2):
        total = sum_of(parts, half)
        for tile in range(tiles):
            at = pl.ds(2 * tile + half, rows, 2 * tiles)
            grad_ref[at, :] = total[:, tile * 128 : (tile + 1) * 128]
    results = adam_step(w_ref[...], mean_ref[...], square_ref[...], grad_ref[...], rate)
    for ref, value in zip(outs, results):
        ref[...] = value


def adam_in(parts, weight, mean, square, rate):
    _, width, _, size = weight.shape
    tiles = size // 128
    block = math.gcd(width, 128)

    def rows_of(value):
        value = value[0].reshape(width, 2, tiles, 128).transpose(0, 2, 1, 3)
        return value.reshape(width * 2 * tiles, 128)

    spec = pl.BlockSpec((block * 2 * tiles, 128), lambda i: (i, 0))
    outs = pl.pallas_call(
        functools.partial(adam_in_kernel, len(parts), rate),
        grid=(width // block,),
        in_specs=[pl.BlockSpec((1, 2, block, size), lambda i: (0, 0, i, 0))] * len(parts) + [spec] * 3,
        out_specs=[spec] * 3,
        out_shape=[jax.ShapeDtypeStruct((width * 2 * tiles, 128), FULL)] * 3,
        scratch_shapes=[pltpu.VMEM((block * 2 * tiles, 128), FULL)],
        compiler_params=pltpu.CompilerParams(vmem_limit_bytes=48 * 1024 * 1024),
        cost_estimate=SMALL,
        name="adam_in",
    )(*parts, rows_of(weight), rows_of(mean), rows_of(square))
    return [
        out.reshape(width, tiles, 2, 128).transpose(0, 2, 1, 3).reshape(weight.shape)
        for out in outs
    ]


def adam_out_kernel(count, rate, *refs):
    parts, (w_ref, mean_ref, square_ref), outs = refs[:count], refs[count : count + 3], refs[-3:]
    total = sum_of(parts, 0).T
    results = adam_step(w_ref[0], mean_ref[0], square_ref[0], total, rate)
    for ref, value in zip(outs, results):
        ref[0] = value


def adam_out(parts, weight, mean, square, rate):
    _, size, width = weight.shape
    block = math.gcd(width, 128)
    spec = pl.BlockSpec((1, size, block), lambda i: (0, 0, i))
    last = [
        pl.BlockSpec((1, 1, block, size), functools.partial(lambda n, i: (0, n, i, 0), p.shape[1] - 1))
        for p in parts
    ]
    return pl.pallas_call(
        functools.partial(adam_out_kernel, len(parts), rate),
        grid=(width // block,),
        in_specs=last + [spec] * 3,
        out_specs=[spec] * 3,
        out_shape=[jax.ShapeDtypeStruct(weight.shape, FULL)] * 3,
        compiler_params=pltpu.CompilerParams(vmem_limit_bytes=48 * 1024 * 1024),
        cost_estimate=SMALL,
        name="adam_out",
    )(*parts, weight, mean, square)


def swap(value, axis, mask, count):
    return lax.ppermute(value, axis, [(i, i ^ mask) for i in range(count)])


def after(value, *earlier):
    return lax.optimization_barrier((value,) + earlier)[0]


def by_rank(parts, rank):
    count = len(parts)
    ordered = []
    for place in range(count):
        chosen = parts[place]
        for other in range(1, count):
            chosen = jnp.where(rank == other, parts[place ^ other], chosen)
        ordered.append(chosen)
    return ordered


def gather_relative(value, count):
    if count != 4:
        rank = lax.axis_index("tensor")
        every = lax.all_gather(value, "tensor", axis=0)
        return [lax.dynamic_index_in_dim(every, rank ^ m, 0, False) for m in range(count)]
    far = swap(value, "tensor", 2, count)
    near = swap(value, "tensor", 1, count)
    return [value, near, far, swap(far, "tensor", 1, count)]


def send_relative(parts):
    count = len(parts)
    return [parts[0]] + [swap(parts[m], "tensor", m, count) for m in range(1, count)]


def sum_relative(parts):
    got = send_relative([p.astype(LOW) for p in parts])
    total = parts[0].astype(FULL)
    for part in got[1:]:
        total = total + part.astype(FULL)
    return total


def block_of(value, place, size, dim=0):
    return lax.dynamic_slice_in_dim(value, place * size, size, dim)


def exchange(value):
    return lax.all_to_all(value, "wide", split_axis=0, concat_axis=0, tiled=True)


def body(
    tokens,
    cotangent,
    gate_logits,
    routes,
    parents,
    mixing_in,
    mixing_in_mean,
    mixing_in_square,
    mixing_out,
    mixing_out_mean,
    mixing_out_square,
    norm_gains,
    norm_gains_mean,
    norm_gains_square,
    shared_in,
    shared_in_mean,
    shared_in_square,
    shared_out,
    shared_out_mean,
    shared_out_square,
    expert_in,
    expert_in_mean,
    expert_in_square,
    expert_out,
    expert_out_mean,
    expert_out_square,
):
    rows_dev, width = tokens.shape
    wide = lax.axis_size("wide")
    count = lax.axis_size("tensor")
    rank = lax.axis_index("tensor")
    tree_length = rows_dev * count
    capacity = 2 * rows_dev * TOP // wide
    slots = wide * capacity
    heads = width // HEAD
    heads_dev = -(-heads // count)
    head_pad = heads_dev * count - heads
    head_width = heads_dev * HEAD
    rows_weight = mixing_in.shape[0]

    cut = mixing_in.astype(LOW).reshape(rows_weight, 3, heads, HEAD)
    cut = jnp.pad(cut, ((0, 0), (0, 0), (0, head_pad), (0, 0)))
    cut = cut.reshape(rows_weight, 3, count, head_width).transpose(2, 0, 1, 3)
    cut = cut.reshape(count, rows_weight, 3 * head_width)
    gain_columns = jnp.broadcast_to(norm_gains.astype(LOW).T[None], (count, rows_weight, 2))
    cut = jnp.concatenate([cut, gain_columns], axis=2)
    sent = jnp.broadcast_to(cut[None], (wide,) + cut.shape).reshape(
        wide * count, rows_weight, 3 * head_width + 2
    )
    sent, mix_out_low = lax.optimization_barrier((sent, mixing_out.astype(LOW)))
    got = lax.all_to_all(sent, ("wide", "tensor"), split_axis=0, concat_axis=0, tiled=True)
    got = got.reshape(width, 3 * head_width + 2)
    w_qkv = got[:, : 3 * head_width]
    gain_pair = got[:, 3 * head_width :].astype(FULL).T

    token_parts = gather_relative(tokens, count)
    tokens_all = jnp.concatenate(by_rank(token_parts, rank), axis=0)
    expert_low = jnp.concatenate(
        [expert_in[0].astype(LOW).transpose(1, 0, 2), expert_out.astype(LOW).transpose(0, 2, 1)],
        axis=0,
    )
    expert_chunks = gather_relative(expert_low, count)
    if count == 4:
        expert_chunks = [expert_chunks[m] for m in (0, 2, 1, 3)]
    shared_low = jnp.concatenate(
        [shared_in.astype(LOW).transpose(1, 0, 2), shared_out.astype(LOW).T[None]], axis=0
    )
    w_mix_out = lax.all_gather(mix_out_low, ("wide", "tensor"), axis=0, tiled=True)
    shared_low = after(shared_low, w_mix_out)
    w_shared = lax.all_gather(shared_low, "wide", axis=1, tiled=True)

    own_routes = lax.dynamic_slice_in_dim(routes, rank * rows_dev, rows_dev, 0)
    own_logits = lax.dynamic_slice_in_dim(gate_logits, rank * rows_dev, rows_dev, 0)
    gates = jax.nn.softmax(own_logits, axis=-1)
    flat = own_routes.reshape(-1)
    named = (flat[:, None] == jnp.arange(wide, dtype=jnp.int32)[None, :]).astype(LOW)
    order = jnp.arange(flat.shape[0], dtype=jnp.int32)
    earlier = (order[None, :] < order[:, None]).astype(LOW)
    before = jnp.sum(dot(earlier, named) * named.astype(FULL), axis=1).astype(jnp.int32)
    places = (flat * capacity + before).reshape(rows_dev, TOP)
    slot_ids = jnp.arange(slots, dtype=jnp.int32)
    picks = [(slot_ids[:, None] == places[:, k][None, :]).astype(LOW) for k in range(TOP)]
    pick_any = picks[0] + picks[1]
    grad_out = cotangent.astype(FULL)
    grad_routes = [(gates[:, k : k + 1] * grad_out).astype(LOW) for k in range(TOP)]
    grad_slots = (dot(picks[0], grad_routes[0]) + dot(picks[1], grad_routes[1])).astype(LOW)
    grad_slots = after(grad_slots, got)
    expert_grads = exchange(grad_slots.reshape(wide, capacity, width)).reshape(slots, width)

    tree_places = jnp.arange(tree_length, dtype=jnp.int32)
    segment, upward, position = tree_layout(parents[0], tree_places)
    allowed = allowed_mask(segment, upward, tree_places)
    cosine, sine = rotary_tables(position.astype(FULL))
    tree_rows = tokens_all.astype(FULL)
    normed_one = (tree_rows * rms_factor(tree_rows) * gain_pair[0]).astype(LOW)
    projected = dot(normed_one, w_qkv).reshape(tree_length, 3, heads_dev, HEAD)
    queries = rotate(projected[:, 0], cosine, sine).astype(LOW)
    keys = rotate(projected[:, 1], cosine, sine).astype(LOW)
    values = projected[:, 2].astype(LOW)
    attended, log_totals = attend_forward(queries, keys, values, allowed)
    attended = attended.astype(LOW).reshape(tree_length, head_width)
    attended_own = attended
    attended = send_relative([block_of(attended, rank ^ m, rows_dev) for m in range(count)])
    attended_low = jnp.concatenate(by_rank(attended, rank), axis=1)[:, :width]
    attended_low = after(attended_low, expert_chunks[1])
    input_rows = tokens.astype(FULL)
    residual = input_rows + dot(attended_low, w_mix_out)
    factor_two = rms_factor(residual)
    normed_two = (residual * factor_two * gain_pair[1]).astype(LOW)

    row_slots = dot(pick_any, normed_two).astype(LOW)
    row_slots = after(row_slots, expert_grads)
    expert_rows = exchange(row_slots.reshape(wide, capacity, width)).reshape(slots, width)
    shared_rows = jnp.concatenate(gather_relative(normed_two, count), axis=0)
    cotangent_late = after(cotangent, normed_two)
    cotangent_rel = jnp.concatenate(gather_relative(cotangent_late, count), axis=0)
    expert_rows, shared_rows, cotangent_rel = lax.optimization_barrier(
        (expert_rows, shared_rows, cotangent_rel)
    )

    *ex_states, ex_grad_rows, ex_xt, ex_gt = branch_rows(expert_rows, expert_grads, expert_chunks)
    back_rows = exchange(ex_grad_rows.reshape(wide, capacity, width)).reshape(slots, width)
    shared_rows = after(shared_rows, ex_grad_rows)
    *sh_states, sh_grad_rows, sh_xt, sh_gt = branch_rows(shared_rows, cotangent_rel, [w_shared])
    ex_states = list(after(tuple(ex_states), sh_grad_rows))
    sh_grad_rows = sum_relative(jnp.split(sh_grad_rows, count))
    sh_part = branch_out(sh_states[0], [w_shared])
    sh_part = sum_relative(jnp.split(sh_part, count))
    sh_size = sh_states[0].shape[1]
    sh_grads = shared_grads((sh_xt, sh_gt), sh_states, wide)
    rows_shared = width // wide
    ex_size = ex_states[0].shape[1] // count
    ex_grads = functools.partial(branch_grads, (ex_xt, ex_gt), ex_states)
    if count == 4:
        ex_sent = swap(ex_grads(2, 2, ex_size), "tensor", 1, count)
        ex_kept = ()
    else:
        ex_sent, ex_kept = (), ex_grads(0, count, ex_size)
    out_rows = branch_out(ex_states[0], expert_chunks)
    back_rows, out_rows, ex_kept, sh_grads, sh_part = lax.optimization_barrier(
        (back_rows, out_rows, ex_kept, sh_grads, sh_part)
    )
    returned = exchange(out_rows.reshape(wide, capacity, width)).reshape(slots, width)

    grad_normed_two = dot_tn(pick_any, back_rows) + sh_grad_rows
    grad_part, hat_two = rms_back(residual, factor_two, gain_pair[1], grad_normed_two)
    gain_two_part = jnp.sum(grad_normed_two * hat_two, axis=0)
    grad_residual = grad_out + grad_part
    grad_res_low = grad_residual.astype(LOW)
    if count == 4:
        ex_states = list(after(tuple(ex_states), grad_res_low))
        ex_kept = branch_grads((ex_xt, ex_gt), ex_states, 0, 2, ex_size)
    w_mix_pad = jnp.pad(w_mix_out, ((0, head_pad * HEAD), (0, 0)))
    grad_res_parts = gather_relative(grad_res_low, count)
    grad_res_all = jnp.concatenate(by_rank(grad_res_parts, rank), axis=0)
    w_mix_own = block_of(w_mix_pad, rank, head_width)
    grad_attended = dot_nt(grad_res_all, w_mix_own).astype(LOW)
    grad_attended = grad_attended.reshape(tree_length, heads_dev, HEAD)
    if head_width == rows_weight * wide:
        grad_mix_out = dot_tn(attended_own, grad_res_all).astype(LOW)
        lines = rows_weight * width // sh_size
        sums = jnp.concatenate(
            [
                sh_grads.reshape(wide, 3 * rows_shared, sh_size),
                grad_mix_out.reshape(wide, lines, sh_size),
            ],
            axis=1,
        )
        grad_attended, sums = lax.optimization_barrier((grad_attended, sums))
        sums = lax.psum_scatter(sums, "wide", scatter_dimension=0, tiled=True)[0]
        turns = [(w * count + t, t * wide + w) for w in range(wide) for t in range(count)]
    else:
        grad_mix_out = dot_tn(attended_low, grad_res_low).astype(LOW)
        sums = lax.all_to_all(
            grad_mix_out.reshape(wide * count, rows_weight, width),
            ("wide", "tensor"),
            split_axis=0,
            concat_axis=0,
            tiled=True,
        )
        sh_grads = lax.psum_scatter(sh_grads, "wide", scatter_dimension=0, tiled=True)
        turns = None
    across = ()
    if count == 4:
        across = ex_kept[1].astype(FULL) + ex_sent[1].astype(FULL)
        across = across.astype(LOW)
        across_in, across_out, grad_attended = lax.optimization_barrier(
            (across[:2], across[2:], grad_attended)
        )
        across_in = swap(across_in, "tensor", 2, count)
        across_out = swap(after(across_out, across_in), "tensor", 2, count)
        across = (across_in,)

    grad_query, grad_key, grad_value = attend_backward(
        queries, keys, values, allowed, grad_attended, log_totals
    )
    grad_projected = jnp.stack(
        [rotate(grad_query, cosine, -sine), rotate(grad_key, cosine, -sine), grad_value], axis=1
    )
    grad_projected = grad_projected.astype(LOW).reshape(tree_length, 3 * head_width)
    grad_normed_one = dot_nt(grad_projected, w_qkv).astype(LOW)
    row_grads = send_relative(
        [block_of(grad_normed_one, rank ^ m, rows_dev) for m in range(count)]
    )
    grad_mix_in = dot_tn(normed_one, grad_projected).astype(LOW)
    grad_mix_in = after(grad_mix_in, returned, *across)
    if count == 4:
        in_parts = [ex_kept, ex_sent, across_in[None]]
        out_parts = [ex_kept, ex_sent, after(across_out, grad_projected)[None]]
    else:
        in_parts = [part[None] for part in send_relative([ex_kept[m] for m in range(count)])]
        out_parts = in_parts
    returned = after(returned, grad_projected)
    sent = jnp.concatenate([grad_mix_in, gain_two_part.astype(LOW)[:, None]], axis=1)
    got = lax.all_to_all(
        sent.reshape(wide * count, rows_weight, 3 * head_width + 1),
        ("wide", "tensor"),
        split_axis=0,
        concat_axis=0,
        tiled=True,
    )
    in_results = adam_in(in_parts, expert_in, expert_in_mean, expert_in_square, RATES[5])
    out_results = adam_out(out_parts, expert_out, expert_out_mean, expert_out_square, RATES[6])
    row_grads, in_results = lax.optimization_barrier((row_grads, in_results))
    sums, sh_grads, out_results = lax.optimization_barrier((sums, sh_grads, out_results))
    grad_normed_one = sum(part.astype(FULL) for part in row_grads)
    if turns:
        sh_grads = sums[: 3 * rows_shared].reshape(3, rows_shared, sh_size).astype(FULL)
        grad_mix_out = sums[3 * rows_shared :].reshape(rows_weight, width)
        grad_mix_out = lax.ppermute(grad_mix_out, ("wide", "tensor"), turns).astype(FULL)
    else:
        sh_grads = sh_grads[0].astype(FULL)
        grad_mix_out = jnp.sum(sums.astype(FULL), axis=0)
    got = jnp.sum(got.astype(FULL).reshape(wide, count, rows_weight, -1), axis=0)
    grad_gain_two = jnp.sum(got[:, :, 3 * head_width], axis=0)
    grad_mix_in = got[:, :, : 3 * head_width].reshape(count, rows_weight, 3, head_width)
    grad_mix_in = grad_mix_in.transpose(1, 2, 0, 3).reshape(rows_weight, 3, count * head_width)
    grad_mix_in = grad_mix_in[:, :, :width].reshape(rows_weight, 3 * width)
    grad_gain_one = jnp.sum(mixing_in.astype(LOW).astype(FULL) * grad_mix_in, axis=1)
    grad_gain_one = grad_gain_one / norm_gains[0].astype(LOW).astype(FULL)

    grad_part, _ = rms_back(input_rows, rms_factor(input_rows), gain_pair[0], grad_normed_one)
    input_grad = grad_residual + grad_part

    per_route = [dot_tn(picks[k], returned) for k in range(TOP)]
    mixed = residual + gates[:, :1] * per_route[0] + gates[:, 1:] * per_route[1]
    mixed = mixed + sh_part
    gate_grad = jnp.stack([jnp.sum(grad_out * rows, axis=-1) for rows in per_route], axis=1)
    logit_grad = gates * (gate_grad - jnp.sum(gates * gate_grad, axis=-1, keepdims=True))

    gradients = (
        (mixing_in, mixing_in_mean, mixing_in_square, grad_mix_in),
        (mixing_out, mixing_out_mean, mixing_out_square, grad_mix_out),
        (
            norm_gains,
            norm_gains_mean,
            norm_gains_square,
            jnp.stack([grad_gain_one, grad_gain_two]),
        ),
        (shared_in, shared_in_mean, shared_in_square, sh_grads[:2].transpose(1, 0, 2)),
        (shared_out, shared_out_mean, shared_out_square, sh_grads[2].T),
    )
    results = [mixed.astype(LOW), input_grad, logit_grad]
    for number, (weight, mean, square, gradient) in enumerate(gradients):
        results.extend(adam_step(weight, mean, square, gradient, RATES[number]))
    results.extend(in_results)
    results.extend(out_results)
    return tuple(results)


def solution(mesh):
    placed = (
        P(("wide", "tensor"), None),
        P(("wide", "tensor"), None),
        P("wide", None),
        P("wide", None),
        P("wide", None),
        P(("wide", "tensor"), None),
        P(("wide", "tensor"), None),
        P(("wide", "tensor"), None),
        P(("wide", "tensor"), None),
        P(("wide", "tensor"), None),
        P(("wide", "tensor"), None),
        P(None, ("wide", "tensor")),
        P(None, ("wide", "tensor")),
        P(None, ("wide", "tensor")),
        P("wide", None, "tensor"),
        P("wide", None, "tensor"),
        P("wide", None, "tensor"),
        P("tensor", "wide"),
        P("tensor", "wide"),
        P("tensor", "wide"),
        P("wide", None, None, "tensor"),
        P("wide", None, None, "tensor"),
        P("wide", None, None, "tensor"),
        P("wide", "tensor", None),
        P("wide", "tensor", None),
        P("wide", "tensor", None),
    )
    return jax.shard_map(
        body,
        mesh=mesh,
        in_specs=placed,
        out_specs=(
            P(("wide", "tensor"), None),
            P(("wide", "tensor"), None),
            P(("wide", "tensor"), None),
            P(("wide", "tensor"), None),
            P(("wide", "tensor"), None),
            P(("wide", "tensor"), None),
            P(("wide", "tensor"), None),
            P(("wide", "tensor"), None),
            P(("wide", "tensor"), None),
            P(None, ("wide", "tensor")),
            P(None, ("wide", "tensor")),
            P(None, ("wide", "tensor")),
            P("wide", None, "tensor"),
            P("wide", None, "tensor"),
            P("wide", None, "tensor"),
            P("tensor", "wide"),
            P("tensor", "wide"),
            P("tensor", "wide"),
            P("wide", None, None, "tensor"),
            P("wide", None, None, "tensor"),
            P("wide", None, None, "tensor"),
            P("wide", "tensor", None),
            P("wide", "tensor", None),
            P("wide", "tensor", None),
        ),
        check_vma=False,
    )
```

```python
import functools
import math

import jax
import jax.numpy as jnp
from jax import lax
from jax.experimental import pallas as pl
from jax.experimental.pallas import tpu as pltpu
from jax.sharding import PartitionSpec as P

HEAD = 64
TOP = 2
TRUNK = 256
SEG = 64
STEP = 5
SEGS = 13


NORM_EPS = 1e-06
BETA_ONE = 0.5
BETA_TWO = 0.5
ADAM_EPS = 1e-08
DECAY = 0.01
RATES = (0.02, 0.15, 0.3, 0.02, 0.012, 0.02, 0.012)

LOW = jnp.bfloat16
FULL = jnp.float32
SMALL = pl.CostEstimate(flops=1000, bytes_accessed=1000, transcendentals=0)


def dot(a, b):
    return jnp.dot(a, b, preferred_element_type=FULL)


def dot_nt(a, b):
    return lax.dot_general(a, b, (((1,), (1,)), ((), ())), preferred_element_type=FULL)


def dot_tn(a, b):
    return lax.dot_general(a, b, (((0,), (0,)), ((), ())), preferred_element_type=FULL)


def rms_factor(values):
    return lax.rsqrt(jnp.mean(values * values, axis=-1, keepdims=True) + NORM_EPS)


def rms_back(values, factor, gain, grad):
    hat = values * factor
    scaled = grad * gain
    return factor * (scaled - hat * jnp.mean(scaled * hat, axis=-1, keepdims=True)), hat


def rotary_tables(position):
    half = HEAD // 2
    frequency = 10000.0 ** (-jnp.arange(half, dtype=FULL) / half)
    angles = position[:, None] * frequency[None, :]
    return jnp.cos(angles)[:, None, :], jnp.sin(angles)[:, None, :]


def rotate(values, cosine, sine):
    half = values.shape[-1] // 2
    one, two = values[..., :half], values[..., half:]
    return jnp.concatenate([one * cosine - two * sine, two * cosine + one * sine], axis=-1)


def tree_layout(parent_row, places):
    segment = jnp.where(places < TRUNK, 0, 1 + (places - TRUNK) // SEG)
    seg_start = jnp.where(segment == 0, 0, TRUNK + (segment - 1) * SEG)
    matches = segment[:, None] == jnp.arange(SEGS, dtype=jnp.int32)[None, :]
    upward = jnp.sum(jnp.where(matches, parent_row[None, :], 0), axis=1)
    depth_base = jnp.where(upward == 0, TRUNK, TRUNK + SEG)
    position = jnp.where(segment == 0, places, depth_base + places - seg_start)
    return (segment, upward, position)


def allowed_mask(segment, upward, places):
    same_segment = (segment[None, :] == segment[:, None]) & (places[None, :] <= places[:, None])
    ancestor = (segment[:, None] != 0) & (
        (segment[None, :] == 0) | (segment[None, :] == upward[:, None])
    )
    return same_segment | ancestor


def attend_forward(queries, keys, values, allowed):
    scale = 1.0 / math.sqrt(HEAD)
    scores = jnp.einsum("qhd,khd->hqk", queries, keys, preferred_element_type=FULL) * scale
    scores = jnp.where(allowed[None], scores, -1e30)
    row_top = jnp.max(scores, axis=-1, keepdims=True)
    shifted = jnp.exp(scores - row_top)
    row_total = jnp.sum(shifted, axis=-1, keepdims=True)
    weights = (shifted / row_total).astype(LOW)
    attended = jnp.einsum("hqk,khd->qhd", weights, values, preferred_element_type=FULL)
    return attended, row_top + jnp.log(row_total)


def attend_backward(queries, keys, values, allowed, grad_attended, log_totals):
    scale = 1.0 / math.sqrt(HEAD)
    scores = jnp.einsum("qhd,khd->hqk", queries, keys, preferred_element_type=FULL) * scale
    scores = jnp.where(allowed[None], scores, -1e30)
    probs = jnp.exp(scores - log_totals)
    grad_probs = jnp.einsum("qhd,khd->hqk", grad_attended, values, preferred_element_type=FULL)
    inner = jnp.sum(probs * grad_probs, axis=-1, keepdims=True)
    grad_scores = (probs * (grad_probs - inner)).astype(LOW)
    grad_query = jnp.einsum("hqk,khd->qhd", grad_scores, keys, preferred_element_type=FULL) * scale
    grad_key = jnp.einsum("hqk,qhd->khd", grad_scores, queries, preferred_element_type=FULL) * scale
    grad_value = jnp.einsum(
        "hqk,qhd->khd", probs.astype(LOW), grad_attended, preferred_element_type=FULL
    )
    return grad_query, grad_key, grad_value


def branch_rows_kernel(chunks, x_ref, g_ref, *refs):
    weights = refs[:chunks]
    hidden_ref, ggate_ref, gup_ref, grad_ref, xt_ref, gt_ref = refs[chunks:]
    x, g = x_ref[...], g_ref[...]
    xt_ref[...] = x.T
    gt_ref[...] = g.T
    total = None
    for chunk in range(chunks):
        w = weights[chunk]
        size = w.shape[2]
        at = pl.ds(chunk * size, size)
        gate, up, grad_hidden = dot(x, w[0]), dot(x, w[1]), dot(g, w[2])
        sigmoid = 1.0 / (1.0 + jnp.exp(-gate))
        active = gate * sigmoid
        hidden_ref[:, at] = (active * up).astype(LOW)
        ggate = (grad_hidden * up * sigmoid * (1.0 + gate * (1.0 - sigmoid))).astype(LOW)
        gup = (grad_hidden * active).astype(LOW)
        ggate_ref[:, at] = ggate
        gup_ref[:, at] = gup
        part = dot_nt(ggate, w[0]) + dot_nt(gup, w[1])
        total = part if total is None else total + part
    grad_ref[...] = total.astype(LOW)


def branch_rows(x, g, chunks):
    rows, width = x.shape
    size = chunks[0].shape[2]
    hidden = size * len(chunks)
    block = math.gcd(rows, 256)
    row_spec = pl.BlockSpec((block, width), lambda i: (i, 0))
    hidden_spec = pl.BlockSpec((block, hidden), lambda i: (i, 0))
    whole = [
        pl.BlockSpec(w.shape, lambda i: (0, 0, 0), pipeline_mode=pl.Buffered(1)) for w in chunks
    ]
    hidden_type = jax.ShapeDtypeStruct((rows, hidden), LOW)
    turned_spec = pl.BlockSpec((width, block), lambda i: (0, i))
    turned_type = jax.ShapeDtypeStruct((width, rows), LOW)
    return pl.pallas_call(
        functools.partial(branch_rows_kernel, len(chunks)),
        grid=(rows // block,),
        in_specs=[row_spec, row_spec] + whole,
        out_specs=[hidden_spec] * 3 + [row_spec] + [turned_spec] * 2,
        out_shape=[hidden_type] * 3
        + [jax.ShapeDtypeStruct((rows, width), LOW)]
        + [turned_type] * 2,
        compiler_params=pltpu.CompilerParams(vmem_limit_bytes=48 * 1024 * 1024),
        cost_estimate=SMALL,
        name="branch_rows",
    )(x, g, *chunks)


def branch_out_kernel(chunks, hidden_ref, *refs):
    weights, out_ref = refs[:chunks], refs[chunks]
    total = None
    for chunk in range(chunks):
        w_out = weights[chunk][0]
        size = w_out.shape[1]
        part = dot_nt(hidden_ref[:, pl.ds(chunk * size, size)], w_out)
        total = part if total is None else total + part
    out_ref[...] = total.astype(LOW)


def branch_out(hidden, chunks):
    rows, size = hidden.shape
    width = chunks[0].shape[1]
    block = math.gcd(rows, 256)
    return pl.pallas_call(
        functools.partial(branch_out_kernel, len(chunks)),
        grid=(rows // block,),
        in_specs=[pl.BlockSpec((block, size), lambda i: (i, 0))]
        + [
            pl.BlockSpec(
                (1,) + w.shape[1:], lambda i: (2, 0, 0), pipeline_mode=pl.Buffered(1)
            )
            for w in chunks
        ],
        out_specs=pl.BlockSpec((block, width), lambda i: (i, 0)),
        out_shape=jax.ShapeDtypeStruct((rows, width), LOW),
        compiler_params=pltpu.CompilerParams(vmem_limit_bytes=48 * 1024 * 1024),
        cost_estimate=SMALL,
        name="branch_out",
    )(hidden, *chunks)


def branch_grads_kernel(xt_ref, gt_ref, hidden_ref, ggate_ref, gup_ref, grad_ref):
    xt = xt_ref[...]
    grad_ref[0, 0] = dot(xt, ggate_ref[...]).astype(LOW)
    grad_ref[0, 1] = dot(xt, gup_ref[...]).astype(LOW)
    grad_ref[0, 2] = dot(gt_ref[...], hidden_ref[...]).astype(LOW)


def branch_grads(turned, states, first, chunks, size):
    width, rows = turned[0].shape
    block = math.gcd(width, 256)
    turned_spec = pl.BlockSpec((block, rows), lambda j, i: (i, 0))
    hidden_spec = pl.BlockSpec((rows, size), lambda j, i: (0, first + j))
    return pl.pallas_call(
        branch_grads_kernel,
        grid=(chunks, width // block),
        in_specs=[turned_spec] * 2 + [hidden_spec] * 3,
        out_specs=pl.BlockSpec((1, 3, block, size), lambda j, i: (j, 0, i, 0)),
        out_shape=jax.ShapeDtypeStruct((chunks, 3, width, size), LOW),
        compiler_params=pltpu.CompilerParams(vmem_limit_bytes=48 * 1024 * 1024),
        cost_estimate=SMALL,
        name="branch_grads",
    )(*turned, *states)


def adam_step(weight, mean_old, square_old, gradient, rate):
    mean_new = BETA_ONE * mean_old + (1.0 - BETA_ONE) * gradient
    square_new = BETA_TWO * square_old + (1.0 - BETA_TWO) * gradient * gradient
    mean_hat = mean_new / (1.0 - BETA_ONE**STEP)
    square_hat = square_new / (1.0 - BETA_TWO**STEP)
    updated = weight - rate * (mean_hat / (jnp.sqrt(square_hat) + ADAM_EPS) + DECAY * weight)
    return (mean_new, square_new, updated)


def shared_grads_kernel(xt_ref, gt_ref, hidden_ref, ggate_ref, gup_ref, grad_ref):
    groups, _, rows, _ = grad_ref.shape
    for plane, (turned, state) in enumerate(
        ((xt_ref, ggate_ref), (xt_ref, gup_ref), (gt_ref, hidden_ref))
    ):
        grad = dot(turned[...], state[...])
        for group in range(groups):
            grad_ref[group, plane] = grad[group * rows : (group + 1) * rows].astype(LOW)


def shared_grads(turned, states, wide):
    width, rows = turned[0].shape
    size = states[0].shape[1]
    share = width // wide
    groups = max(g for g in range(1, wide + 1) if wide % g == 0 and g * share <= 384)
    turned_spec = pl.BlockSpec((groups * share, rows), lambda i: (i, 0))
    return pl.pallas_call(
        shared_grads_kernel,
        grid=(wide // groups,),
        in_specs=[turned_spec] * 2 + [pl.BlockSpec((rows, size), lambda i: (0, 0))] * 3,
        out_specs=pl.BlockSpec((groups, 3, share, size), lambda i: (i, 0, 0, 0)),
        out_shape=jax.ShapeDtypeStruct((wide, 3, share, size), LOW),
        compiler_params=pltpu.CompilerParams(vmem_limit_bytes=48 * 1024 * 1024),
        cost_estimate=SMALL,
        name="shared_grads",
    )(*turned, *states)


def sum_of(refs, plane):
    total = refs[0][0, plane].astype(FULL)
    for ref in refs[1:]:
        total = total + ref[0, plane].astype(FULL)
    return total


def adam_in_kernel(count, rate, *refs):
    parts, (w_ref, mean_ref, square_ref), outs = refs[:count], refs[count : count + 3], refs[-4:-1]
    grad_ref = refs[-1]
    _, _, rows, size = parts[0].shape
    tiles = size // 128
    for half in range(2):
        total = sum_of(parts, half)
        for tile in range(tiles):
            at = pl.ds(2 * tile + half, rows, 2 * tiles)
            grad_ref[at, :] = total[:, tile * 128 : (tile + 1) * 128]
    results = adam_step(w_ref[...], mean_ref[...], square_ref[...], grad_ref[...], rate)
    for ref, value in zip(outs, results):
        ref[...] = value


def adam_in(parts, weight, mean, square, rate):
    _, width, _, size = weight.shape
    tiles = size // 128
    block = math.gcd(width, 128)

    def rows_of(value):
        value = value[0].reshape(width, 2, tiles, 128).transpose(0, 2, 1, 3)
        return value.reshape(width * 2 * tiles, 128)

    spec = pl.BlockSpec((block * 2 * tiles, 128), lambda i: (i, 0))
    outs = pl.pallas_call(
        functools.partial(adam_in_kernel, len(parts), rate),
        grid=(width // block,),
        in_specs=[pl.BlockSpec((1, 2, block, size), lambda i: (0, 0, i, 0))] * len(parts) + [spec] * 3,
        out_specs=[spec] * 3,
        out_shape=[jax.ShapeDtypeStruct((width * 2 * tiles, 128), FULL)] * 3,
        scratch_shapes=[pltpu.VMEM((block * 2 * tiles, 128), FULL)],
        compiler_params=pltpu.CompilerParams(vmem_limit_bytes=48 * 1024 * 1024),
        cost_estimate=SMALL,
        name="adam_in",
    )(*parts, rows_of(weight), rows_of(mean), rows_of(square))
    return [
        out.reshape(width, tiles, 2, 128).transpose(0, 2, 1, 3).reshape(weight.shape)
        for out in outs
    ]


def adam_out_kernel(count, rate, *refs):
    parts, (w_ref, mean_ref, square_ref), outs = refs[:count], refs[count : count + 3], refs[-3:]
    total = sum_of(parts, 0).T
    results = adam_step(w_ref[0], mean_ref[0], square_ref[0], total, rate)
    for ref, value in zip(outs, results):
        ref[0] = value


def adam_out(parts, weight, mean, square, rate):
    _, size, width = weight.shape
    block = math.gcd(width, 128)
    spec = pl.BlockSpec((1, size, block), lambda i: (0, 0, i))
    last = [
        pl.BlockSpec((1, 1, block, size), functools.partial(lambda n, i: (0, n, i, 0), p.shape[1] - 1))
        for p in parts
    ]
    return pl.pallas_call(
        functools.partial(adam_out_kernel, len(parts), rate),
        grid=(width // block,),
        in_specs=last + [spec] * 3,
        out_specs=[spec] * 3,
        out_shape=[jax.ShapeDtypeStruct(weight.shape, FULL)] * 3,
        compiler_params=pltpu.CompilerParams(vmem_limit_bytes=48 * 1024 * 1024),
        cost_estimate=SMALL,
        name="adam_out",
    )(*parts, weight, mean, square)


def swap(value, axis, mask, count):
    return lax.ppermute(value, axis, [(i, i ^ mask) for i in range(count)])


def after(value, *earlier):
    return lax.optimization_barrier((value,) + earlier)[0]


def by_rank(parts, rank):
    count = len(parts)
    ordered = []
    for place in range(count):
        chosen = parts[place]
        for other in range(1, count):
            chosen = jnp.where(rank == other, parts[place ^ other], chosen)
        ordered.append(chosen)
    return ordered


def gather_relative(value, count):
    if count != 4:
        rank = lax.axis_index("tensor")
        every = lax.all_gather(value, "tensor", axis=0)
        return [lax.dynamic_index_in_dim(every, rank ^ m, 0, False) for m in range(count)]
    far = swap(value, "tensor", 2, count)
    near = swap(value, "tensor", 1, count)
    return [value, near, far, swap(far, "tensor", 1, count)]


def send_relative(parts):
    count = len(parts)
    return [parts[0]] + [swap(parts[m], "tensor", m, count) for m in range(1, count)]


def sum_relative(parts):
    got = send_relative([p.astype(LOW) for p in parts])
    total = parts[0].astype(FULL)
    for part in got[1:]:
        total = total + part.astype(FULL)
    return total


def block_of(value, place, size, dim=0):
    return lax.dynamic_slice_in_dim(value, place * size, size, dim)


def exchange(value):
    return lax.all_to_all(value, "wide", split_axis=0, concat_axis=0, tiled=True)


def body(
    tokens,
    cotangent,
    gate_logits,
    routes,
    parents,
    mixing_in,
    mixing_in_mean,
    mixing_in_square,
    mixing_out,
    mixing_out_mean,
    mixing_out_square,
    norm_gains,
    norm_gains_mean,
    norm_gains_square,
    shared_in,
    shared_in_mean,
    shared_in_square,
    shared_out,
    shared_out_mean,
    shared_out_square,
    expert_in,
    expert_in_mean,
    expert_in_square,
    expert_out,
    expert_out_mean,
    expert_out_square,
):
    rows_dev, width = tokens.shape
    wide = lax.axis_size("wide")
    count = lax.axis_size("tensor")
    rank = lax.axis_index("tensor")
    tree_length = rows_dev * count
    capacity = 2 * rows_dev * TOP // wide
    slots = wide * capacity
    heads = width // HEAD
    heads_dev = -(-heads // count)
    head_pad = heads_dev * count - heads
    head_width = heads_dev * HEAD
    rows_weight = mixing_in.shape[0]

    cut = mixing_in.astype(LOW).reshape(rows_weight, 3, heads, HEAD)
    cut = jnp.pad(cut, ((0, 0), (0, 0), (0, head_pad), (0, 0)))
    cut = cut.reshape(rows_weight, 3, count, head_width).transpose(2, 0, 1, 3)
    cut = cut.reshape(count, rows_weight, 3 * head_width)
    gain_columns = jnp.broadcast_to(norm_gains.astype(LOW).T[None], (count, rows_weight, 2))
    cut = jnp.concatenate([cut, gain_columns], axis=2)
    sent = jnp.broadcast_to(cut[None], (wide,) + cut.shape).reshape(
        wide * count, rows_weight, 3 * head_width + 2
    )
    sent, mix_out_low = lax.optimization_barrier((sent, mixing_out.astype(LOW)))
    got = lax.all_to_all(sent, ("wide", "tensor"), split_axis=0, concat_axis=0, tiled=True)
    got = got.reshape(width, 3 * head_width + 2)
    w_qkv = got[:, : 3 * head_width]
    gain_pair = got[:, 3 * head_width :].astype(FULL).T

    token_parts = gather_relative(tokens, count)
    tokens_all = jnp.concatenate(by_rank(token_parts, rank), axis=0)
    expert_low = jnp.concatenate(
        [expert_in[0].astype(LOW).transpose(1, 0, 2), expert_out.astype(LOW).transpose(0, 2, 1)],
        axis=0,
    )
    expert_chunks = gather_relative(expert_low, count)
    if count == 4:
        expert_chunks = [expert_chunks[m] for m in (0, 2, 1, 3)]
    shared_low = jnp.concatenate(
        [shared_in.astype(LOW).transpose(1, 0, 2), shared_out.astype(LOW).T[None]], axis=0
    )
    w_mix_out = lax.all_gather(mix_out_low, ("wide", "tensor"), axis=0, tiled=True)
    shared_low = after(shared_low, w_mix_out)
    w_shared = lax.all_gather(shared_low, "wide", axis=1, tiled=True)

    own_routes = lax.dynamic_slice_in_dim(routes, rank * rows_dev, rows_dev, 0)
    own_logits = lax.dynamic_slice_in_dim(gate_logits, rank * rows_dev, rows_dev, 0)
    gates = jax.nn.softmax(own_logits, axis=-1)
    flat = own_routes.reshape(-1)
    named = (flat[:, None] == jnp.arange(wide, dtype=jnp.int32)[None, :]).astype(LOW)
    order = jnp.arange(flat.shape[0], dtype=jnp.int32)
    earlier = (order[None, :] < order[:, None]).astype(LOW)
    before = jnp.sum(dot(earlier, named) * named.astype(FULL), axis=1).astype(jnp.int32)
    places = (flat * capacity + before).reshape(rows_dev, TOP)
    slot_ids = jnp.arange(slots, dtype=jnp.int32)
    picks = [(slot_ids[:, None] == places[:, k][None, :]).astype(LOW) for k in range(TOP)]
    pick_any = picks[0] + picks[1]
    grad_out = cotangent.astype(FULL)
    grad_routes = [(gates[:, k : k + 1] * grad_out).astype(LOW) for k in range(TOP)]
    grad_slots = (dot(picks[0], grad_routes[0]) + dot(picks[1], grad_routes[1])).astype(LOW)
    grad_slots = after(grad_slots, got)
    expert_grads = exchange(grad_slots.reshape(wide, capacity, width)).reshape(slots, width)

    tree_places = jnp.arange(tree_length, dtype=jnp.int32)
    segment, upward, position = tree_layout(parents[0], tree_places)
    allowed = allowed_mask(segment, upward, tree_places)
    cosine, sine = rotary_tables(position.astype(FULL))
    tree_rows = tokens_all.astype(FULL)
    normed_one = (tree_rows * rms_factor(tree_rows) * gain_pair[0]).astype(LOW)
    projected = dot(normed_one, w_qkv).reshape(tree_length, 3, heads_dev, HEAD)
    queries = rotate(projected[:, 0], cosine, sine).astype(LOW)
    keys = rotate(projected[:, 1], cosine, sine).astype(LOW)
    values = projected[:, 2].astype(LOW)
    attended, log_totals = attend_forward(queries, keys, values, allowed)
    attended = attended.astype(LOW).reshape(tree_length, head_width)
    attended_own = attended
    attended = send_relative([block_of(attended, rank ^ m, rows_dev) for m in range(count)])
    attended_low = jnp.concatenate(by_rank(attended, rank), axis=1)[:, :width]
    attended_low = after(attended_low, expert_chunks[1])
    input_rows = tokens.astype(FULL)
    residual = input_rows + dot(attended_low, w_mix_out)
    factor_two = rms_factor(residual)
    normed_two = (residual * factor_two * gain_pair[1]).astype(LOW)

    row_slots = dot(pick_any, normed_two).astype(LOW)
    row_slots = after(row_slots, expert_grads)
    expert_rows = exchange(row_slots.reshape(wide, capacity, width)).reshape(slots, width)
    shared_rows = jnp.concatenate(gather_relative(normed_two, count), axis=0)
    cotangent_late = after(cotangent, normed_two)
    cotangent_rel = jnp.concatenate(gather_relative(cotangent_late, count), axis=0)
    expert_rows, shared_rows, cotangent_rel = lax.optimization_barrier(
        (expert_rows, shared_rows, cotangent_rel)
    )

    *ex_states, ex_grad_rows, ex_xt, ex_gt = branch_rows(expert_rows, expert_grads, expert_chunks)
    back_rows = exchange(ex_grad_rows.reshape(wide, capacity, width)).reshape(slots, width)
    shared_rows = after(shared_rows, ex_grad_rows)
    *sh_states, sh_grad_rows, sh_xt, sh_gt = branch_rows(shared_rows, cotangent_rel, [w_shared])
    ex_states = list(after(tuple(ex_states), sh_grad_rows))
    sh_grad_rows = sum_relative(jnp.split(sh_grad_rows, count))
    sh_part = branch_out(sh_states[0], [w_shared])
    sh_part = sum_relative(jnp.split(sh_part, count))
    sh_size = sh_states[0].shape[1]
    sh_grads = shared_grads((sh_xt, sh_gt), sh_states, wide)
    rows_shared = width // wide
    ex_size = ex_states[0].shape[1] // count
    ex_grads = functools.partial(branch_grads, (ex_xt, ex_gt), ex_states)
    if count == 4:
        ex_sent = swap(ex_grads(2, 2, ex_size), "tensor", 1, count)
        ex_kept = ex_grads(0, 2, ex_size)
    else:
        ex_sent, ex_kept = (), ex_grads(0, count, ex_size)
    out_rows = branch_out(ex_states[0], expert_chunks)
    back_rows, out_rows, ex_kept, sh_grads, sh_part = lax.optimization_barrier(
        (back_rows, out_rows, ex_kept, sh_grads, sh_part)
    )
    returned = exchange(out_rows.reshape(wide, capacity, width)).reshape(slots, width)

    grad_normed_two = dot_tn(pick_any, back_rows) + sh_grad_rows
    grad_part, hat_two = rms_back(residual, factor_two, gain_pair[1], grad_normed_two)
    gain_two_part = jnp.sum(grad_normed_two * hat_two, axis=0)
    grad_residual = grad_out + grad_part
    grad_res_low = grad_residual.astype(LOW)
    w_mix_pad = jnp.pad(w_mix_out, ((0, head_pad * HEAD), (0, 0)))
    grad_res_parts = gather_relative(grad_res_low, count)
    grad_res_all = jnp.concatenate(by_rank(grad_res_parts, rank), axis=0)
    w_mix_own = block_of(w_mix_pad, rank, head_width)
    grad_attended = dot_nt(grad_res_all, w_mix_own).astype(LOW)
    grad_attended = grad_attended.reshape(tree_length, heads_dev, HEAD)
    if head_width == rows_weight * wide:
        grad_mix_out = dot_tn(attended_own, grad_res_all).astype(LOW)
        lines = rows_weight * width // sh_size
        sums = jnp.concatenate(
            [
                sh_grads.reshape(wide, 3 * rows_shared, sh_size),
                grad_mix_out.reshape(wide, lines, sh_size),
            ],
            axis=1,
        )
        grad_attended, sums = lax.optimization_barrier((grad_attended, sums))
        sums = lax.psum_scatter(sums, "wide", scatter_dimension=0, tiled=True)[0]
        turns = [(w * count + t, t * wide + w) for w in range(wide) for t in range(count)]
    else:
        grad_mix_out = dot_tn(attended_low, grad_res_low).astype(LOW)
        sums = lax.all_to_all(
            grad_mix_out.reshape(wide * count, rows_weight, width),
            ("wide", "tensor"),
            split_axis=0,
            concat_axis=0,
            tiled=True,
        )
        sh_grads = lax.psum_scatter(sh_grads, "wide", scatter_dimension=0, tiled=True)
        turns = None
    across = ()
    if count == 4:
        across = ex_kept[1].astype(FULL) + ex_sent[1].astype(FULL)
        across = across.astype(LOW)
        across_in, across_out, grad_attended = lax.optimization_barrier(
            (across[:2], across[2:], grad_attended)
        )
        across_in = swap(across_in, "tensor", 2, count)
        across_out = swap(after(across_out, across_in), "tensor", 2, count)
        across = (across_in,)

    grad_query, grad_key, grad_value = attend_backward(
        queries, keys, values, allowed, grad_attended, log_totals
    )
    grad_projected = jnp.stack(
        [rotate(grad_query, cosine, -sine), rotate(grad_key, cosine, -sine), grad_value], axis=1
    )
    grad_projected = grad_projected.astype(LOW).reshape(tree_length, 3 * head_width)
    grad_normed_one = dot_nt(grad_projected, w_qkv).astype(LOW)
    row_grads = send_relative(
        [block_of(grad_normed_one, rank ^ m, rows_dev) for m in range(count)]
    )
    grad_mix_in = dot_tn(normed_one, grad_projected).astype(LOW)
    grad_mix_in = after(grad_mix_in, returned, *across)
    if count == 4:
        in_parts = [ex_kept, ex_sent, across_in[None]]
        out_parts = [ex_kept, ex_sent, after(across_out, grad_projected)[None]]
    else:
        in_parts = [part[None] for part in send_relative([ex_kept[m] for m in range(count)])]
        out_parts = in_parts
    returned = after(returned, grad_projected)
    sent = jnp.concatenate([grad_mix_in, gain_two_part.astype(LOW)[:, None]], axis=1)
    got = lax.all_to_all(
        sent.reshape(wide * count, rows_weight, 3 * head_width + 1),
        ("wide", "tensor"),
        split_axis=0,
        concat_axis=0,
        tiled=True,
    )
    in_results = adam_in(in_parts, expert_in, expert_in_mean, expert_in_square, RATES[5])
    out_results = adam_out(out_parts, expert_out, expert_out_mean, expert_out_square, RATES[6])
    row_grads, in_results = lax.optimization_barrier((row_grads, in_results))
    sums, sh_grads, out_results = lax.optimization_barrier((sums, sh_grads, out_results))
    grad_normed_one = sum(part.astype(FULL) for part in row_grads)
    if turns:
        sh_grads = sums[: 3 * rows_shared].reshape(3, rows_shared, sh_size).astype(FULL)
        grad_mix_out = sums[3 * rows_shared :].reshape(rows_weight, width)
        grad_mix_out = lax.ppermute(grad_mix_out, ("wide", "tensor"), turns).astype(FULL)
    else:
        sh_grads = sh_grads[0].astype(FULL)
        grad_mix_out = jnp.sum(sums.astype(FULL), axis=0)
    got = jnp.sum(got.astype(FULL).reshape(wide, count, rows_weight, -1), axis=0)
    grad_gain_two = jnp.sum(got[:, :, 3 * head_width], axis=0)
    grad_mix_in = got[:, :, : 3 * head_width].reshape(count, rows_weight, 3, head_width)
    grad_mix_in = grad_mix_in.transpose(1, 2, 0, 3).reshape(rows_weight, 3, count * head_width)
    grad_mix_in = grad_mix_in[:, :, :width].reshape(rows_weight, 3 * width)
    grad_gain_one = jnp.sum(mixing_in.astype(LOW).astype(FULL) * grad_mix_in, axis=1)
    grad_gain_one = grad_gain_one / norm_gains[0].astype(LOW).astype(FULL)

    grad_part, _ = rms_back(input_rows, rms_factor(input_rows), gain_pair[0], grad_normed_one)
    input_grad = grad_residual + grad_part

    per_route = [dot_tn(picks[k], returned) for k in range(TOP)]
    mixed = residual + gates[:, :1] * per_route[0] + gates[:, 1:] * per_route[1]
    mixed = mixed + sh_part
    gate_grad = jnp.stack([jnp.sum(grad_out * rows, axis=-1) for rows in per_route], axis=1)
    logit_grad = gates * (gate_grad - jnp.sum(gates * gate_grad, axis=-1, keepdims=True))

    gradients = (
        (mixing_in, mixing_in_mean, mixing_in_square, grad_mix_in),
        (mixing_out, mixing_out_mean, mixing_out_square, grad_mix_out),
        (
            norm_gains,
            norm_gains_mean,
            norm_gains_square,
            jnp.stack([grad_gain_one, grad_gain_two]),
        ),
        (shared_in, shared_in_mean, shared_in_square, sh_grads[:2].transpose(1, 0, 2)),
        (shared_out, shared_out_mean, shared_out_square, sh_grads[2].T),
    )
    results = [mixed.astype(LOW), input_grad, logit_grad]
    for number, (weight, mean, square, gradient) in enumerate(gradients):
        results.extend(adam_step(weight, mean, square, gradient, RATES[number]))
    results.extend(in_results)
    results.extend(out_results)
    return tuple(results)


def solution(mesh):
    placed = (
        P(("wide", "tensor"), None),
        P(("wide", "tensor"), None),
        P("wide", None),
        P("wide", None),
        P("wide", None),
        P(("wide", "tensor"), None),
        P(("wide", "tensor"), None),
        P(("wide", "tensor"), None),
        P(("wide", "tensor"), None),
        P(("wide", "tensor"), None),
        P(("wide", "tensor"), None),
        P(None, ("wide", "tensor")),
        P(None, ("wide", "tensor")),
        P(None, ("wide", "tensor")),
        P("wide", None, "tensor"),
        P("wide", None, "tensor"),
        P("wide", None, "tensor"),
        P("tensor", "wide"),
        P("tensor", "wide"),
        P("tensor", "wide"),
        P("wide", None, None, "tensor"),
        P("wide", None, None, "tensor"),
        P("wide", None, None, "tensor"),
        P("wide", "tensor", None),
        P("wide", "tensor", None),
        P("wide", "tensor", None),
    )
    return jax.shard_map(
        body,
        mesh=mesh,
        in_specs=placed,
        out_specs=(
            P(("wide", "tensor"), None),
            P(("wide", "tensor"), None),
            P(("wide", "tensor"), None),
            P(("wide", "tensor"), None),
            P(("wide", "tensor"), None),
            P(("wide", "tensor"), None),
            P(("wide", "tensor"), None),
            P(("wide", "tensor"), None),
            P(("wide", "tensor"), None),
            P(None, ("wide", "tensor")),
            P(None, ("wide", "tensor")),
            P(None, ("wide", "tensor")),
            P("wide", None, "tensor"),
            P("wide", None, "tensor"),
            P("wide", None, "tensor"),
            P("tensor", "wide"),
            P("tensor", "wide"),
            P("tensor", "wide"),
            P("wide", None, None, "tensor"),
            P("wide", None, None, "tensor"),
            P("wide", None, None, "tensor"),
            P("wide", "tensor", None),
            P("wide", "tensor", None),
            P("wide", "tensor", None),
        ),
        check_vma=False,
    )
```

```python
import functools
import math

import jax
import jax.numpy as jnp
from jax import lax
from jax.experimental import pallas as pl
from jax.experimental.pallas import tpu as pltpu
from jax.sharding import PartitionSpec as P

HEAD = 64
TOP = 2
TRUNK = 256
SEG = 64
STEP = 5
SEGS = 13


NORM_EPS = 1e-06
BETA_ONE = 0.5
BETA_TWO = 0.5
ADAM_EPS = 1e-08
DECAY = 0.01
RATES = (0.02, 0.15, 0.3, 0.02, 0.012, 0.02, 0.012)

LOW = jnp.bfloat16
FULL = jnp.float32
SMALL = pl.CostEstimate(flops=1000, bytes_accessed=1000, transcendentals=0)


def dot(a, b):
    return jnp.dot(a, b, preferred_element_type=FULL)


def dot_nt(a, b):
    return lax.dot_general(a, b, (((1,), (1,)), ((), ())), preferred_element_type=FULL)


def dot_tn(a, b):
    return lax.dot_general(a, b, (((0,), (0,)), ((), ())), preferred_element_type=FULL)


def rms_factor(values):
    return lax.rsqrt(jnp.mean(values * values, axis=-1, keepdims=True) + NORM_EPS)


def rms_back(values, factor, gain, grad):
    hat = values * factor
    scaled = grad * gain
    return factor * (scaled - hat * jnp.mean(scaled * hat, axis=-1, keepdims=True)), hat


def rotary_tables(position):
    half = HEAD // 2
    frequency = 10000.0 ** (-jnp.arange(half, dtype=FULL) / half)
    angles = position[:, None] * frequency[None, :]
    return jnp.cos(angles)[:, None, :], jnp.sin(angles)[:, None, :]


def rotate(values, cosine, sine):
    half = values.shape[-1] // 2
    one, two = values[..., :half], values[..., half:]
    return jnp.concatenate([one * cosine - two * sine, two * cosine + one * sine], axis=-1)


def tree_layout(parent_row, places):
    segment = jnp.where(places < TRUNK, 0, 1 + (places - TRUNK) // SEG)
    seg_start = jnp.where(segment == 0, 0, TRUNK + (segment - 1) * SEG)
    matches = segment[:, None] == jnp.arange(SEGS, dtype=jnp.int32)[None, :]
    upward = jnp.sum(jnp.where(matches, parent_row[None, :], 0), axis=1)
    depth_base = jnp.where(upward == 0, TRUNK, TRUNK + SEG)
    position = jnp.where(segment == 0, places, depth_base + places - seg_start)
    return (segment, upward, position)


def allowed_mask(segment, upward, places):
    same_segment = (segment[None, :] == segment[:, None]) & (places[None, :] <= places[:, None])
    ancestor = (segment[:, None] != 0) & (
        (segment[None, :] == 0) | (segment[None, :] == upward[:, None])
    )
    return same_segment | ancestor


def attend_forward(queries, keys, values, allowed):
    scale = 1.0 / math.sqrt(HEAD)
    scores = jnp.einsum("qhd,khd->hqk", queries, keys, preferred_element_type=FULL) * scale
    scores = jnp.where(allowed[None], scores, -1e30)
    row_top = jnp.max(scores, axis=-1, keepdims=True)
    shifted = jnp.exp(scores - row_top)
    row_total = jnp.sum(shifted, axis=-1, keepdims=True)
    weights = (shifted / row_total).astype(LOW)
    attended = jnp.einsum("hqk,khd->qhd", weights, values, preferred_element_type=FULL)
    return attended, row_top + jnp.log(row_total)


def attend_backward(queries, keys, values, allowed, grad_attended, log_totals):
    scale = 1.0 / math.sqrt(HEAD)
    scores = jnp.einsum("qhd,khd->hqk", queries, keys, preferred_element_type=FULL) * scale
    scores = jnp.where(allowed[None], scores, -1e30)
    probs = jnp.exp(scores - log_totals)
    grad_probs = jnp.einsum("qhd,khd->hqk", grad_attended, values, preferred_element_type=FULL)
    inner = jnp.sum(probs * grad_probs, axis=-1, keepdims=True)
    grad_scores = (probs * (grad_probs - inner)).astype(LOW)
    grad_query = jnp.einsum("hqk,khd->qhd", grad_scores, keys, preferred_element_type=FULL) * scale
    grad_key = jnp.einsum("hqk,qhd->khd", grad_scores, queries, preferred_element_type=FULL) * scale
    grad_value = jnp.einsum(
        "hqk,qhd->khd", probs.astype(LOW), grad_attended, preferred_element_type=FULL
    )
    return grad_query, grad_key, grad_value


def branch_rows_kernel(chunks, x_ref, g_ref, *refs):
    weights = refs[:chunks]
    hidden_ref, ggate_ref, gup_ref, grad_ref, xt_ref, gt_ref = refs[chunks:]
    x, g = x_ref[...], g_ref[...]
    xt_ref[...] = x.T
    gt_ref[...] = g.T
    total = None
    for chunk in range(chunks):
        w = weights[chunk]
        size = w.shape[2]
        at = pl.ds(chunk * size, size)
        gate, up, grad_hidden = dot(x, w[0]), dot(x, w[1]), dot(g, w[2])
        sigmoid = 1.0 / (1.0 + jnp.exp(-gate))
        active = gate * sigmoid
        hidden_ref[:, at] = (active * up).astype(LOW)
        ggate = (grad_hidden * up * sigmoid * (1.0 + gate * (1.0 - sigmoid))).astype(LOW)
        gup = (grad_hidden * active).astype(LOW)
        ggate_ref[:, at] = ggate
        gup_ref[:, at] = gup
        part = dot_nt(ggate, w[0]) + dot_nt(gup, w[1])
        total = part if total is None else total + part
    grad_ref[...] = total.astype(LOW)


def branch_rows(x, g, chunks):
    rows, width = x.shape
    size = chunks[0].shape[2]
    hidden = size * len(chunks)
    block = math.gcd(rows, 256)
    row_spec = pl.BlockSpec((block, width), lambda i: (i, 0))
    hidden_spec = pl.BlockSpec((block, hidden), lambda i: (i, 0))
    whole = [
        pl.BlockSpec(w.shape, lambda i: (0, 0, 0), pipeline_mode=pl.Buffered(1)) for w in chunks
    ]
    hidden_type = jax.ShapeDtypeStruct((rows, hidden), LOW)
    turned_spec = pl.BlockSpec((width, block), lambda i: (0, i))
    turned_type = jax.ShapeDtypeStruct((width, rows), LOW)
    return pl.pallas_call(
        functools.partial(branch_rows_kernel, len(chunks)),
        grid=(rows // block,),
        in_specs=[row_spec, row_spec] + whole,
        out_specs=[hidden_spec] * 3 + [row_spec] + [turned_spec] * 2,
        out_shape=[hidden_type] * 3
        + [jax.ShapeDtypeStruct((rows, width), LOW)]
        + [turned_type] * 2,
        compiler_params=pltpu.CompilerParams(vmem_limit_bytes=48 * 1024 * 1024),
        cost_estimate=SMALL,
        name="branch_rows",
    )(x, g, *chunks)


def branch_out_kernel(chunks, hidden_ref, *refs):
    weights, out_ref = refs[:chunks], refs[chunks]
    total = None
    for chunk in range(chunks):
        w_out = weights[chunk][0]
        size = w_out.shape[1]
        part = dot_nt(hidden_ref[:, pl.ds(chunk * size, size)], w_out)
        total = part if total is None else total + part
    out_ref[...] = total.astype(LOW)


def branch_out(hidden, chunks):
    rows, size = hidden.shape
    width = chunks[0].shape[1]
    block = math.gcd(rows, 256)
    return pl.pallas_call(
        functools.partial(branch_out_kernel, len(chunks)),
        grid=(rows // block,),
        in_specs=[pl.BlockSpec((block, size), lambda i: (i, 0))]
        + [
            pl.BlockSpec(
                (1,) + w.shape[1:], lambda i: (2, 0, 0), pipeline_mode=pl.Buffered(1)
            )
            for w in chunks
        ],
        out_specs=pl.BlockSpec((block, width), lambda i: (i, 0)),
        out_shape=jax.ShapeDtypeStruct((rows, width), LOW),
        compiler_params=pltpu.CompilerParams(vmem_limit_bytes=48 * 1024 * 1024),
        cost_estimate=SMALL,
        name="branch_out",
    )(hidden, *chunks)


def branch_grads_kernel(xt_ref, gt_ref, hidden_ref, ggate_ref, gup_ref, grad_ref):
    xt = xt_ref[...]
    grad_ref[0, 0] = dot(xt, ggate_ref[...]).astype(LOW)
    grad_ref[0, 1] = dot(xt, gup_ref[...]).astype(LOW)
    grad_ref[0, 2] = dot(gt_ref[...], hidden_ref[...]).astype(LOW)


def branch_grads(turned, states, first, chunks, size):
    width, rows = turned[0].shape
    block = math.gcd(width, 256)
    turned_spec = pl.BlockSpec((block, rows), lambda j, i: (i, 0))
    hidden_spec = pl.BlockSpec((rows, size), lambda j, i: (0, first + j))
    return pl.pallas_call(
        branch_grads_kernel,
        grid=(chunks, width // block),
        in_specs=[turned_spec] * 2 + [hidden_spec] * 3,
        out_specs=pl.BlockSpec((1, 3, block, size), lambda j, i: (j, 0, i, 0)),
        out_shape=jax.ShapeDtypeStruct((chunks, 3, width, size), LOW),
        compiler_params=pltpu.CompilerParams(vmem_limit_bytes=48 * 1024 * 1024),
        cost_estimate=SMALL,
        name="branch_grads",
    )(*turned, *states)


def adam_step(weight, mean_old, square_old, gradient, rate):
    mean_new = BETA_ONE * mean_old + (1.0 - BETA_ONE) * gradient
    square_new = BETA_TWO * square_old + (1.0 - BETA_TWO) * gradient * gradient
    mean_hat = mean_new / (1.0 - BETA_ONE**STEP)
    square_hat = square_new / (1.0 - BETA_TWO**STEP)
    updated = weight - rate * (mean_hat / (jnp.sqrt(square_hat) + ADAM_EPS) + DECAY * weight)
    return (mean_new, square_new, updated)


def shared_grads_kernel(xt_ref, gt_ref, hidden_ref, ggate_ref, gup_ref, grad_ref):
    groups, _, rows, _ = grad_ref.shape
    for plane, (turned, state) in enumerate(
        ((xt_ref, ggate_ref), (xt_ref, gup_ref), (gt_ref, hidden_ref))
    ):
        grad = dot(turned[...], state[...])
        for group in range(groups):
            grad_ref[group, plane] = grad[group * rows : (group + 1) * rows].astype(LOW)


def shared_grads(turned, states, wide):
    width, rows = turned[0].shape
    size = states[0].shape[1]
    share = width // wide
    groups = max(g for g in range(1, wide + 1) if wide % g == 0 and g * share <= 384)
    turned_spec = pl.BlockSpec((groups * share, rows), lambda i: (i, 0))
    return pl.pallas_call(
        shared_grads_kernel,
        grid=(wide // groups,),
        in_specs=[turned_spec] * 2 + [pl.BlockSpec((rows, size), lambda i: (0, 0))] * 3,
        out_specs=pl.BlockSpec((groups, 3, share, size), lambda i: (i, 0, 0, 0)),
        out_shape=jax.ShapeDtypeStruct((wide, 3, share, size), LOW),
        compiler_params=pltpu.CompilerParams(vmem_limit_bytes=48 * 1024 * 1024),
        cost_estimate=SMALL,
        name="shared_grads",
    )(*turned, *states)


def sum_of(refs, plane):
    total = refs[0][0, plane].astype(FULL)
    for ref in refs[1:]:
        total = total + ref[0, plane].astype(FULL)
    return total


def adam_in_kernel(count, rate, *refs):
    parts, (w_ref, mean_ref, square_ref), outs = refs[:count], refs[count : count + 3], refs[-4:-1]
    grad_ref = refs[-1]
    _, _, rows, size = parts[0].shape
    tiles = size // 128
    for half in range(2):
        total = sum_of(parts, half)
        for tile in range(tiles):
            at = pl.ds(2 * tile + half, rows, 2 * tiles)
            grad_ref[at, :] = total[:, tile * 128 : (tile + 1) * 128]
    results = adam_step(w_ref[...], mean_ref[...], square_ref[...], grad_ref[...], rate)
    for ref, value in zip(outs, results):
        ref[...] = value


def adam_in(parts, weight, mean, square, rate):
    _, width, _, size = weight.shape
    tiles = size // 128
    block = math.gcd(width, 128)

    def rows_of(value):
        value = value[0].reshape(width, 2, tiles, 128).transpose(0, 2, 1, 3)
        return value.reshape(width * 2 * tiles, 128)

    spec = pl.BlockSpec((block * 2 * tiles, 128), lambda i: (i, 0))
    outs = pl.pallas_call(
        functools.partial(adam_in_kernel, len(parts), rate),
        grid=(width // block,),
        in_specs=[pl.BlockSpec((1, 2, block, size), lambda i: (0, 0, i, 0))] * len(parts) + [spec] * 3,
        out_specs=[spec] * 3,
        out_shape=[jax.ShapeDtypeStruct((width * 2 * tiles, 128), FULL)] * 3,
        scratch_shapes=[pltpu.VMEM((block * 2 * tiles, 128), FULL)],
        compiler_params=pltpu.CompilerParams(vmem_limit_bytes=48 * 1024 * 1024),
        cost_estimate=SMALL,
        name="adam_in",
    )(*parts, rows_of(weight), rows_of(mean), rows_of(square))
    return [
        out.reshape(width, tiles, 2, 128).transpose(0, 2, 1, 3).reshape(weight.shape)
        for out in outs
    ]


def adam_out_kernel(count, rate, *refs):
    parts, (w_ref, mean_ref, square_ref), outs = refs[:count], refs[count : count + 3], refs[-3:]
    total = sum_of(parts, 0).T
    results = adam_step(w_ref[0], mean_ref[0], square_ref[0], total, rate)
    for ref, value in zip(outs, results):
        ref[0] = value


def adam_out(parts, weight, mean, square, rate):
    _, size, width = weight.shape
    block = math.gcd(width, 128)
    spec = pl.BlockSpec((1, size, block), lambda i: (0, 0, i))
    last = [
        pl.BlockSpec((1, 1, block, size), functools.partial(lambda n, i: (0, n, i, 0), p.shape[1] - 1))
        for p in parts
    ]
    return pl.pallas_call(
        functools.partial(adam_out_kernel, len(parts), rate),
        grid=(width // block,),
        in_specs=last + [spec] * 3,
        out_specs=[spec] * 3,
        out_shape=[jax.ShapeDtypeStruct(weight.shape, FULL)] * 3,
        compiler_params=pltpu.CompilerParams(vmem_limit_bytes=48 * 1024 * 1024),
        cost_estimate=SMALL,
        name="adam_out",
    )(*parts, weight, mean, square)


def swap(value, axis, mask, count):
    return lax.ppermute(value, axis, [(i, i ^ mask) for i in range(count)])


def after(value, *earlier):
    return lax.optimization_barrier((value,) + earlier)[0]


def by_rank(parts, rank):
    count = len(parts)
    ordered = []
    for place in range(count):
        chosen = parts[place]
        for other in range(1, count):
            chosen = jnp.where(rank == other, parts[place ^ other], chosen)
        ordered.append(chosen)
    return ordered


def gather_relative(value, count):
    if count != 4:
        rank = lax.axis_index("tensor")
        every = lax.all_gather(value, "tensor", axis=0)
        return [lax.dynamic_index_in_dim(every, rank ^ m, 0, False) for m in range(count)]
    far = swap(value, "tensor", 2, count)
    near = swap(value, "tensor", 1, count)
    return [value, near, far, swap(far, "tensor", 1, count)]


def send_relative(parts):
    count = len(parts)
    return [parts[0]] + [swap(parts[m], "tensor", m, count) for m in range(1, count)]


def sum_relative(parts):
    got = send_relative([p.astype(LOW) for p in parts])
    total = parts[0].astype(FULL)
    for part in got[1:]:
        total = total + part.astype(FULL)
    return total


def block_of(value, place, size, dim=0):
    return lax.dynamic_slice_in_dim(value, place * size, size, dim)


def exchange(value):
    return lax.all_to_all(value, "wide", split_axis=0, concat_axis=0, tiled=True)


def body(
    tokens,
    cotangent,
    gate_logits,
    routes,
    parents,
    mixing_in,
    mixing_in_mean,
    mixing_in_square,
    mixing_out,
    mixing_out_mean,
    mixing_out_square,
    norm_gains,
    norm_gains_mean,
    norm_gains_square,
    shared_in,
    shared_in_mean,
    shared_in_square,
    shared_out,
    shared_out_mean,
    shared_out_square,
    expert_in,
    expert_in_mean,
    expert_in_square,
    expert_out,
    expert_out_mean,
    expert_out_square,
):
    rows_dev, width = tokens.shape
    wide = lax.axis_size("wide")
    count = lax.axis_size("tensor")
    rank = lax.axis_index("tensor")
    tree_length = rows_dev * count
    capacity = 2 * rows_dev * TOP // wide
    slots = wide * capacity
    heads = width // HEAD
    heads_dev = -(-heads // count)
    head_pad = heads_dev * count - heads
    head_width = heads_dev * HEAD
    rows_weight = mixing_in.shape[0]

    cut = mixing_in.astype(LOW).reshape(rows_weight, 3, heads, HEAD)
    cut = jnp.pad(cut, ((0, 0), (0, 0), (0, head_pad), (0, 0)))
    cut = cut.reshape(rows_weight, 3, count, head_width).transpose(2, 0, 1, 3)
    cut = cut.reshape(count, rows_weight, 3 * head_width)
    gain_columns = jnp.broadcast_to(norm_gains.astype(LOW).T[None], (count, rows_weight, 2))
    cut = jnp.concatenate([cut, gain_columns], axis=2)
    sent = jnp.broadcast_to(cut[None], (wide,) + cut.shape).reshape(
        wide * count, rows_weight, 3 * head_width + 2
    )
    mix_out_low = lax.optimization_barrier(mixing_out.astype(LOW))
    sent = after(sent, mix_out_low)
    got = lax.all_to_all(sent, ("wide", "tensor"), split_axis=0, concat_axis=0, tiled=True)
    got = got.reshape(width, 3 * head_width + 2)
    w_qkv = got[:, : 3 * head_width]
    gain_pair = got[:, 3 * head_width :].astype(FULL).T

    token_parts = gather_relative(tokens, count)
    tokens_all = jnp.concatenate(by_rank(token_parts, rank), axis=0)
    expert_low = jnp.concatenate(
        [expert_in[0].astype(LOW).transpose(1, 0, 2), expert_out.astype(LOW).transpose(0, 2, 1)],
        axis=0,
    )
    expert_chunks = gather_relative(expert_low, count)
    if count == 4:
        expert_chunks = [expert_chunks[m] for m in (0, 2, 1, 3)]
    shared_low = jnp.concatenate(
        [shared_in.astype(LOW).transpose(1, 0, 2), shared_out.astype(LOW).T[None]], axis=0
    )
    w_mix_out = lax.all_gather(mix_out_low, ("wide", "tensor"), axis=0, tiled=True)
    shared_low = after(shared_low, w_mix_out)
    w_shared = lax.all_gather(shared_low, "wide", axis=1, tiled=True)

    own_routes = lax.dynamic_slice_in_dim(routes, rank * rows_dev, rows_dev, 0)
    own_logits = lax.dynamic_slice_in_dim(gate_logits, rank * rows_dev, rows_dev, 0)
    gates = jax.nn.softmax(own_logits, axis=-1)
    flat = own_routes.reshape(-1)
    named = (flat[:, None] == jnp.arange(wide, dtype=jnp.int32)[None, :]).astype(LOW)
    order = jnp.arange(flat.shape[0], dtype=jnp.int32)
    earlier = (order[None, :] < order[:, None]).astype(LOW)
    before = jnp.sum(dot(earlier, named) * named.astype(FULL), axis=1).astype(jnp.int32)
    places = (flat * capacity + before).reshape(rows_dev, TOP)
    slot_ids = jnp.arange(slots, dtype=jnp.int32)
    picks = [(slot_ids[:, None] == places[:, k][None, :]).astype(LOW) for k in range(TOP)]
    pick_any = picks[0] + picks[1]
    grad_out = cotangent.astype(FULL)
    grad_routes = [(gates[:, k : k + 1] * grad_out).astype(LOW) for k in range(TOP)]
    grad_slots = (dot(picks[0], grad_routes[0]) + dot(picks[1], grad_routes[1])).astype(LOW)
    grad_slots = after(grad_slots, got)
    expert_grads = exchange(grad_slots.reshape(wide, capacity, width)).reshape(slots, width)

    tree_places = jnp.arange(tree_length, dtype=jnp.int32)
    segment, upward, position = tree_layout(parents[0], tree_places)
    allowed = allowed_mask(segment, upward, tree_places)
    cosine, sine = rotary_tables(position.astype(FULL))
    tree_rows = tokens_all.astype(FULL)
    normed_one = (tree_rows * rms_factor(tree_rows) * gain_pair[0]).astype(LOW)
    projected = dot(normed_one, w_qkv).reshape(tree_length, 3, heads_dev, HEAD)
    queries = rotate(projected[:, 0], cosine, sine).astype(LOW)
    keys = rotate(projected[:, 1], cosine, sine).astype(LOW)
    values = projected[:, 2].astype(LOW)
    attended, log_totals = attend_forward(queries, keys, values, allowed)
    attended = attended.astype(LOW).reshape(tree_length, head_width)
    attended_own = attended
    attended = send_relative([block_of(attended, rank ^ m, rows_dev) for m in range(count)])
    attended_low = jnp.concatenate(by_rank(attended, rank), axis=1)[:, :width]
    attended_low = after(attended_low, expert_chunks[1])
    input_rows = tokens.astype(FULL)
    residual = input_rows + dot(attended_low, w_mix_out)
    factor_two = rms_factor(residual)
    normed_two = (residual * factor_two * gain_pair[1]).astype(LOW)

    row_slots = dot(pick_any, normed_two).astype(LOW)
    row_slots = after(row_slots, expert_grads)
    expert_rows = exchange(row_slots.reshape(wide, capacity, width)).reshape(slots, width)
    shared_rows = jnp.concatenate(gather_relative(normed_two, count), axis=0)
    cotangent_late = after(cotangent, normed_two)
    cotangent_rel = jnp.concatenate(gather_relative(cotangent_late, count), axis=0)
    expert_rows, shared_rows, cotangent_rel = lax.optimization_barrier(
        (expert_rows, shared_rows, cotangent_rel)
    )

    *ex_states, ex_grad_rows, ex_xt, ex_gt = branch_rows(expert_rows, expert_grads, expert_chunks)
    back_rows = exchange(ex_grad_rows.reshape(wide, capacity, width)).reshape(slots, width)
    shared_rows = after(shared_rows, ex_grad_rows)
    *sh_states, sh_grad_rows, sh_xt, sh_gt = branch_rows(shared_rows, cotangent_rel, [w_shared])
    ex_states = list(after(tuple(ex_states), sh_grad_rows))
    sh_grad_rows = sum_relative(jnp.split(sh_grad_rows, count))
    sh_part = branch_out(sh_states[0], [w_shared])
    sh_part = sum_relative(jnp.split(sh_part, count))
    sh_size = sh_states[0].shape[1]
    sh_grads = shared_grads((sh_xt, sh_gt), sh_states, wide)
    rows_shared = width // wide
    ex_size = ex_states[0].shape[1] // count
    ex_grads = functools.partial(branch_grads, (ex_xt, ex_gt), ex_states)
    if count == 4:
        ex_sent = swap(ex_grads(2, 2, ex_size), "tensor", 1, count)
        ex_kept = ex_grads(0, 2, ex_size)
    else:
        ex_sent, ex_kept = (), ex_grads(0, count, ex_size)
    out_rows = branch_out(ex_states[0], expert_chunks)
    back_rows, out_rows, ex_kept, sh_grads, sh_part = lax.optimization_barrier(
        (back_rows, out_rows, ex_kept, sh_grads, sh_part)
    )
    returned = exchange(out_rows.reshape(wide, capacity, width)).reshape(slots, width)

    grad_normed_two = dot_tn(pick_any, back_rows) + sh_grad_rows
    grad_part, hat_two = rms_back(residual, factor_two, gain_pair[1], grad_normed_two)
    gain_two_part = jnp.sum(grad_normed_two * hat_two, axis=0)
    grad_residual = grad_out + grad_part
    grad_res_low = grad_residual.astype(LOW)
    w_mix_pad = jnp.pad(w_mix_out, ((0, head_pad * HEAD), (0, 0)))
    grad_res_parts = gather_relative(grad_res_low, count)
    grad_res_all = jnp.concatenate(by_rank(grad_res_parts, rank), axis=0)
    w_mix_own = block_of(w_mix_pad, rank, head_width)
    grad_attended = dot_nt(grad_res_all, w_mix_own).astype(LOW)
    grad_attended = grad_attended.reshape(tree_length, heads_dev, HEAD)
    if head_width == rows_weight * wide:
        grad_mix_out = dot_tn(attended_own, grad_res_all).astype(LOW)
        lines = rows_weight * width // sh_size
        sums = jnp.concatenate(
            [
                sh_grads.reshape(wide, 3 * rows_shared, sh_size),
                grad_mix_out.reshape(wide, lines, sh_size),
            ],
            axis=1,
        )
        grad_attended, sums = lax.optimization_barrier((grad_attended, sums))
        sums = lax.psum_scatter(sums, "wide", scatter_dimension=0, tiled=True)[0]
        turns = [(w * count + t, t * wide + w) for w in range(wide) for t in range(count)]
    else:
        grad_mix_out = dot_tn(attended_low, grad_res_low).astype(LOW)
        sums = lax.all_to_all(
            grad_mix_out.reshape(wide * count, rows_weight, width),
            ("wide", "tensor"),
            split_axis=0,
            concat_axis=0,
            tiled=True,
        )
        sh_grads = lax.psum_scatter(sh_grads, "wide", scatter_dimension=0, tiled=True)
        turns = None
    across = ()
    if count == 4:
        across = ex_kept[1].astype(FULL) + ex_sent[1].astype(FULL)
        across = across.astype(LOW)
        across_in, across_out, grad_attended = lax.optimization_barrier(
            (across[:2], across[2:], grad_attended)
        )
        across_in = swap(across_in, "tensor", 2, count)
        across_out = swap(after(across_out, across_in), "tensor", 2, count)
        across = (across_in,)

    grad_query, grad_key, grad_value = attend_backward(
        queries, keys, values, allowed, grad_attended, log_totals
    )
    grad_projected = jnp.stack(
        [rotate(grad_query, cosine, -sine), rotate(grad_key, cosine, -sine), grad_value], axis=1
    )
    grad_projected = grad_projected.astype(LOW).reshape(tree_length, 3 * head_width)
    grad_normed_one = dot_nt(grad_projected, w_qkv).astype(LOW)
    row_grads = send_relative(
        [block_of(grad_normed_one, rank ^ m, rows_dev) for m in range(count)]
    )
    grad_mix_in = dot_tn(normed_one, grad_projected).astype(LOW)
    grad_mix_in = after(grad_mix_in, returned, *across)
    if count == 4:
        in_parts = [ex_kept, ex_sent, across_in[None]]
        out_parts = [ex_kept, ex_sent, after(across_out, grad_projected)[None]]
    else:
        in_parts = [part[None] for part in send_relative([ex_kept[m] for m in range(count)])]
        out_parts = in_parts
    returned = after(returned, grad_projected)
    sent = jnp.concatenate([grad_mix_in, gain_two_part.astype(LOW)[:, None]], axis=1)
    got = lax.all_to_all(
        sent.reshape(wide * count, rows_weight, 3 * head_width + 1),
        ("wide", "tensor"),
        split_axis=0,
        concat_axis=0,
        tiled=True,
    )
    in_results = adam_in(in_parts, expert_in, expert_in_mean, expert_in_square, RATES[5])
    out_results = adam_out(out_parts, expert_out, expert_out_mean, expert_out_square, RATES[6])
    row_grads, in_results = lax.optimization_barrier((row_grads, in_results))
    sums, sh_grads, out_results = lax.optimization_barrier((sums, sh_grads, out_results))
    grad_normed_one = sum(part.astype(FULL) for part in row_grads)
    if turns:
        sh_grads = sums[: 3 * rows_shared].reshape(3, rows_shared, sh_size).astype(FULL)
        grad_mix_out = sums[3 * rows_shared :].reshape(rows_weight, width)
        grad_mix_out = lax.ppermute(grad_mix_out, ("wide", "tensor"), turns).astype(FULL)
    else:
        sh_grads = sh_grads[0].astype(FULL)
        grad_mix_out = jnp.sum(sums.astype(FULL), axis=0)
    got = jnp.sum(got.astype(FULL).reshape(wide, count, rows_weight, -1), axis=0)
    grad_gain_two = jnp.sum(got[:, :, 3 * head_width], axis=0)
    grad_mix_in = got[:, :, : 3 * head_width].reshape(count, rows_weight, 3, head_width)
    grad_mix_in = grad_mix_in.transpose(1, 2, 0, 3).reshape(rows_weight, 3, count * head_width)
    grad_mix_in = grad_mix_in[:, :, :width].reshape(rows_weight, 3 * width)
    grad_gain_one = jnp.sum(mixing_in.astype(LOW).astype(FULL) * grad_mix_in, axis=1)
    grad_gain_one = grad_gain_one / norm_gains[0].astype(LOW).astype(FULL)

    grad_part, _ = rms_back(input_rows, rms_factor(input_rows), gain_pair[0], grad_normed_one)
    input_grad = grad_residual + grad_part

    per_route = [dot_tn(picks[k], returned) for k in range(TOP)]
    mixed = residual + gates[:, :1] * per_route[0] + gates[:, 1:] * per_route[1]
    mixed = mixed + sh_part
    gate_grad = jnp.stack([jnp.sum(grad_out * rows, axis=-1) for rows in per_route], axis=1)
    logit_grad = gates * (gate_grad - jnp.sum(gates * gate_grad, axis=-1, keepdims=True))

    gradients = (
        (mixing_in, mixing_in_mean, mixing_in_square, grad_mix_in),
        (mixing_out, mixing_out_mean, mixing_out_square, grad_mix_out),
        (
            norm_gains,
            norm_gains_mean,
            norm_gains_square,
            jnp.stack([grad_gain_one, grad_gain_two]),
        ),
        (shared_in, shared_in_mean, shared_in_square, sh_grads[:2].transpose(1, 0, 2)),
        (shared_out, shared_out_mean, shared_out_square, sh_grads[2].T),
    )
    results = [mixed.astype(LOW), input_grad, logit_grad]
    for number, (weight, mean, square, gradient) in enumerate(gradients):
        results.extend(adam_step(weight, mean, square, gradient, RATES[number]))
    results.extend(in_results)
    results.extend(out_results)
    return tuple(results)


def solution(mesh):
    placed = (
        P(("wide", "tensor"), None),
        P(("wide", "tensor"), None),
        P("wide", None),
        P("wide", None),
        P("wide", None),
        P(("wide", "tensor"), None),
        P(("wide", "tensor"), None),
        P(("wide", "tensor"), None),
        P(("wide", "tensor"), None),
        P(("wide", "tensor"), None),
        P(("wide", "tensor"), None),
        P(None, ("wide", "tensor")),
        P(None, ("wide", "tensor")),
        P(None, ("wide", "tensor")),
        P("wide", None, "tensor"),
        P("wide", None, "tensor"),
        P("wide", None, "tensor"),
        P("tensor", "wide"),
        P("tensor", "wide"),
        P("tensor", "wide"),
        P("wide", None, None, "tensor"),
        P("wide", None, None, "tensor"),
        P("wide", None, None, "tensor"),
        P("wide", "tensor", None),
        P("wide", "tensor", None),
        P("wide", "tensor", None),
    )
    return jax.shard_map(
        body,
        mesh=mesh,
        in_specs=placed,
        out_specs=(
            P(("wide", "tensor"), None),
            P(("wide", "tensor"), None),
            P(("wide", "tensor"), None),
            P(("wide", "tensor"), None),
            P(("wide", "tensor"), None),
            P(("wide", "tensor"), None),
            P(("wide", "tensor"), None),
            P(("wide", "tensor"), None),
            P(("wide", "tensor"), None),
            P(None, ("wide", "tensor")),
            P(None, ("wide", "tensor")),
            P(None, ("wide", "tensor")),
            P("wide", None, "tensor"),
            P("wide", None, "tensor"),
            P("wide", None, "tensor"),
            P("tensor", "wide"),
            P("tensor", "wide"),
            P("tensor", "wide"),
            P("wide", None, None, "tensor"),
            P("wide", None, None, "tensor"),
            P("wide", None, None, "tensor"),
            P("wide", "tensor", None),
            P("wide", "tensor", None),
            P("wide", "tensor", None),
        ),
        check_vma=False,
    )
```
